256 devices in a mesh: row: 16 (over y, x_hi, core), col: 16 (over z, x_lo).
Axes of the slice: x: 4 (x_hi: 2, x_lo: 2; x = x_hi * 2 + x_lo), y: 4, z: 8, core: 2. Of those that a mesh axis runs over, the one named last changes fastest.
Arguments:
- amplitudes: bfloat16 [192, 192, 12288], P('row', None, 'col'), may hold values from -6 to 6
- integral_plus: bfloat16 [12288, 2048], P('col'), may hold values from -0.078125 to 0.078125
- integral_minus: bfloat16 [12288, 2048], P('col'), may hold values from -0.078125 to 0.078125
- cd_irrep: int32 [96], P('col'), may hold values from 0 to 3
- ab_irrep: int32 [16], replicated, may hold values from 0 to 3
Outputs:
- residual: bfloat16 [2048, 36864], P('col', 'row')
The draws below stay inside these ranges and needn't reach their ends.
All inputs are finite; a program needn't handle non-finite values.
Results may differ from the reference program's by a relative error of at most 0.022.
Values may be sent and summed in bfloat16 or wider, within the bound.
No kernel may reach another device: no remote copies, remote signals or barrier semaphores. Data moves between devices by JAX's collectives and lax.ppermute only.
A program may use at most 128 MiB of HBM per device.

```python
import jax
import jax.numpy as jnp
from jax import lax

OCC = 192
TILE = 128
KT_DEV = 6
PAIRS = 12288
SLAB = 2048
N_COL = 16


def set_ends(values, rng, low, top_value):
    longest = values.shape.index(max(values.shape))
    spots = []
    for shift in (0, 1):
        where = [jax.random.randint(jax.random.fold_in(rng, axis), (), 0, length) for axis, length in enumerate(values.shape)]
        where[longest] = (where[longest] + shift) % values.shape[longest]
        spots.append(tuple(where))
    return values.at[spots[0]].set(low).at[spots[1]].set(top_value)


def with_spikes(drawn, rng, source, target, blocks, factor):
    owner, partner = [(jnp.arange(drawn.shape[position]) // (drawn.shape[position] // blocks)).reshape([-1 if axis == position else 1 for axis in range(drawn.ndim)]) for position in (source, target)]
    chosen = jax.random.permutation(rng, blocks)[partner]
    strong = (owner == chosen) | (owner == (partner + blocks // 2) % blocks)
    return jnp.where(strong, factor * drawn, drawn)


def block_levels(key, dims, cuts, least, top_value):
    def one(position, parts):
        heights = jax.random.uniform(jax.random.fold_in(jax.random.fold_in(key, 6), position), (parts,), jnp.float32, least / len(cuts), top_value / len(cuts))
        return jnp.repeat(jnp.exp(heights), dims[position] // parts).reshape((-1,) + (1,) * (len(dims) - position - 1))

    level = one(*cuts[0])
    for cut in cuts[1:]:
        level = level * one(*cut)
    return level


def noise(key, dims, scale, bound, pieces=(), kind=jnp.bfloat16):
    loudness = block_levels(key, dims, pieces, -0.22, 0.18) if pieces else 1.0
    array = jax.random.normal(key, dims, jnp.float32) * scale * loudness
    return jnp.minimum(jnp.maximum(array, -bound), bound).astype(kind)


def heavy_noise(own_key, extent, spread, limit, cuts, heavy, kind=jnp.bfloat16):
    array = spread * jax.random.normal(own_key, extent, jnp.float32)
    if cuts:
        array = array * block_levels(own_key, extent, cuts, -0.22, 0.18)
    return jnp.clip(with_spikes(array, jax.random.fold_in(own_key, 3), *heavy), -limit, limit).astype(kind)


def setup_inputs(seed: int = 0) -> dict:
    seeds = jax.random.split(jax.random.key(seed), 6)
    amplitudes = noise(seeds[0], (OCC, OCC, PAIRS), 1.0, 6.0, ((0, 16), (2, 16)))
    integral_plus = heavy_noise(seeds[1], (PAIRS, SLAB), PAIRS ** -0.5, 0.078125, ((0, 16),), (0, 1, 16, 2.0))
    integral_minus = heavy_noise(seeds[2], (PAIRS, SLAB), PAIRS ** -0.5, 0.078125, ((0, 16),), (0, 1, 16, 2.0))
    cd_irrep = set_ends(jax.random.randint(seeds[3], (PAIRS // TILE,), 0, 4), jax.random.fold_in(seeds[3], 1), 0, 3).astype(jnp.int32)
    ab_irrep = set_ends(jax.random.randint(seeds[4], (SLAB // TILE,), 0, 4), jax.random.fold_in(seeds[4], 1), 0, 3).astype(jnp.int32)
    return dict(amplitudes=amplitudes, integral_plus=integral_plus, integral_minus=integral_minus, cd_irrep=cd_irrep, ab_irrep=ab_irrep)


def reference(amplitudes, integral_plus, integral_minus, cd_irrep, ab_irrep):
    wide = amplitudes.astype(jnp.float32)
    swapped = jnp.swapaxes(wide, 0, 1)
    amp_plus = (wide + swapped).astype(jnp.bfloat16).reshape(OCC * OCC, PAIRS)
    amp_minus = (wide - swapped).astype(jnp.bfloat16).reshape(OCC * OCC, PAIRS)
    tile_mask = (cd_irrep[:, None] == ab_irrep[None, :]).astype(jnp.bfloat16)
    width = KT_DEV * TILE
    slab_tiles = SLAB // TILE

    def masked(block, mask_rows):
        shaped = block.reshape(KT_DEV, TILE, slab_tiles, TILE) * mask_rows[:, None, :, None]
        return shaped.reshape(width, SLAB)

    def accumulate(total, index):
        start = (index * width).astype(jnp.int32)
        tile_start = (index * KT_DEV).astype(jnp.int32)
        mask_rows = lax.dynamic_slice_in_dim(tile_mask, tile_start, KT_DEV, 0)
        plus_block = masked(lax.dynamic_slice_in_dim(integral_plus, start, width, 0), mask_rows)
        minus_block = masked(lax.dynamic_slice_in_dim(integral_minus, start, width, 0), mask_rows)
        left_plus = lax.dynamic_slice_in_dim(amp_plus, start, width, 1)
        left_minus = lax.dynamic_slice_in_dim(amp_minus, start, width, 1)
        term = lax.dot_general(plus_block, left_plus, (((0,), (1,)), ((), ())), preferred_element_type=jnp.float32)
        term = term + lax.dot_general(minus_block, left_minus, (((0,), (1,)), ((), ())), preferred_element_type=jnp.float32)
        partial_k = (0.5 * term).astype(jnp.bfloat16)
        return total + partial_k.astype(jnp.float32), None

    total, _ = lax.scan(accumulate, jnp.zeros((SLAB, OCC * OCC), jnp.float32), jnp.arange(N_COL, dtype=jnp.int32))
    return total.astype(jnp.bfloat16)
```

```python
import functools

import jax
import jax.numpy as jnp
import numpy as np
from jax import lax
from jax.experimental import pallas as pl
from jax.experimental.pallas import tpu as pltpu
from jax.sharding import Mesh
from jax.sharding import PartitionSpec as P

TILE = 128
GROUP = 4
N_X = 2
VMEM = 48 * 2**20


def params():
    return pltpu.CompilerParams(vmem_limit_bytes=VMEM)


def send_order(rows):
    out = []
    for chunk in range(rows // GROUP):
        for r in range(GROUP):
            for jl in range(GROUP):
                for i in range(rows):
                    out.append((i * GROUP + r) * rows + chunk * GROUP + jl)
    return np.eye(GROUP * rows * rows, dtype=np.float32)[np.array(out)]


def receive_order(rows):
    out = [
        (s * GROUP + i) * rows + jl
        for i in range(GROUP)
        for s in range(GROUP)
        for jl in range(rows)
    ]
    return np.eye(GROUP * GROUP * rows, dtype=np.float32)[np.array(out)]


def pack_kernel(order_ref, amp_ref, *out_refs):
    rows, wide, width = amp_ref.shape
    block = amp_ref[...].reshape(rows * wide, width)
    per = out_refs[0].shape[0]
    for c, out_ref in enumerate(out_refs):
        out_ref[...] = jnp.dot(
            order_ref[c * per : (c + 1) * per, :], block, preferred_element_type=jnp.float32
        ).astype(out_ref.dtype)


def pack(amplitudes, order, count):
    rows, occ, width = amplitudes.shape
    steps = occ // (GROUP * rows)
    per = GROUP * GROUP * rows
    return pl.pallas_call(
        pack_kernel,
        grid=(steps,),
        in_specs=[
            pl.BlockSpec((count * per, order.shape[1]), lambda q: (0, 0)),
            pl.BlockSpec((rows, GROUP * rows, width), lambda q: (0, q, 0)),
        ],
        out_specs=[pl.BlockSpec((per, width), lambda q: (q, 0))] * count,
        out_shape=[jax.ShapeDtypeStruct((steps * per, width), jnp.bfloat16)] * count,
        compiler_params=params(),
        cost_estimate=pl.CostEstimate(
            flops=2 * count * steps * per * order.shape[1] * width,
            bytes_accessed=2 * (rows * occ * width + count * steps * per * width),
            transcendentals=0,
        ),
    )(order, amplitudes)


def mask_kernel(cd_ref, ab_ref, me_ref, plus_ref, minus_ref, out_ref):
    z = pl.program_id(0)
    me = me_ref[0]
    kt = cd_ref.shape[0]
    for half, ref in enumerate((plus_ref, minus_ref)):
        for w in range(N_X):
            lanes = pl.ds(pl.multiple_of((w ^ me) * TILE, TILE), TILE)
            for p in range(kt):
                rows = pl.ds((half * kt + p) * TILE, TILE)
                kept = cd_ref[p] == ab_ref[z * N_X + w]

                @pl.when(kept)
                def _():
                    out_ref[rows, lanes] = ref[p * TILE : (p + 1) * TILE, w * TILE : (w + 1) * TILE]

                @pl.when(jnp.logical_not(kept))
                def _():
                    out_ref[rows, lanes] = jnp.zeros((TILE, TILE), out_ref.dtype)


def mask(cd_irrep, ab_irrep, me, plus, minus):
    width, slab = plus.shape
    pair = N_X * TILE
    smem = pl.BlockSpec(memory_space=pltpu.SMEM)
    return pl.pallas_call(
        mask_kernel,
        grid=(slab // pair,),
        in_specs=[
            smem,
            smem,
            smem,
            pl.BlockSpec((width, pair), lambda z: (0, z)),
            pl.BlockSpec((width, pair), lambda z: (0, z)),
        ],
        out_specs=pl.BlockSpec((2 * width, pair), lambda z: (0, z)),
        out_shape=jax.ShapeDtypeStruct((2 * width, slab), jnp.bfloat16),
        compiler_params=params(),
        cost_estimate=pl.CostEstimate(
            flops=0, bytes_accessed=8 * width * slab, transcendentals=0
        ),
    )(cd_irrep, ab_irrep, me, plus, minus)


def ladder_kernel(order_ref, own_ref, received_ref, weight_ref, *refs):
    out_refs, both = refs[:-1], refs[-1]
    group, occ, width = own_ref.shape
    span = order_ref.shape[0]
    piece = span // group

    @pl.when(pl.program_id(0) == 0)
    def _():
        for q in range(occ // piece):
            other = jnp.dot(
                order_ref[...],
                received_ref[q * span : (q + 1) * span, :],
                preferred_element_type=jnp.float32,
            )
            for i in range(group):
                cols = slice(q * piece, (q + 1) * piece)
                own = own_ref[i, cols, :].astype(jnp.float32)
                swap = other[i * piece : (i + 1) * piece]
                rows = slice(i * occ + q * piece, i * occ + (q + 1) * piece)
                both[rows, :width] = (own + swap).astype(jnp.bfloat16)
                both[rows, width:] = (own - swap).astype(jnp.bfloat16)

    for i in range(group):
        rows = slice(i * occ, (i + 1) * occ)
        term = 0.5 * jnp.dot(both[rows, :], weight_ref[...], preferred_element_type=jnp.float32)
        for w in range(N_X):
            half = term[:, w * TILE : (w + 1) * TILE].astype(jnp.bfloat16)
            if len(out_refs) == 1:
                out_refs[0][0, w, rows, :] = half
            else:
                out_refs[w][0, rows, :] = half


def ladder(order, amplitudes, received, weights, chunk, apart):
    _, occ, width = amplitudes.shape
    rows = GROUP * occ
    pair = N_X * TILE
    steps = weights.shape[1] // pair
    if apart:
        out = [jax.ShapeDtypeStruct((steps, rows, TILE), jnp.bfloat16)] * N_X
        out_specs = [pl.BlockSpec((1, rows, TILE), lambda z: (z, 0, 0))] * N_X
    else:
        out = jax.ShapeDtypeStruct((steps, N_X, rows, TILE), jnp.bfloat16)
        out_specs = pl.BlockSpec((1, N_X, rows, TILE), lambda z: (z, 0, 0, 0))
    return pl.pallas_call(
        ladder_kernel,
        grid=(steps,),
        in_specs=[
            pl.BlockSpec(order.shape, lambda z: (0, 0)),
            pl.BlockSpec((GROUP, occ, width), lambda z: (chunk, 0, 0)),
            pl.BlockSpec((rows, width), lambda z: (0, 0)),
            pl.BlockSpec((2 * width, pair), lambda z: (0, z)),
        ],
        out_specs=out_specs,
        out_shape=out,
        scratch_shapes=[pltpu.VMEM((rows, 2 * width), jnp.bfloat16)],
        compiler_params=params(),
        cost_estimate=pl.CostEstimate(
            flops=4 * rows * width * steps * pair,
            bytes_accessed=4 * rows * width + 4 * width * steps * pair + 2 * rows * steps * pair,
            transcendentals=0,
        ),
    )(order, amplitudes, received, weights)


def finish_kernel(a0, a1, b0, c0, c1, out_ref):
    rows = b0.shape[0]
    first = a0[...].astype(jnp.float32) + a1[...].astype(jnp.float32)
    last = c0[...].astype(jnp.float32) + c1[...].astype(jnp.float32)
    for k, part in enumerate((first, b0[...].astype(jnp.float32), last)):
        out_ref[:, k * rows : (k + 1) * rows] = part.T.astype(out_ref.dtype)


def on_device(order_out, order_in, amplitudes, integral_plus, integral_minus, cd_irrep, ab_irrep):
    me = lax.axis_index("xl").reshape(1).astype(jnp.int32)
    swap = functools.partial(lax.ppermute, axis_name="xl", perm=[(0, 1), (1, 0)])
    per = order_in.shape[0]

    def exchange(packed):
        return lax.all_to_all(packed, "row", split_axis=0, concat_axis=0, tiled=True)

    def scatter(part):
        return lax.psum_scatter(part, "z", scatter_dimension=0, tiled=True)

    (packed0,) = pack(amplitudes, order_out[:per], 1)
    received0 = exchange(packed0)
    packed1, packed2 = pack(amplitudes, order_out[per:], 2)
    weights = mask(cd_irrep, ab_irrep, me, integral_plus, integral_minus)
    received0, packed1, packed2, weights = lax.optimization_barrier(
        (received0, packed1, packed2, weights)
    )
    received1 = exchange(packed1)
    sum0 = scatter(ladder(order_in, amplitudes, received0, weights, 0, False))
    received1, packed2 = lax.optimization_barrier((received1, packed2))
    received2 = exchange(packed2)
    near1, far1 = ladder(order_in, amplitudes, received1, weights, 1, True)
    other1 = swap(far1)
    sum2 = scatter(ladder(order_in, amplitudes, received2, weights, 2, False))
    sum1 = scatter(
        (near1.astype(jnp.float32) + other1.astype(jnp.float32)).astype(jnp.bfloat16)
    )
    last0 = swap(sum0[0, 1])
    last2 = swap(sum2[0, 1])
    rows = sum1.shape[1]
    return pl.pallas_call(
        finish_kernel,
        out_shape=jax.ShapeDtypeStruct((TILE, 3 * rows), jnp.bfloat16),
        compiler_params=params(),
    )(sum0[0, 0], last0, sum1[0], sum2[0, 0], last2)


def solution(mesh):
    rows, cols = mesh.shape["row"], mesh.shape["col"]
    fine = Mesh(mesh.devices.reshape(rows, cols // N_X, N_X), ("row", "z", "xl"))

    def program(amplitudes, integral_plus, integral_minus, cd_irrep, ab_irrep):
        own = amplitudes.shape[0] // rows
        order_out = jnp.asarray(send_order(own), jnp.bfloat16)
        order_in = jnp.asarray(receive_order(own), jnp.bfloat16)
        col = ("z", "xl")
        return jax.shard_map(
            on_device,
            mesh=fine,
            in_specs=(P(), P(), P("row", None, col), P(col, None), P(col, None), P(col), P()),
            out_specs=P(col, "row"),
            check_vma=False,
        )(order_out, order_in, amplitudes, integral_plus, integral_minus, cd_irrep, ab_irrep)

    return program
```

```python
import functools

import jax
import jax.numpy as jnp
import numpy as np
from jax import lax
from jax.experimental import pallas as pl
from jax.experimental.pallas import tpu as pltpu
from jax.sharding import Mesh
from jax.sharding import PartitionSpec as P

TILE = 128
GROUP = 4
N_X = 2
PAIR = N_X * TILE
FIRST = 5


def params(mib=16):
    return pltpu.CompilerParams(vmem_limit_bytes=mib * 2**20)


def send_order(rows):
    return [
        (i * GROUP + r) * rows + chunk * GROUP + jl
        for chunk in range(rows // GROUP)
        for r in range(GROUP)
        for jl in range(GROUP)
        for i in range(rows)
    ]


def receive_order(rows):
    return [
        (s * GROUP + i) * rows + jl
        for i in range(GROUP)
        for s in range(GROUP)
        for jl in range(rows)
    ]


def column(places):
    return jnp.asarray(np.array(places, np.int32)[:, None])


def picker(places, width):
    lanes = lax.broadcasted_iota(jnp.int32, (places.shape[0], width), 1)
    return jnp.where(lanes == places, 1.0, 0.0).astype(jnp.bfloat16)


def pack_kernel(order_ref, *refs):
    count = 4
    amp_refs, out_refs = refs[:count], refs[count:]
    block = jnp.concatenate(
        [r[...].reshape(r.shape[0] * r.shape[1], r.shape[2]) for r in amp_refs], 0
    )
    per = out_refs[0].shape[0]
    for c, out_ref in enumerate(out_refs):
        order = picker(order_ref[c * per : (c + 1) * per, :], block.shape[0])
        out_ref[...] = jnp.dot(order, block, preferred_element_type=jnp.float32).astype(
            out_ref.dtype
        )


def pack(amplitudes, order, mib):
    rows, occ, width = amplitudes.shape
    steps = occ // (GROUP * rows)
    per = GROUP * GROUP * rows
    count = order.shape[0] // per
    return pl.pallas_call(
        pack_kernel,
        grid=(steps,),
        in_specs=[pl.BlockSpec(order.shape, lambda q: (0, 0))]
        + [
            pl.BlockSpec((rows // 4, GROUP * rows, width), lambda q, k=k: (k, q, 0))
            for k in range(4)
        ],
        out_specs=[pl.BlockSpec((per, width), lambda q: (q, 0))] * count,
        out_shape=[jax.ShapeDtypeStruct((steps * per, width), jnp.bfloat16)] * count,
        compiler_params=params(mib),
        cost_estimate=pl.CostEstimate(
            flops=2 * count * steps * per * GROUP * rows * rows * width,
            bytes_accessed=2 * (rows * occ * width + count * steps * per * width),
            transcendentals=0,
        ),
    )(order, *[amplitudes] * 4)


def mask_kernel(cd_ref, ab_ref, me_ref, plus_ref, minus_ref, out_ref):
    p = pl.program_id(0)
    me = me_ref[0]
    for q in range(out_ref.shape[0] * N_X):
        z, w = q // N_X, q % N_X
        lanes = pl.ds(pl.multiple_of((w ^ me) * TILE, TILE), TILE)
        kept = cd_ref[p] == ab_ref[q]

        @pl.when(kept)
        def _():
            for half, ref in enumerate((plus_ref, minus_ref)):
                out_ref[z, half, :, lanes] = ref[:, q * TILE : (q + 1) * TILE]

        @pl.when(jnp.logical_not(kept))
        def _():
            for half in range(2):
                out_ref[z, half, :, lanes] = jnp.zeros((TILE, TILE), out_ref.dtype)


def mask(cd_irrep, ab_irrep, me, plus, minus):
    width, slab = plus.shape
    smem = pl.BlockSpec(memory_space=pltpu.SMEM)
    masked = pl.pallas_call(
        mask_kernel,
        grid=(width // TILE,),
        in_specs=[smem] * 3 + [pl.BlockSpec((TILE, slab), lambda p: (p, 0))] * 2,
        out_specs=pl.BlockSpec((slab // PAIR, 2, TILE, PAIR), lambda p: (0, 0, p, 0)),
        out_shape=jax.ShapeDtypeStruct((slab // PAIR, 2, width, PAIR), jnp.bfloat16),
        compiler_params=params(),
        cost_estimate=pl.CostEstimate(
            flops=0, bytes_accessed=8 * width * slab, transcendentals=0
        ),
    )(cd_irrep, ab_irrep, me, plus, minus)
    return masked.reshape(slab // PAIR, 2 * width, PAIR)


def ladder_kernel(target_ref, order_ref, own_ref, received_ref, weight_ref, *refs):
    out_refs, both = refs[:-1], refs[-1]
    group, occ, width = own_ref.shape
    span = order_ref.shape[0]
    piece = span // group
    step = pl.program_id(0)

    @pl.when(step == 0)
    def _():
        order = picker(order_ref[...], span)
        for q in range(occ // piece):
            other = jnp.dot(
                order,
                received_ref[q * span : (q + 1) * span, :],
                preferred_element_type=jnp.float32,
            )
            for i in range(group):
                cols = slice(q * piece, (q + 1) * piece)
                own = own_ref[i, cols, :].astype(jnp.float32)
                swap = other[i * piece : (i + 1) * piece]
                rows = slice(i * occ + q * piece, i * occ + (q + 1) * piece)
                both[rows, :width] = (own + swap).astype(jnp.bfloat16)
                both[rows, width:] = (own - swap).astype(jnp.bfloat16)

    term = 0.5 * jnp.dot(both[...], weight_ref[0], preferred_element_type=jnp.float32)
    near = term[:, :TILE].astype(jnp.bfloat16)
    far = term[:, TILE:].astype(jnp.bfloat16)
    if len(out_refs) == 1:
        out_refs[0][0, 0] = near
        out_refs[0][0, 1] = far
    else:
        near_ref, early_ref, late_ref = out_refs
        near_ref[0] = near

        @pl.when(step < FIRST)
        def _():
            early_ref[0] = far

        @pl.when(step >= FIRST)
        def _():
            late_ref[0] = far


def ladder(targets, order, amplitudes, received, weights, chunk, apart):
    _, occ, width = amplitudes.shape
    rows = GROUP * occ
    steps = weights.shape[0]
    if apart:
        counts = (steps, FIRST, steps - FIRST)
        out = [jax.ShapeDtypeStruct((n, rows, TILE), jnp.bfloat16) for n in counts]
        block = (1, rows, TILE)
        out_specs = [
            pl.BlockSpec(block, lambda g, t: (g, 0, 0)),
            pl.BlockSpec(block, lambda g, t: (jnp.minimum(g, FIRST - 1), 0, 0)),
            pl.BlockSpec(block, lambda g, t: (jnp.maximum(g - FIRST, 0), 0, 0)),
        ]
    else:
        out = jax.ShapeDtypeStruct((steps, N_X, rows, TILE), jnp.bfloat16)
        out_specs = pl.BlockSpec((1, N_X, rows, TILE), lambda g, t: (g, 0, 0, 0))
    return pl.pallas_call(
        ladder_kernel,
        grid_spec=pltpu.PrefetchScalarGridSpec(
            num_scalar_prefetch=1,
            grid=(steps,),
            in_specs=[
                pl.BlockSpec(order.shape, lambda g, t: (0, 0)),
                pl.BlockSpec((GROUP, occ, width), lambda g, t: (chunk, 0, 0)),
                pl.BlockSpec((rows, width), lambda g, t: (0, 0)),
                pl.BlockSpec((1, 2 * width, PAIR), lambda g, t: (t[g], 0, 0)),
            ],
            out_specs=out_specs,
            scratch_shapes=[pltpu.VMEM((rows, 2 * width), jnp.bfloat16)],
        ),
        out_shape=out,
        compiler_params=params(),
        cost_estimate=pl.CostEstimate(
            flops=4 * rows * width * steps * PAIR,
            bytes_accessed=4 * rows * width + 4 * width * steps * PAIR + 2 * rows * steps * PAIR,
            transcendentals=0,
        ),
    )(targets, order, amplitudes, received, weights)


def finish_kernel(*refs):
    out_ref = refs[-1]
    at = 0
    for names in ((0, 1), (2, 3, 4, 5), (6, 7)):
        total = 0.0
        for n in names:
            part = refs[n][...].astype(jnp.float32)
            total = total + part.reshape(part.shape[-2:])
        rows = total.shape[0]
        out_ref[:, at : at + rows] = total.T.astype(out_ref.dtype)
        at += rows


def finish(sum0, last0, near1, late1, up1, down1, sum2, last2):
    rows = last0.shape[0]
    whole = pl.BlockSpec((rows, TILE), lambda g: (0, 0))
    last = near1.shape[0] - 1
    late = late1.shape[0] - 1
    scattered = pl.BlockSpec((1, 1, rows, TILE), lambda g: (0, 0, 0, 0))
    return pl.pallas_call(
        finish_kernel,
        grid=(1,),
        in_specs=[
            scattered,
            whole,
            pl.BlockSpec((1, rows, TILE), lambda g: (last, 0, 0)),
            pl.BlockSpec((1, rows, TILE), lambda g: (late, 0, 0)),
            whole,
            whole,
            scattered,
            whole,
        ],
        out_specs=pl.BlockSpec((TILE, 3 * rows), lambda g: (0, 0)),
        out_shape=jax.ShapeDtypeStruct((TILE, 3 * rows), jnp.bfloat16),
        compiler_params=params(),
    )(sum0, last0, near1, late1, up1, down1, sum2, last2)


def add(*parts):
    total = parts[0].astype(jnp.float32)
    for part in parts[1:]:
        total = total + part.astype(jnp.float32)
    return total.astype(jnp.bfloat16)


def on_device(n_z, order_out, order_in, amplitudes, integral_plus, integral_minus, cd_irrep, ab_irrep):
    me = lax.axis_index("xl").reshape(1).astype(jnp.int32)
    place = lax.axis_index("z").astype(jnp.int32)
    half = n_z // 2
    away = [half]
    for d in range(half - 1, 0, -1):
        away += [d, -d]
    away.append(0)
    fixed = jnp.arange(n_z, dtype=jnp.int32)
    turned = (place + jnp.array(away, jnp.int32)) % n_z
    swap = functools.partial(lax.ppermute, axis_name="xl", perm=[(0, 1), (1, 0)])
    up = functools.partial(
        lax.ppermute, axis_name="z", perm=[(k, (k + 1) % n_z) for k in range(n_z)]
    )
    down = functools.partial(
        lax.ppermute, axis_name="z", perm=[((k + 1) % n_z, k) for k in range(n_z)]
    )
    per = GROUP * GROUP * amplitudes.shape[0]

    def exchange(packed):
        return lax.all_to_all(packed, "row", split_axis=0, concat_axis=0, tiled=True)

    def scatter(part):
        return lax.psum_scatter(part, "z", scatter_dimension=0, tiled=True)

    (packed0,) = pack(amplitudes, order_out[:per], 60)
    received0 = exchange(packed0)
    packed1, packed2 = pack(amplitudes, order_out[per:], 16)
    weights = mask(cd_irrep, ab_irrep, me, integral_plus, integral_minus)
    received0, packed1, packed2, weights = lax.optimization_barrier(
        (received0, packed1, packed2, weights)
    )
    part0 = ladder(fixed, order_in, amplitudes, received0, weights, 0, False)
    sum0 = scatter(part0)
    received1 = exchange(packed1)
    received1, packed2, _ = lax.optimization_barrier((received1, packed2, part0))
    near1, early1, late1 = ladder(turned, order_in, amplitudes, received1, weights, 1, True)
    early1 = swap(early1)
    late1 = swap(late1)
    received2 = exchange(packed2)
    received2, early1 = lax.optimization_barrier((received2, early1))
    sum2 = scatter(ladder(fixed, order_in, amplitudes, received2, weights, 2, False))

    middle = near1.shape[1] // 2
    top = ((0, middle), (0, 0))
    bottom = ((middle, 0), (0, 0))

    def send(goes_up, goes_down):
        goes_up, goes_down = lax.optimization_barrier((goes_up, goes_down))
        return lax.optimization_barrier((up(goes_up), down(goes_down)))

    goes_up, goes_down = send(
        add(near1[0, :middle], early1[0, :middle]), add(near1[0, middle:], early1[0, middle:])
    )
    goes_up, goes_down = jnp.pad(goes_up, top), jnp.pad(goes_down, bottom)
    for step in range(1, half):
        a, b = 2 * step - 1, 2 * step
        if step == half - 2:
            goes_up, goes_down, late1 = lax.optimization_barrier((goes_up, goes_down, late1))
        far_a, far_b = (early1[n] if n < FIRST else late1[n - FIRST] for n in (a, b))
        goes_up, goes_down = send(
            add(near1[a], far_a, goes_up), add(near1[b], far_b, goes_down)
        )

    last0 = swap(sum0[0, 1])
    last2 = swap(sum2[0, 1])
    return finish(sum0, last0, near1, late1, goes_up, goes_down, sum2, last2)


def solution(mesh):
    rows, cols = mesh.shape["row"], mesh.shape["col"]
    n_z = cols // N_X
    fine = Mesh(mesh.devices.reshape(rows, n_z, N_X), ("row", "z", "xl"))

    def program(amplitudes, integral_plus, integral_minus, cd_irrep, ab_irrep):
        own = amplitudes.shape[0] // rows
        order_out = column(send_order(own))
        order_in = column(receive_order(own))
        col = ("z", "xl")
        return jax.shard_map(
            functools.partial(on_device, n_z),
            mesh=fine,
            in_specs=(P(), P(), P("row", None, col), P(col, None), P(col, None), P(col), P()),
            out_specs=P(col, "row"),
            check_vma=False,
        )(order_out, order_in, amplitudes, integral_plus, integral_minus, cd_irrep, ab_irrep)

    return program
```

```python
import functools

import jax
import jax.numpy as jnp
import numpy as np
from jax import lax
from jax.experimental import pallas as pl
from jax.experimental.pallas import tpu as pltpu
from jax.sharding import Mesh
from jax.sharding import PartitionSpec as P

TILE = 128
N_X = 2
PAIR = N_X * TILE
N_P = 4
N_Y = 4
FIRST = 5
VMEM = 60 * 2**20
SHIFTS = (0, 1, 3, 2)

SIDE, PLACE, TO, FROM, TARGETS = 0, 1, 2, 2 + N_Y, 2 + 2 * N_Y


def distances(n_z):
    away = [n_z // 2]
    for d in range(n_z // 2 - 1, 0, -1):
        away += [d, -d]
    return away + [0]


def positions(rows, n_z):
    table = []
    for row in range(rows):
        y, p = divmod(row, N_P)
        for z in range(n_z):
            for x in range(N_X):
                table.append(
                    [x, p]
                    + [(y + s) % N_Y for s in SHIFTS]
                    + [(y - s) % N_Y for s in SHIFTS]
                    + list(range(n_z))
                    + [(z + d) % n_z for d in distances(n_z)]
                )
    return np.array(table, np.int32)


def params():
    return pltpu.CompilerParams(vmem_limit_bytes=VMEM)


def send_order(rows):
    return np.array(
        [
            [
                (i * N_P + (p ^ m)) * rows + jl
                for m in range(N_P)
                for jl in range(rows)
                for i in range(rows)
            ]
            for p in range(N_P)
        ],
        np.int32,
    )[:, :, None]


def receive_order(rows):
    return np.array(
        [
            [
                ((p ^ s) * rows + i) * rows + jl
                for i in range(rows)
                for s in range(N_P)
                for jl in range(rows)
            ]
            for p in range(N_P)
        ],
        np.int32,
    )[:, :, None]


def picker(places):
    size = places.shape[0]
    lanes = lax.broadcasted_iota(jnp.int32, (size, size), 1)
    return jnp.where(lanes == places, 1.0, 0.0).astype(jnp.bfloat16)


def pack_kernel(info_ref, order_ref, *refs):
    count = len(refs) // (1 + N_P)
    order = picker(order_ref[0])
    for amp_ref, out_refs in zip(refs[:count], [refs[count + N_P * k :] for k in range(count)]):
        rows, wide, width = amp_ref.shape
        block = amp_ref[...].reshape(rows * wide, width)
        sent = jnp.dot(order, block, preferred_element_type=jnp.float32)
        for m in range(N_P):
            out_refs[m][...] = sent[m * rows * rows : (m + 1) * rows * rows].astype(jnp.bfloat16)


def pack(info, order, amplitudes, first, count):
    rows, _, width = amplitudes.shape
    wide = N_P * rows
    out = jax.ShapeDtypeStruct((rows * rows, width), jnp.bfloat16)
    sent = pl.pallas_call(
        pack_kernel,
        grid_spec=pltpu.PrefetchScalarGridSpec(
            num_scalar_prefetch=1,
            grid=(1,),
            in_specs=[pl.BlockSpec((1, rows * wide, 1), lambda g, w: (w[PLACE], 0, 0))]
            + [
                pl.BlockSpec((rows, wide, width), lambda g, w, k=k: (0, w[TO + first + k], 0))
                for k in range(count)
            ],
            out_specs=[pl.BlockSpec(out.shape, lambda g, w: (0, 0))] * (N_P * count),
        ),
        out_shape=[out] * (N_P * count),
        compiler_params=params(),
        cost_estimate=pl.CostEstimate(
            flops=0, bytes_accessed=4 * count * rows * wide * width, transcendentals=0
        ),
    )(info, order, *[amplitudes] * count)
    return [sent[N_P * k : N_P * (k + 1)] for k in range(count)]


def ladder_kernel(n_out, plane, targets, info_ref, cd_ref, ab_ref, order_ref, amp_ref, *refs):
    got_refs = refs[:N_P]
    plus_ref, minus_ref = refs[N_P : N_P + 2]
    out_refs = refs[N_P + 2 : N_P + 2 + n_out]
    own, got, weights, both, staged, own_sem, got_sem, weight_sem, out_sem = refs[N_P + 2 + n_out :]
    rows, wide, width = own.shape
    steps = weights.shape[0]
    kt = width // TILE
    me = info_ref[SIDE]
    blocks = rows * rows

    fetch = [
        pltpu.make_async_copy(
            amp_ref.at[:, pl.ds(pl.multiple_of(info_ref[plane] * wide, 16), wide), :], own, own_sem
        )
    ]
    for m in range(N_P):
        fetch.append(
            pltpu.make_async_copy(
                got_refs[m], got.at[m * blocks : (m + 1) * blocks, :], got_sem.at[m]
            )
        )
    loads = []
    for g in range(steps):
        lanes = pl.ds(pl.multiple_of(info_ref[targets + g] * PAIR, PAIR), PAIR)
        loads.append(
            [
                pltpu.make_async_copy(
                    ref.at[:, lanes],
                    weights.at[g, half * width : (half + 1) * width, :],
                    weight_sem.at[g, half],
                )
                for half, ref in enumerate((plus_ref, minus_ref))
            ]
        )
    for copy in fetch:
        copy.start()
    for pair in loads:
        for copy in pair:
            copy.start()
    order = picker(order_ref[0])
    for copy in fetch:
        copy.wait()
    other = jnp.dot(order, got[...], preferred_element_type=jnp.float32)
    mine = own[...].reshape(rows * wide, width).astype(jnp.float32)
    both[:, :width] = (mine + other).astype(jnp.bfloat16)
    both[:, width:] = (mine - other).astype(jnp.bfloat16)

    stores = []
    for g in range(steps):
        for copy in loads[g]:
            copy.wait()
        for w in range(N_X):
            irrep = ab_ref[info_ref[targets + g] * N_X + w]
            for p in range(kt):

                @pl.when(cd_ref[p] != irrep)
                def _():
                    for half in range(2):
                        weights[
                            g,
                            half * width + p * TILE : half * width + (p + 1) * TILE,
                            w * TILE : (w + 1) * TILE,
                        ] = jnp.zeros((TILE, TILE), weights.dtype)

        term = 0.5 * jnp.dot(both[...], weights[g], preferred_element_type=jnp.float32)
        left, right = term[:, :TILE], term[:, TILE:]
        staged[g, 0] = jnp.where(me == 0, left, right).astype(staged.dtype)
        staged[g, 1] = jnp.where(me == 0, right, left).astype(staged.dtype)
        if n_out == 1:
            copies = [pltpu.make_async_copy(staged.at[g], out_refs[0].at[g], out_sem.at[g, 0])]
        else:
            far = out_refs[1].at[g] if g < FIRST else out_refs[2].at[g - FIRST]
            copies = [
                pltpu.make_async_copy(staged.at[g, 0], out_refs[0].at[g], out_sem.at[g, 0]),
                pltpu.make_async_copy(staged.at[g, 1], far, out_sem.at[g, 1]),
            ]
        for copy in copies:
            copy.start()
        stores += copies
    for copy in stores:
        copy.wait()


def ladder(info, cd_irrep, ab_irrep, order, amplitudes, received, plus, minus, plane, targets, apart):
    rows, _, width = amplitudes.shape
    wide = N_P * rows
    total = rows * wide
    steps = plus.shape[1] // PAIR
    if apart:
        shapes = [(steps, total, TILE), (FIRST, total, TILE), (steps - FIRST, total, TILE)]
    else:
        shapes = [(steps, N_X, total, TILE)]
    smem = pl.BlockSpec(memory_space=pltpu.SMEM)
    hbm = pl.BlockSpec(memory_space=pl.ANY)
    dma = pltpu.SemaphoreType.DMA
    return pl.pallas_call(
        functools.partial(ladder_kernel, len(shapes), plane, targets),
        grid_spec=pltpu.PrefetchScalarGridSpec(
            num_scalar_prefetch=1,
            grid=(1,),
            in_specs=[smem, smem, pl.BlockSpec((1, total, 1), lambda k, w: (w[PLACE], 0, 0))]
            + [hbm] * (1 + N_P + 2),
            out_specs=[hbm] * len(shapes),
            scratch_shapes=[
                pltpu.VMEM((rows, wide, width), jnp.bfloat16),
                pltpu.VMEM((total, width), jnp.bfloat16),
                pltpu.VMEM((steps, 2 * width, PAIR), jnp.bfloat16),
                pltpu.VMEM((total, 2 * width), jnp.bfloat16),
                pltpu.VMEM((steps, N_X, total, TILE), jnp.bfloat16),
                dma,
                dma((N_P,)),
                dma((steps, 2)),
                dma((steps, 2)),
            ],
        ),
        out_shape=[jax.ShapeDtypeStruct(s, jnp.bfloat16) for s in shapes],
        compiler_params=params(),
        cost_estimate=pl.CostEstimate(
            flops=0, bytes_accessed=4 * total * width, transcendentals=0
        ),
    )(info, cd_irrep, ab_irrep, order, amplitudes, *received, plus, minus)


def finish_kernel(info_ref, *refs):
    groups, out_ref, whole = refs[:-2], refs[-2], refs[-1]
    rows, occ, tile = whole.shape
    wide = occ // N_Y
    at = 0
    for k, count in enumerate(FINISH):
        total = 0.0
        for ref in groups[at : at + count]:
            part = ref[...].astype(jnp.float32)
            total = total + part.reshape(rows, wide, tile)
        at += count
        whole[:, pl.ds(pl.multiple_of(info_ref[FROM + k] * wide, 16), wide), :] = total
    out_ref[...] = whole[...].reshape(rows * occ, tile).T.astype(out_ref.dtype)


FINISH = (2, 4, 2, 4)


def finish(info, rows, occ, terms):
    vmem = pl.BlockSpec(memory_space=pltpu.VMEM)
    return pl.pallas_call(
        finish_kernel,
        in_specs=[pl.BlockSpec(memory_space=pltpu.SMEM)] + [vmem] * len(terms),
        out_specs=vmem,
        out_shape=jax.ShapeDtypeStruct((TILE, rows * occ), jnp.bfloat16),
        scratch_shapes=[pltpu.VMEM((rows, occ, TILE), jnp.float32)],
        compiler_params=params(),
    )(info, *terms)


def add(*parts):
    total = parts[0].astype(jnp.float32)
    for part in parts[1:]:
        total = total + part.astype(jnp.float32)
    return total.astype(jnp.bfloat16)


def on_device(n_z, info, order_out, order_in, amplitudes, plus, minus, cd_irrep, ab_irrep):
    rows, occ, _ = amplitudes.shape
    info = info.reshape(-1)
    half = n_z // 2
    fixed, turned = TARGETS, TARGETS + n_z
    swap = functools.partial(lax.ppermute, axis_name="xl", perm=[(0, 1), (1, 0)])
    up = functools.partial(
        lax.ppermute, axis_name="z", perm=[(k, (k + 1) % n_z) for k in range(n_z)]
    )
    down = functools.partial(
        lax.ppermute, axis_name="z", perm=[((k + 1) % n_z, k) for k in range(n_z)]
    )

    def scatter(part):
        return lax.psum_scatter(part, "z", scatter_dimension=0, tiled=True)

    def exchange(blocks, shift):
        got = []
        for m, block in enumerate(blocks):
            if (shift, m) != (0, 0):
                perm = [
                    (a * N_P + b, (a + shift) % N_Y * N_P + (b ^ m))
                    for a in range(N_Y)
                    for b in range(N_P)
                ]
                block = lax.ppermute(block, "row", perm)
            got.append(block)
        return got

    def product(k, received, targets, apart=False):
        return ladder(
            info, cd_irrep, ab_irrep, order_in, amplitudes, received, plus, minus, FROM + k, targets, apart
        )

    def send(goes_up, goes_down):
        goes_up, goes_down = lax.optimization_barrier((goes_up, goes_down))
        return lax.optimization_barrier((up(goes_up), down(goes_down)))

    def set_out(terms):
        first = terms(0)
        return send(add(*[t[:1] for t in first]), add(*[t[1:] for t in first]))

    def go_on(terms, goes_up, goes_down):
        goes_up = jnp.pad(goes_up, ((0, 1), (0, 0), (0, 0)))
        goes_down = jnp.pad(goes_down, ((1, 0), (0, 0), (0, 0)))
        for step in range(1, half):
            goes_up, goes_down = send(
                add(goes_up, *terms(2 * step - 1)), add(goes_down, *terms(2 * step))
            )
        return goes_up, goes_down

    (sent0,) = pack(info, order_out, amplitudes, 0, 1)
    received0 = exchange(sent0, SHIFTS[0])
    sent0, later = lax.optimization_barrier((sent0, amplitudes))
    sent1, sent2 = pack(info, order_out, later, 1, 2)
    received1 = exchange(sent1, SHIFTS[1])
    received2 = exchange(sent2, SHIFTS[2])
    sent1, later = lax.optimization_barrier((sent1, later))
    (sent3,) = pack(info, order_out, later, 3, 1)
    received3 = exchange(sent3, SHIFTS[3])

    received0, ahead, _ = lax.optimization_barrier((received0, received1[:2], (sent2, sent3)))
    received1 = ahead + received1[2:]
    (part0,) = product(0, received0, fixed)
    sum0 = scatter(part0)
    received1, _ = lax.optimization_barrier((received1, part0))
    (part1,) = product(1, received1, turned)

    def whole(k):
        return (part1[k],)

    away1 = set_out(whole)
    received2, ahead, away1 = lax.optimization_barrier((received2, received3[:2], away1))
    received3 = ahead + received3[2:]
    (part2,) = product(2, received2, fixed)
    sum2 = scatter(part2)
    received3, _ = lax.optimization_barrier((received3, part2))
    near3, early3, late3 = product(3, received3, turned, True)
    early3, late3 = swap(early3), swap(late3)

    up1, down1 = go_on(whole, *away1)

    def halves(k):
        far = early3[k] if k < FIRST else late3[k - FIRST]
        return [t.reshape(2, -1, TILE) for t in (near3[k], far)]

    up3, down3 = go_on(halves, *set_out(halves))

    last = n_z - 1
    far0 = swap(sum0[0, 1])
    far1 = swap(add(part1[last, 1], up1[1], down1[1]))
    far2 = swap(sum2[0, 1])
    terms = (
        (sum0[0, 0], far0),
        (part1[last, 0], up1[0], down1[0], far1),
        (sum2[0, 0], far2),
        (near3[last], late3[last - FIRST], up3, down3),
    )
    return finish(info, rows, occ, [t for group in terms for t in group])


def solution(mesh):
    rows, cols = mesh.shape["row"], mesh.shape["col"]
    n_z = cols // N_X
    fine = Mesh(mesh.devices.reshape(rows, n_z, N_X), ("row", "z", "xl"))

    def program(amplitudes, integral_plus, integral_minus, cd_irrep, ab_irrep):
        own = amplitudes.shape[0] // rows
        col = ("z", "xl")
        return jax.shard_map(
            functools.partial(on_device, n_z),
            mesh=fine,
            in_specs=(P(("row",) + col), P(), P(), P("row", None, col), P(col, None), P(col, None), P(col), P()),
            out_specs=P(col, "row"),
            check_vma=False,
        )(
            jnp.asarray(positions(rows, n_z)),
            jnp.asarray(send_order(own)),
            jnp.asarray(receive_order(own)),
            amplitudes,
            integral_plus,
            integral_minus,
            cd_irrep,
            ab_irrep,
        )

    return program
```

```python
import functools

import jax
import jax.numpy as jnp
import numpy as np
from jax import lax
from jax.experimental import pallas as pl
from jax.experimental.pallas import tpu as pltpu
from jax.sharding import Mesh
from jax.sharding import PartitionSpec as P

TILE = 128
N_X = 2
PAIR = N_X * TILE
N_S = 4
N_IRREP = 4
CUTS = 2
VMEM = 60 * 2**20


def params():
    return pltpu.CompilerParams(vmem_limit_bytes=VMEM)


def send_order(rows, first, n_i):
    return column(
        (i * N_S + s) * rows + first + jl
        for s in range(N_S)
        for jl in range(n_i)
        for i in range(rows)
    )


def receive_order(rows, chunk, first, n_i):
    return column(
        (s * chunk + first + i) * rows + jl
        for i in range(n_i)
        for s in range(N_S)
        for jl in range(rows)
    )


def column(places):
    return jnp.asarray(np.array(list(places), np.int32)[:, None])


def pack_kernel(order_ref, *refs):
    amp_refs, out_ref = refs[:-1], refs[-1]
    block = jnp.concatenate(
        [r[...].reshape(r.shape[0] * r.shape[1], r.shape[2]) for r in amp_refs], 0
    )
    order = picker(order_ref[...], block.shape[0])
    out_ref[...] = jnp.dot(order, block, preferred_element_type=jnp.float32).astype(out_ref.dtype)


def pack(order, amplitudes):
    rows, occ, width = amplitudes.shape
    wide = N_S * rows
    steps = occ // wide
    per = order.shape[0]
    parts = 4
    return pl.pallas_call(
        pack_kernel,
        grid=(steps,),
        in_specs=[pl.BlockSpec(order.shape, lambda q: (0, 0))]
        + [
            pl.BlockSpec((rows // parts, wide, width), lambda q, k=k: (k, q, 0))
            for k in range(parts)
        ],
        out_specs=pl.BlockSpec((per, width), lambda q: (q, 0)),
        out_shape=jax.ShapeDtypeStruct((steps * per, width), jnp.bfloat16),
        compiler_params=params(),
        cost_estimate=pl.CostEstimate(
            flops=0, bytes_accessed=4 * rows * occ * width, transcendentals=0
        ),
    )(order, *[amplitudes] * parts)


def picker(places, width):
    lanes = lax.broadcasted_iota(jnp.int32, (places.shape[0], width), 1)
    return jnp.where(lanes == places, 1.0, 0.0).astype(jnp.bfloat16)

def ladder_kernel(joined, row_block, first, me_ref, cd_ref, ab_ref, order_ref, amp_ref, got_ref, plus_ref, minus_ref, *refs):
    n_out = 1 if joined else 2
    out_refs = refs[:n_out]
    own, got, held, both, packed, staged, lists, counts, load_sem, out_sem = refs[n_out:]
    n_i, occ, width = own.shape
    kt = width // TILE
    tiles = staged.shape[0]
    me = me_ref[0]
    loads = [
        pltpu.make_async_copy(amp_ref.at[first : first + n_i], own, load_sem.at[0]),
        pltpu.make_async_copy(got_ref, got, load_sem.at[1]),
        pltpu.make_async_copy(plus_ref, held.at[0], load_sem.at[2]),
        pltpu.make_async_copy(minus_ref, held.at[1], load_sem.at[3]),
    ]
    for copy in loads:
        copy.start()

    def of_irrep(g, carry):
        begin, step = carry

        def tile_of(p, n):
            same = cd_ref[p] == g

            @pl.when(same)
            def _():
                lists[begin + n] = p

            return n + same.astype(jnp.int32)

        n = lax.fori_loop(0, kt, tile_of, 0)
        counts[g] = n
        counts[N_IRREP + g] = begin

        def target(q, carry):
            step, waiting = carry
            same = ab_ref[q] == g
            pair = same & (waiting >= 0)
            alone = same & (waiting < 0)

            @pl.when(alone)
            def _():
                lists[kt + 3 * step] = g
                lists[kt + 3 * step + 1] = q
                lists[kt + 3 * step + 2] = q

            @pl.when(pair)
            def _():
                lists[kt + 3 * step + 2] = q

            return (
                jnp.where(pair, step + 1, step),
                jnp.where(same, jnp.where(pair, -1, q), waiting),
            )

        step, waiting = lax.fori_loop(0, tiles, target, (step, -1))
        return begin + n, jnp.where(waiting >= 0, step + 1, step)

    _, steps = lax.fori_loop(0, N_IRREP, of_irrep, (0, 0))

    span = order_ref.shape[0]
    piece = span // n_i
    received = got.shape[0] * piece // occ
    order = picker(order_ref[...], received)
    loads[0].wait()
    loads[1].wait()
    for q in range(occ // piece):
        other = jnp.dot(
            order, got[q * received : (q + 1) * received, :], preferred_element_type=jnp.float32
        )
        mine = own[:, q * piece : (q + 1) * piece, :].reshape(span, width).astype(jnp.float32)
        summed = (mine + other).astype(jnp.bfloat16).reshape(n_i, piece, width)
        differed = (mine - other).astype(jnp.bfloat16).reshape(n_i, piece, width)
        own_rows = slice(q * piece, (q + 1) * piece)
        both[:, own_rows, :width] = summed
        both[:, own_rows, width:] = differed
    loads[2].wait()
    loads[3].wait()

    def out_copy(q):
        z, w = q // N_X, (q % N_X) ^ me
        return z, w, lambda dst: pltpu.make_async_copy(staged.at[q], dst, out_sem.at[q])

    def start(q):
        z, w, copy = out_copy(q)
        if joined:
            copy(out_refs[0].at[z, w]).start()
        else:

            @pl.when(w == 0)
            def _():
                copy(out_refs[0].at[z]).start()

            @pl.when(w == 1)
            def _():
                copy(out_refs[1].at[z]).start()

    rows = n_i * occ

    @pl.loop(0, steps)
    def _(step):
        g, a, b = (lists[kt + 3 * step + k] for k in range(3))
        n, begin = counts[g], counts[N_IRREP + g]

        @pl.loop(0, n)
        def _(k):
            p = lists[begin + k]
            for half in range(2):
                for w, q in enumerate((a, b)):
                    packed[half, pl.ds(pl.multiple_of(k * TILE, TILE), TILE), w * TILE : (w + 1) * TILE] = held[
                        half,
                        pl.ds(pl.multiple_of(p * TILE, TILE), TILE),
                        pl.ds(pl.multiple_of(q * TILE, TILE), TILE),
                    ]

        @pl.when(n == 0)
        def _():
            zero = jnp.zeros(staged.shape[1:], staged.dtype)
            staged[a] = zero
            staged[b] = zero

        for size in range(1, kt + 1):

            @pl.when(n == size)
            def _():
                weights = [packed[half, : size * TILE, :] for half in range(2)]
                for r in range(0, rows, row_block):
                    terms = []
                    for half in range(2):
                        left = jnp.concatenate(
                            [
                                both.reshape(rows, 2 * width)[
                                    r : r + row_block,
                                    pl.ds(
                                        pl.multiple_of(half * width + lists[begin + k] * TILE, TILE),
                                        TILE,
                                    ),
                                ]
                                for k in range(size)
                            ],
                            1,
                        )
                        terms.append(left)
                    term = 0.5 * jnp.dot(
                        jnp.concatenate(terms, 1),
                        jnp.concatenate(weights, 0),
                        preferred_element_type=jnp.float32,
                    )
                    staged[a, r : r + row_block] = term[:, :TILE].astype(staged.dtype)
                    staged[b, r : r + row_block] = term[:, TILE:].astype(staged.dtype)

        start(a)

        @pl.when(b != a)
        def _():
            start(b)

    @pl.loop(0, tiles)
    def _(q):
        z, w, copy = out_copy(q)
        copy(out_refs[0].at[z, w] if joined else out_refs[0].at[z]).wait()


def ladder(me, cd_irrep, ab_irrep, order, amplitudes, received, plus, minus, first, n_i, slots, cost=4e6):
    _, occ, width = amplitudes.shape
    rows = n_i * occ
    tiles = plus.shape[1] // TILE
    n_z = tiles // N_X
    if slots:
        shapes = [(n_z, slots, rows, TILE)]
    else:
        shapes = [(n_z, rows, TILE)] * N_X
    smem = pl.BlockSpec(memory_space=pltpu.SMEM)
    hbm = pl.BlockSpec(memory_space=pl.ANY)
    dma = pltpu.SemaphoreType.DMA
    bf16 = jnp.bfloat16
    return pl.pallas_call(
        functools.partial(ladder_kernel, bool(slots), rows // 2, first),
        in_specs=[smem] * 3 + [pl.BlockSpec(memory_space=pltpu.VMEM)] + [hbm] * 4,
        out_specs=[hbm] * len(shapes),
        out_shape=[jax.ShapeDtypeStruct(s, bf16) for s in shapes],
        scratch_shapes=[
            pltpu.VMEM((n_i, occ, width), bf16),
            pltpu.VMEM(received.shape, bf16),
            pltpu.VMEM((2,) + plus.shape, bf16),
            pltpu.VMEM((n_i, occ, 2 * width), bf16),
            pltpu.VMEM((2, width, PAIR), bf16),
            pltpu.VMEM((tiles, rows, TILE), bf16),
            pltpu.SMEM((width // TILE + 3 * tiles,), jnp.int32),
            pltpu.SMEM((2 * N_IRREP,), jnp.int32),
            dma((4,)),
            dma((tiles,)),
        ],
        compiler_params=params(),
        cost_estimate=pl.CostEstimate(
            flops=0, bytes_accessed=int(cost), transcendentals=0
        ),
    )(me, cd_irrep, ab_irrep, order, amplitudes, received, plus, minus)

def finish_kernel(*refs):
    parts, out_ref = refs[:-1], refs[-1]
    terms = [[parts[0], parts[1]], [parts[4]], [parts[2], parts[3]]]
    at = 0
    for names in terms:
        total = 0.0
        for ref in names:
            part = ref[...].astype(jnp.float32)
            total = total + part.reshape(part.shape[-2:])
        rows = total.shape[0]
        out_ref[:, at : at + rows] = total.T.astype(out_ref.dtype)
        at += rows


def finish(sum0, far0, sum1, far1):
    n0, n1 = far0.shape[0], far1.shape[0]

    def slot(ref, k):
        return pl.BlockSpec((1, 1) + ref.shape[2:], lambda g: (0, k, 0, 0))

    return pl.pallas_call(
        finish_kernel,
        grid=(1,),
        in_specs=[
            slot(sum0, 0),
            pl.BlockSpec(far0.shape, lambda g: (0, 0)),
            slot(sum1, 0),
            pl.BlockSpec(far1.shape, lambda g: (0, 0)),
            slot(sum1, 2),
        ],
        out_specs=pl.BlockSpec((TILE, n0 + 2 * n1), lambda g: (0, 0)),
        out_shape=jax.ShapeDtypeStruct((TILE, n0 + 2 * n1), jnp.bfloat16),
        compiler_params=params(),
    )(sum0, far0, sum1, far1, sum1)


def on_device(amplitudes, plus, minus, cd_irrep, ab_irrep):
    rows = amplitudes.shape[0]
    me = lax.axis_index("xl").reshape(1).astype(jnp.int32)
    swap = functools.partial(lax.ppermute, axis_name="xl", perm=[(0, 1), (1, 0)])
    chunk = rows // CUTS
    part = chunk // 2

    def exchange(packed):
        return lax.all_to_all(packed, "row", split_axis=0, concat_axis=0, tiled=True)

    def scatter(terms):
        return lax.psum_scatter(terms, "z", scatter_dimension=0, tiled=True)

    def product(received, cut, first, n_i, slots, cost=4e6):
        return ladder(
            me,
            cd_irrep,
            ab_irrep,
            receive_order(rows, chunk, first, n_i),
            amplitudes,
            received,
            plus,
            minus,
            cut * chunk + first,
            n_i,
            slots,
            cost,
        )

    packed0 = pack(send_order(rows, 0, chunk), amplitudes)
    received0 = exchange(packed0)
    packed0, later = lax.optimization_barrier((packed0, amplitudes))
    packed1 = pack(send_order(rows, chunk, chunk), later)
    received0, packed1 = lax.optimization_barrier((received0, packed1))
    received1 = exchange(packed1)
    (terms0,) = product(received0, 0, 0, chunk, 2, COST0)
    sum0 = scatter(terms0)
    received1, _ = lax.optimization_barrier((received1, terms0))
    near1, far1 = product(received1, 1, 0, part, 0)
    far1 = swap(far1)
    received1, _ = lax.optimization_barrier((received1, near1))
    (terms1,) = product(received1, 1, part, part, 3)
    added = (near1.astype(jnp.float32) + far1.astype(jnp.float32)).astype(jnp.bfloat16)
    sum1 = scatter(lax.dynamic_update_slice(terms1, added[:, None], (0, 2, 0, 0)))
    return finish(sum0, swap(sum0[0, 1]), sum1, swap(sum1[0, 1]))


COST0 = 4e6


def solution(mesh):
    rows, cols = mesh.shape["row"], mesh.shape["col"]
    fine = Mesh(mesh.devices.reshape(rows, cols // N_X, N_X), ("row", "z", "xl"))
    col = ("z", "xl")
    return jax.shard_map(
        on_device,
        mesh=fine,
        in_specs=(P("row", None, col), P(col, None), P(col, None), P(col), P()),
        out_specs=P(col, "row"),
        check_vma=False,
    )
```

```python
import functools

import jax
import jax.numpy as jnp
import numpy as np
from jax import lax
from jax.experimental import pallas as pl
from jax.experimental.pallas import tpu as pltpu
from jax.sharding import Mesh
from jax.sharding import PartitionSpec as P

TILE = 128
N_X = 2
PAIR = N_X * TILE
N_S = 4
N_IRREP = 4
BUNDLE = 4
CUTS = 2
EARLY = 2


def params(mib=60):
    return pltpu.CompilerParams(vmem_limit_bytes=mib * 2**20)


def send_order(rows, first, n_i):
    return column(
        (i * N_S + s) * rows + first + jl
        for s in range(N_S)
        for jl in range(n_i)
        for i in range(rows)
    )


def receive_order(rows, chunk, first, n_i):
    return column(
        (s * chunk + first + i) * rows + jl
        for i in range(n_i)
        for s in range(N_S)
        for jl in range(rows)
    )


def column(places):
    return jnp.asarray(np.array(list(places), np.int32)[:, None])


def pack_kernel(order_ref, amp_ref, out_ref, held, sent, in_sem, out_sem):
    rows, occ, width = amp_ref.shape
    per = order_ref.shape[0]
    steps = held.shape[0]
    wide = occ // steps
    loads = [
        pltpu.make_async_copy(amp_ref.at[:, q * wide : (q + 1) * wide, :], held.at[q], in_sem.at[q])
        for q in range(steps)
    ]
    stores = [
        pltpu.make_async_copy(sent.at[q], out_ref.at[q * per : (q + 1) * per, :], out_sem.at[q])
        for q in range(steps)
    ]
    for copy in loads:
        copy.start()
    order = picker(order_ref[...], rows * wide)
    for q in range(steps):
        loads[q].wait()
        block = held[q].reshape(rows * wide, width)
        sent[q] = jnp.dot(order, block, preferred_element_type=jnp.float32).astype(sent.dtype)
        stores[q].start()
    for copy in stores:
        copy.wait()


def pack(order, amplitudes):
    rows, occ, width = amplitudes.shape
    wide = N_S * rows
    steps = occ // wide
    per = order.shape[0]
    hbm = pl.BlockSpec(memory_space=pl.ANY)
    return pl.pallas_call(
        pack_kernel,
        in_specs=[pl.BlockSpec(memory_space=pltpu.VMEM), hbm],
        out_specs=hbm,
        out_shape=jax.ShapeDtypeStruct((steps * per, width), jnp.bfloat16),
        scratch_shapes=[
            pltpu.VMEM((steps, rows, wide, width), jnp.bfloat16),
            pltpu.VMEM((steps, per, width), jnp.bfloat16),
            pltpu.SemaphoreType.DMA((steps,)),
            pltpu.SemaphoreType.DMA((steps,)),
        ],
        compiler_params=params(),
        cost_estimate=pl.CostEstimate(
            flops=0, bytes_accessed=4 * rows * occ * width, transcendentals=0
        ),
    )(order, amplitudes)


def picker(places, width):
    lanes = lax.broadcasted_iota(jnp.int32, (places.shape[0], width), 1)
    return jnp.where(lanes == places, 1.0, 0.0).astype(jnp.bfloat16)

def match_kernel(cd_ref, ab_ref, plus_ref, minus_ref, lists, out_ref, held, packed, in_sem, out_sem):
    kt = cd_ref.shape[0]
    tiles = ab_ref.shape[0]
    loads = [
        pltpu.make_async_copy(plus_ref, held.at[0], in_sem.at[0]),
        pltpu.make_async_copy(minus_ref, held.at[1], in_sem.at[1]),
    ]
    for copy in loads:
        copy.start()
    there = 2 * N_IRREP
    first_step = there + 2 * kt + 2

    def of_irrep(g, carry):
        begin, step, block = carry

        def tile_of(p, n):
            same = cd_ref[p] == g

            @pl.when(same)
            def _():
                lists[there + p] = begin + n
                lists[there + kt + begin + n] = p

            return n + same.astype(jnp.int32)

        n = lax.fori_loop(0, kt, tile_of, 0)
        lists[g] = n
        lists[N_IRREP + g] = begin

        def target(q, carry):
            step, waiting, block = carry
            same = ab_ref[q] == g
            alone = same & (waiting < 0)
            second = same & (waiting >= 0)

            @pl.when(alone)
            def _():
                for k, value in enumerate((g, q, q, block)):
                    lists[first_step + 4 * step + k] = value

            @pl.when(second)
            def _():
                lists[first_step + 4 * step + 2] = q

            return (
                jnp.where(second, step + 1, step),
                jnp.where(same, jnp.where(second, -1, q), waiting),
                jnp.where(alone, block + n, block),
            )

        step, waiting, block = lax.fori_loop(0, tiles, target, (step, -1, block))
        return begin + n, jnp.where(waiting >= 0, step + 1, step), block

    _, steps, blocks = lax.fori_loop(0, N_IRREP, of_irrep, (0, 0, 0))
    bundles = (blocks + BUNDLE - 1) // BUNDLE
    lists[first_step - 2] = bundles
    lists[first_step - 1] = steps
    for copy in loads:
        copy.wait()

    @pl.loop(0, steps)
    def _(step):
        g, a, b, block = (lists[first_step + 4 * step + k] for k in range(4))
        begin = lists[N_IRREP + g]

        @pl.loop(0, lists[g])
        def _(k):
            p = pl.ds(pl.multiple_of(lists[there + kt + begin + k] * TILE, TILE), TILE)
            for half in range(2):
                for w, q in enumerate((a, b)):
                    packed[block + k, half * TILE : (half + 1) * TILE, w * TILE : (w + 1) * TILE] = (
                        held[half, p, pl.ds(pl.multiple_of(q * TILE, TILE), TILE)]
                    )

    def store(k):
        where = pl.ds(k * BUNDLE, BUNDLE)
        return pltpu.make_async_copy(packed.at[where], out_ref.at[where], out_sem.at[k])

    @pl.loop(0, bundles)
    def _(k):
        store(k).start()

    @pl.loop(0, bundles)
    def _(k):
        store(k).wait()


def match(cd_irrep, ab_irrep, plus, minus):
    width, slab = plus.shape
    kt, tiles = width // TILE, slab // TILE
    steps = (tiles + N_IRREP) // 2
    smem = pl.BlockSpec(memory_space=pltpu.SMEM)
    hbm = pl.BlockSpec(memory_space=pl.ANY)
    blocks = (tiles + 1) // N_X * kt
    shape = (blocks, PAIR, PAIR)
    return pl.pallas_call(
        match_kernel,
        in_specs=[smem, smem, hbm, hbm],
        out_specs=[smem, hbm],
        out_shape=[
            jax.ShapeDtypeStruct((2 * N_IRREP + 2 * kt + 2 + 4 * steps,), jnp.int32),
            jax.ShapeDtypeStruct(shape, jnp.bfloat16),
        ],
        scratch_shapes=[
            pltpu.VMEM((2, width, slab), jnp.bfloat16),
            pltpu.VMEM(shape, jnp.bfloat16),
            pltpu.SemaphoreType.DMA((2,)),
            pltpu.SemaphoreType.DMA((blocks // BUNDLE,)),
        ],
        compiler_params=params(),
        cost_estimate=pl.CostEstimate(
            flops=0, bytes_accessed=8 * width * slab, transcendentals=0
        ),
    )(cd_irrep, ab_irrep, plus, minus)


def ladder_kernel(
    first, me_ref, lists, order_ref, amp_ref, got_ref, weight_ref, *refs
):
    n_out = len(refs) - 8
    out_refs = refs[:n_out]
    own, got, weights, both, staged, load_sem, weight_sem, out_sem = refs[n_out:]
    n_i, occ, width = own.shape
    kt = width // TILE
    tiles, per = staged.shape[:2]
    rows = n_i * occ
    me = me_ref[0]
    there = 2 * N_IRREP
    first_step = there + 2 * kt + 2
    bundles, steps = lists[first_step - 2], lists[first_step - 1]
    loads = [
        pltpu.make_async_copy(amp_ref.at[first : first + n_i], own, load_sem.at[0]),
        pltpu.make_async_copy(got_ref, got, load_sem.at[1]),
    ]
    for copy in loads:
        copy.start()

    def weights_copy(k):
        where = pl.ds(k * BUNDLE, BUNDLE)
        return pltpu.make_async_copy(weight_ref.at[where], weights.at[where], weight_sem.at[k])

    @pl.loop(0, bundles)
    def _(k):
        weights_copy(k).start()

    span = order_ref.shape[0]
    piece = span // n_i
    received = got.shape[0] * piece // occ
    order = picker(order_ref[...], received)
    for copy in loads:
        copy.wait()
    for q in range(occ // piece):
        other = jnp.dot(
            order, got[q * received : (q + 1) * received, :], preferred_element_type=jnp.float32
        )
        mine = own[:, q * piece : (q + 1) * piece, :].reshape(span, width).astype(jnp.float32)
        for half, value in enumerate((mine + other, mine - other)):
            value = value.astype(jnp.bfloat16).reshape(n_i, piece, width)
            for p in range(kt):
                lanes = pl.ds(pl.multiple_of(lists[there + p] * PAIR + half * TILE, TILE), TILE)
                both[:, q * piece : (q + 1) * piece, lanes] = value[:, :, p * TILE : (p + 1) * TILE]

    def out_copy(q, dst):
        return pltpu.make_async_copy(staged.at[q], dst, out_sem)

    def start(q):
        z, w = q // N_X, (q % N_X) ^ me
        if n_out == 1:
            out_copy(q, out_refs[0].at[z, pl.ds(w * per, per)]).start()
        else:
            for k in range(N_X):

                @pl.when(w == k)
                def _():
                    out_copy(q, out_refs[k].at[z]).start()

    @pl.loop(0, bundles)
    def _(k):
        weights_copy(k).wait()

    @pl.loop(0, steps)
    def _(step):
        g, a, b, block = (lists[first_step + 4 * step + k] for k in range(4))
        n, begin = lists[g], lists[N_IRREP + g]

        @pl.when(n == 0)
        def _():
            zero = jnp.zeros(staged.shape[1:], staged.dtype)
            staged[a] = zero
            staged[b] = zero

        for size in range(1, kt + 1):

            @pl.when(n == size)
            def _():
                lanes = pl.ds(pl.multiple_of(begin * PAIR, PAIR), size * PAIR)
                left = both[:, :, lanes].reshape(rows, size * PAIR)
                right = weights[pl.ds(block, size)].reshape(size * PAIR, PAIR)
                term = 0.5 * jnp.dot(left, right, preferred_element_type=jnp.float32)
                staged[a] = term[:, :TILE].astype(staged.dtype).reshape(staged.shape[1:])
                staged[b] = term[:, TILE:].astype(staged.dtype).reshape(staged.shape[1:])

        start(a)

        @pl.when(b != a)
        def _():
            start(b)

    pltpu.make_async_copy(staged, staged, out_sem).wait()


def ladder(me, lists, order, amplitudes, received, weights, first, n_i, n_z, per, slots):
    _, occ, width = amplitudes.shape
    rows = n_i * occ
    tiles = n_z * N_X
    blocks = weights.shape[0]
    if slots:
        shapes = [(n_z, slots, rows // per, TILE)]
    else:
        shapes = [(n_z, per, rows // per, TILE)] * N_X
    smem = pl.BlockSpec(memory_space=pltpu.SMEM)
    hbm = pl.BlockSpec(memory_space=pl.ANY)
    dma = pltpu.SemaphoreType.DMA
    bf16 = jnp.bfloat16
    return pl.pallas_call(
        functools.partial(ladder_kernel, first),
        in_specs=[smem, smem, pl.BlockSpec(memory_space=pltpu.VMEM), hbm, hbm, hbm],
        out_specs=[hbm] * len(shapes),
        out_shape=[jax.ShapeDtypeStruct(s, bf16) for s in shapes],
        scratch_shapes=[
            pltpu.VMEM((n_i, occ, width), bf16),
            pltpu.VMEM(received.shape, bf16),
            pltpu.VMEM(weights.shape, bf16),
            pltpu.VMEM((n_i, occ, 2 * width), bf16),
            pltpu.VMEM((tiles, per, rows // per, TILE), bf16),
            dma((2,)),
            dma((blocks // BUNDLE,)),
            dma,
        ],
        compiler_params=params(50),
        cost_estimate=pl.CostEstimate(
            flops=0, bytes_accessed=8 * rows * (width + n_z * TILE), transcendentals=0
        ),
    )(me, lists, order, amplitudes, received, weights)


def finish_kernel(near, far, *refs):
    out_ref = refs[-1]
    total = near[...].astype(jnp.float32).reshape(-1, TILE) + far[...].astype(jnp.float32)
    if len(refs) > 1:
        early = refs[0][...].astype(jnp.float32).reshape(-1, TILE)
        total = jnp.concatenate([early, total], 0)
    out_ref[...] = total.T.astype(out_ref.dtype)


def slots(ref, count, k):
    return pl.BlockSpec((1, count) + ref.shape[2:], lambda g: (0, k, 0, 0))


def finish_first(near, far):
    rows = far.shape[0]
    return pl.pallas_call(
        finish_kernel,
        grid=(1,),
        in_specs=[slots(near, 1, 0), pl.BlockSpec(far.shape, lambda g: (0, 0))],
        out_specs=pl.BlockSpec((TILE, rows), lambda g: (0, 0)),
        out_shape=jax.ShapeDtypeStruct((TILE, CUTS * rows), jnp.bfloat16),
        compiler_params=params(57),
    )(near, far)


def finish_last(done, sum1, far):
    unit = sum1.shape[2]
    per = far.shape[0] // unit
    return pl.pallas_call(
        lambda done_ref, *refs: finish_kernel(*refs),
        grid=(1,),
        in_specs=[
            pl.BlockSpec(memory_space=pl.ANY),
            slots(sum1, per, 0),
            pl.BlockSpec(far.shape, lambda g: (0, 0)),
            slots(sum1, 1, N_X * per),
        ],
        out_specs=pl.BlockSpec((TILE, done.shape[1] // CUTS), lambda g: (0, 1)),
        out_shape=jax.ShapeDtypeStruct(done.shape, jnp.bfloat16),
        input_output_aliases={0: 0},
        compiler_params=params(57),
    )(done, sum1, far, sum1)


def on_device(amplitudes, plus, minus, cd_irrep, ab_irrep):
    rows = amplitudes.shape[0]
    me = lax.axis_index("xl").reshape(1).astype(jnp.int32)
    swap = functools.partial(lax.ppermute, axis_name="xl", perm=[(0, 1), (1, 0)])
    chunk = rows // CUTS

    def exchange(packed):
        return lax.all_to_all(packed, "row", split_axis=0, concat_axis=0, tiled=True)

    def scatter(terms):
        return lax.psum_scatter(terms, "z", scatter_dimension=0, tiled=True)

    def product(received, cut, first, n_i, per, slots):
        return ladder(
            me,
            lists,
            receive_order(rows, chunk, first, n_i),
            amplitudes,
            received,
            weights,
            cut * chunk + first,
            n_i,
            plus.shape[1] // PAIR,
            per,
            slots,
        )

    packed0 = pack(send_order(rows, 0, chunk), amplitudes)
    received0 = exchange(packed0)
    packed0, later = lax.optimization_barrier((packed0, amplitudes))
    packed1 = pack(send_order(rows, chunk, chunk), later)
    packed0, first_plus = lax.optimization_barrier((packed0, plus))
    lists, weights = match(cd_irrep, ab_irrep, first_plus, minus)
    received0, packed1, weights = lax.optimization_barrier((received0, packed1, weights))
    received1 = exchange(packed1)
    (terms0,) = product(received0, 0, 0, chunk, 1, N_X)
    sum0 = scatter(terms0)
    received1, _ = lax.optimization_barrier((received1, terms0))
    near1, far1 = product(received1, 1, 0, EARLY, 1, 0)
    far1 = swap(far1)
    received1, _ = lax.optimization_barrier((received1, near1))
    per = chunk // EARLY - 1
    (terms1,) = product(received1, 1, EARLY, chunk - EARLY, per, N_X * per + 1)
    added = (near1.astype(jnp.float32) + far1.astype(jnp.float32)).astype(jnp.bfloat16)
    sum1 = scatter(lax.dynamic_update_slice(terms1, added, (0, N_X * per, 0, 0)))
    done = finish_first(sum0, swap(sum0[0, 1]))
    last1 = swap(sum1[0, per : 2 * per].reshape(-1, TILE))
    return finish_last(done, sum1, last1)


def solution(mesh):
    rows, cols = mesh.shape["row"], mesh.shape["col"]
    fine = Mesh(mesh.devices.reshape(rows, cols // N_X, N_X), ("row", "z", "xl"))
    col = ("z", "xl")
    return jax.shard_map(
        on_device,
        mesh=fine,
        in_specs=(P("row", None, col), P(col, None), P(col, None), P(col), P()),
        out_specs=P(col, "row"),
        check_vma=False,
    )
```

```python
import functools

import jax
import jax.numpy as jnp
import numpy as np
from jax import lax
from jax.experimental import pallas as pl
from jax.experimental.pallas import tpu as pltpu
from jax.sharding import Mesh
from jax.sharding import PartitionSpec as P

TILE = 128
N_X = 2
PAIR = N_X * TILE
N_S = 4
N_IRREP = 4
BUNDLE = 4
FIRST = 8
UNIT = 2


def params(mib=60):
    return pltpu.CompilerParams(vmem_limit_bytes=mib * 2**20)


def send_order(rows, first, n_i):
    return column(
        (i * N_S + s) * rows + first + jl
        for s in range(N_S)
        for jl in range(n_i)
        for i in range(rows)
    )


def receive_order(rows, chunk, first, n_i):
    return column(
        (s * chunk + first + i) * rows + jl
        for i in range(n_i)
        for s in range(N_S)
        for jl in range(rows)
    )


def column(places):
    return jnp.asarray(np.array(list(places), np.int32)[:, None])


def pack_kernel(order_ref, amp_ref, out_ref, held, sent, in_sem, out_sem):
    rows, occ, width = amp_ref.shape
    per = order_ref.shape[0]
    steps = held.shape[0]
    wide = occ // steps
    loads = [
        pltpu.make_async_copy(amp_ref.at[:, q * wide : (q + 1) * wide, :], held.at[q], in_sem.at[q])
        for q in range(steps)
    ]
    stores = [
        pltpu.make_async_copy(sent.at[q], out_ref.at[q * per : (q + 1) * per, :], out_sem.at[q])
        for q in range(steps)
    ]
    for copy in loads:
        copy.start()
    order = picker(order_ref[...], rows * wide)
    for q in range(steps):
        loads[q].wait()
        block = held[q].reshape(rows * wide, width)
        sent[q] = jnp.dot(order, block, preferred_element_type=jnp.float32).astype(sent.dtype)
        stores[q].start()
    for copy in stores:
        copy.wait()


def pack(order, amplitudes):
    rows, occ, width = amplitudes.shape
    wide = N_S * rows
    steps = occ // wide
    per = order.shape[0]
    hbm = pl.BlockSpec(memory_space=pl.ANY)
    return pl.pallas_call(
        pack_kernel,
        in_specs=[pl.BlockSpec(memory_space=pltpu.VMEM), hbm],
        out_specs=hbm,
        out_shape=jax.ShapeDtypeStruct((steps * per, width), jnp.bfloat16),
        scratch_shapes=[
            pltpu.VMEM((steps, rows, wide, width), jnp.bfloat16),
            pltpu.VMEM((steps, per, width), jnp.bfloat16),
            pltpu.SemaphoreType.DMA((steps,)),
            pltpu.SemaphoreType.DMA((steps,)),
        ],
        compiler_params=params(),
        cost_estimate=pl.CostEstimate(
            flops=0, bytes_accessed=4 * rows * occ * width, transcendentals=0
        ),
    )(order, amplitudes)


def picker(places, width):
    lanes = lax.broadcasted_iota(jnp.int32, (places.shape[0], width), 1)
    return jnp.where(lanes == places, 1.0, 0.0).astype(jnp.bfloat16)

def match_kernel(cd_ref, ab_ref, plus_ref, minus_ref, lists, out_ref, held, packed, in_sem, out_sem):
    kt = cd_ref.shape[0]
    tiles = ab_ref.shape[0]
    loads = [
        pltpu.make_async_copy(plus_ref, held.at[0], in_sem.at[0]),
        pltpu.make_async_copy(minus_ref, held.at[1], in_sem.at[1]),
    ]
    for copy in loads:
        copy.start()
    there = 2 * N_IRREP
    first_step = there + 2 * kt + 2

    def of_irrep(g, carry):
        begin, step, block = carry

        def tile_of(p, n):
            same = cd_ref[p] == g

            @pl.when(same)
            def _():
                lists[there + p] = begin + n
                lists[there + kt + begin + n] = p

            return n + same.astype(jnp.int32)

        n = lax.fori_loop(0, kt, tile_of, 0)
        lists[g] = n
        lists[N_IRREP + g] = begin

        def target(q, carry):
            step, waiting, block = carry
            same = ab_ref[q] == g
            alone = same & (waiting < 0)
            second = same & (waiting >= 0)

            @pl.when(alone)
            def _():
                for k, value in enumerate((g, q, q, block)):
                    lists[first_step + 4 * step + k] = value

            @pl.when(second)
            def _():
                lists[first_step + 4 * step + 2] = q

            return (
                jnp.where(second, step + 1, step),
                jnp.where(same, jnp.where(second, -1, q), waiting),
                jnp.where(alone, block + n, block),
            )

        step, waiting, block = lax.fori_loop(0, tiles, target, (step, -1, block))
        return begin + n, jnp.where(waiting >= 0, step + 1, step), block

    _, steps, blocks = lax.fori_loop(0, N_IRREP, of_irrep, (0, 0, 0))
    bundles = (blocks + BUNDLE - 1) // BUNDLE
    lists[first_step - 2] = bundles
    lists[first_step - 1] = steps
    for copy in loads:
        copy.wait()

    @pl.loop(0, steps)
    def _(step):
        g, a, b, block = (lists[first_step + 4 * step + k] for k in range(4))
        begin = lists[N_IRREP + g]

        @pl.loop(0, lists[g])
        def _(k):
            p = pl.ds(pl.multiple_of(lists[there + kt + begin + k] * TILE, TILE), TILE)
            for half in range(2):
                for w, q in enumerate((a, b)):
                    packed[block + k, half * TILE : (half + 1) * TILE, w * TILE : (w + 1) * TILE] = (
                        held[half, p, pl.ds(pl.multiple_of(q * TILE, TILE), TILE)]
                    )

    def store(k):
        where = pl.ds(k * BUNDLE, BUNDLE)
        return pltpu.make_async_copy(packed.at[where], out_ref.at[where], out_sem.at[k])

    @pl.loop(0, bundles)
    def _(k):
        store(k).start()

    @pl.loop(0, bundles)
    def _(k):
        store(k).wait()


def match(cd_irrep, ab_irrep, plus, minus):
    width, slab = plus.shape
    kt, tiles = width // TILE, slab // TILE
    steps = (tiles + N_IRREP) // 2
    smem = pl.BlockSpec(memory_space=pltpu.SMEM)
    hbm = pl.BlockSpec(memory_space=pl.ANY)
    blocks = (tiles + 1) // N_X * kt
    shape = (blocks, PAIR, PAIR)
    return pl.pallas_call(
        match_kernel,
        in_specs=[smem, smem, hbm, hbm],
        out_specs=[smem, hbm],
        out_shape=[
            jax.ShapeDtypeStruct((2 * N_IRREP + 2 * kt + 2 + 4 * steps,), jnp.int32),
            jax.ShapeDtypeStruct(shape, jnp.bfloat16),
        ],
        scratch_shapes=[
            pltpu.VMEM((2, width, slab), jnp.bfloat16),
            pltpu.VMEM(shape, jnp.bfloat16),
            pltpu.SemaphoreType.DMA((2,)),
            pltpu.SemaphoreType.DMA((blocks // BUNDLE,)),
        ],
        compiler_params=params(),
        cost_estimate=pl.CostEstimate(
            flops=0, bytes_accessed=8 * width * slab, transcendentals=0
        ),
    )(cd_irrep, ab_irrep, plus, minus)


def ladder_kernel(
    first, me_ref, lists, order_ref, amp_ref, got_ref, weight_ref, *refs
):
    n_out = len(refs) - 8
    out_refs = refs[:n_out]
    own, got, weights, both, staged, load_sem, weight_sem, out_sem = refs[n_out:]
    n_i, occ, width = own.shape
    kt = width // TILE
    tiles, per = staged.shape[:2]
    rows = n_i * occ
    me = me_ref[0]
    there = 2 * N_IRREP
    first_step = there + 2 * kt + 2
    bundles, steps = lists[first_step - 2], lists[first_step - 1]
    loads = [
        pltpu.make_async_copy(amp_ref.at[first : first + n_i], own, load_sem.at[0]),
        pltpu.make_async_copy(got_ref, got, load_sem.at[1]),
    ]
    for copy in loads:
        copy.start()

    def weights_copy(k):
        where = pl.ds(k * BUNDLE, BUNDLE)
        return pltpu.make_async_copy(weight_ref.at[where], weights.at[where], weight_sem.at[k])

    @pl.loop(0, bundles)
    def _(k):
        weights_copy(k).start()

    span = order_ref.shape[0]
    piece = span // n_i
    received = got.shape[0] * piece // occ
    order = picker(order_ref[...], received)
    for copy in loads:
        copy.wait()
    for q in range(occ // piece):
        other = jnp.dot(
            order, got[q * received : (q + 1) * received, :], preferred_element_type=jnp.float32
        )
        mine = own[:, q * piece : (q + 1) * piece, :].reshape(span, width).astype(jnp.float32)
        for half, value in enumerate((mine + other, mine - other)):
            value = value.astype(jnp.bfloat16).reshape(n_i, piece, width)
            for p in range(kt):
                lanes = pl.ds(pl.multiple_of(lists[there + p] * PAIR + half * TILE, TILE), TILE)
                both[:, q * piece : (q + 1) * piece, lanes] = value[:, :, p * TILE : (p + 1) * TILE]

    def out_copy(q, dst):
        return pltpu.make_async_copy(staged.at[q], dst, out_sem)

    def start(q):
        z, w = q // N_X, (q % N_X) ^ me
        if n_out == 1:
            out_copy(q, out_refs[0].at[z, pl.ds(w * per, per)]).start()
        else:
            for k in range(N_X):

                @pl.when(w == k)
                def _():
                    out_copy(q, out_refs[k].at[z]).start()

    @pl.loop(0, bundles)
    def _(k):
        weights_copy(k).wait()

    @pl.loop(0, steps)
    def _(step):
        g, a, b, block = (lists[first_step + 4 * step + k] for k in range(4))
        n, begin = lists[g], lists[N_IRREP + g]

        @pl.when(n == 0)
        def _():
            zero = jnp.zeros(staged.shape[1:], staged.dtype)
            staged[a] = zero
            staged[b] = zero

        for size in range(1, kt + 1):

            @pl.when(n == size)
            def _():
                lanes = pl.ds(pl.multiple_of(begin * PAIR, PAIR), size * PAIR)
                left = both[:, :, lanes].reshape(rows, size * PAIR)
                right = weights[pl.ds(block, size)].reshape(size * PAIR, PAIR)
                term = 0.5 * jnp.dot(left, right, preferred_element_type=jnp.float32)
                staged[a] = term[:, :TILE].astype(staged.dtype).reshape(staged.shape[1:])
                staged[b] = term[:, TILE:].astype(staged.dtype).reshape(staged.shape[1:])

        start(a)

        @pl.when(b != a)
        def _():
            start(b)

    pltpu.make_async_copy(staged, staged, out_sem).wait()


def ladder(me, lists, order, amplitudes, received, weights, first, n_i, n_z, per, slots):
    _, occ, width = amplitudes.shape
    rows = n_i * occ
    tiles = n_z * N_X
    blocks = weights.shape[0]
    if slots:
        shapes = [(n_z, slots, rows // per, TILE)]
    else:
        shapes = [(n_z, per, rows // per, TILE)] * N_X
    smem = pl.BlockSpec(memory_space=pltpu.SMEM)
    hbm = pl.BlockSpec(memory_space=pl.ANY)
    dma = pltpu.SemaphoreType.DMA
    bf16 = jnp.bfloat16
    return pl.pallas_call(
        functools.partial(ladder_kernel, first),
        in_specs=[smem, smem, pl.BlockSpec(memory_space=pltpu.VMEM), hbm, hbm, hbm],
        out_specs=[hbm] * len(shapes),
        out_shape=[jax.ShapeDtypeStruct(s, bf16) for s in shapes],
        scratch_shapes=[
            pltpu.VMEM((n_i, occ, width), bf16),
            pltpu.VMEM(received.shape, bf16),
            pltpu.VMEM(weights.shape, bf16),
            pltpu.VMEM((n_i, occ, 2 * width), bf16),
            pltpu.VMEM((tiles, per, rows // per, TILE), bf16),
            dma((2,)),
            dma((blocks // BUNDLE,)),
            dma,
        ],
        compiler_params=params(50),
        cost_estimate=pl.CostEstimate(
            flops=0, bytes_accessed=8 * rows * (width + n_z * TILE), transcendentals=0
        ),
    )(me, lists, order, amplitudes, received, weights)


def finish_kernel(near, far, *refs):
    out_ref = refs[-1]
    total = near[...].astype(jnp.float32).reshape(-1, TILE) + far[...].astype(jnp.float32)
    if len(refs) > 1:
        early = refs[0][...].astype(jnp.float32).reshape(-1, TILE)
        total = jnp.concatenate([early, total], 0)
    out_ref[...] = total.T.astype(out_ref.dtype)


def slots(ref, count, k):
    return pl.BlockSpec((1, count) + ref.shape[2:], lambda g: (0, k, 0, 0))


def finish_first(near, far):
    rows = far.shape[0]
    return pl.pallas_call(
        finish_kernel,
        grid=(1,),
        in_specs=[slots(near, 1, 0), pl.BlockSpec(far.shape, lambda g: (0, 0))],
        out_specs=pl.BlockSpec((TILE, rows), lambda g: (0, 0)),
        out_shape=jax.ShapeDtypeStruct((TILE, 2 * rows), jnp.bfloat16),
        compiler_params=params(57),
    )(near, far)


def finish_last(done, sum1, far):
    early = sum1.shape[1] - N_X
    return pl.pallas_call(
        lambda done_ref, *refs: finish_kernel(*refs),
        grid=(1,),
        in_specs=[
            pl.BlockSpec(memory_space=pl.ANY),
            slots(sum1, 1, 0),
            pl.BlockSpec(far.shape, lambda g: (0, 0)),
            slots(sum1, early, N_X // early),
        ],
        out_specs=pl.BlockSpec((TILE, done.shape[1] // 2), lambda g: (0, 1)),
        out_shape=jax.ShapeDtypeStruct(done.shape, jnp.bfloat16),
        input_output_aliases={0: 0},
        compiler_params=params(57),
    )(done, sum1, far, sum1)


def on_device(amplitudes, plus, minus, cd_irrep, ab_irrep):
    rows = amplitudes.shape[0]
    me = lax.axis_index("xl").reshape(1).astype(jnp.int32)
    swap = functools.partial(lax.ppermute, axis_name="xl", perm=[(0, 1), (1, 0)])

    def exchange(packed):
        return lax.all_to_all(packed, "row", split_axis=0, concat_axis=0, tiled=True)

    def scatter(terms):
        return lax.psum_scatter(terms, "z", scatter_dimension=0, tiled=True)

    def product(received, begin, count, first, n_i, slots):
        return ladder(
            me,
            lists,
            receive_order(rows, count, first, n_i),
            amplitudes,
            received,
            weights,
            begin + first,
            n_i,
            plus.shape[1] // PAIR,
            1,
            slots,
        )

    rest = rows - FIRST
    packed0 = pack(send_order(rows, 0, FIRST), amplitudes)
    received0 = exchange(packed0)
    packed0, later = lax.optimization_barrier((packed0, amplitudes))
    packed1 = pack(send_order(rows, FIRST, rest), later)
    packed0, first_plus = lax.optimization_barrier((packed0, plus))
    lists, weights = match(cd_irrep, ab_irrep, first_plus, minus)
    received0, packed1, weights = lax.optimization_barrier((received0, packed1, weights))
    received1 = exchange(packed1)
    (terms0,) = product(received0, 0, FIRST, 0, FIRST - UNIT, N_X)
    sum0 = scatter(terms0)
    received0, _ = lax.optimization_barrier((received0, terms0))
    near0, far0 = product(received0, 0, FIRST, FIRST - UNIT, UNIT, 0)
    far0 = swap(far0)
    received1, far0 = lax.optimization_barrier((received1, far0))
    near1, far1 = product(received1, FIRST, rest, 0, UNIT, 0)
    far1 = swap(far1)
    received1, _ = lax.optimization_barrier((received1, near1))
    (terms1,) = product(received1, FIRST, rest, UNIT, rest - UNIT, 2 * N_X)
    for k, (near, far) in enumerate(((near0, far0), (near1, far1))):
        early = (near.astype(jnp.float32) + far.astype(jnp.float32)).astype(jnp.bfloat16)
        terms1 = lax.dynamic_update_slice(terms1, early, (0, N_X + k, 0, 0))
    sum1 = scatter(terms1)
    done = finish_first(sum0, swap(sum0[0, 1]))
    return finish_last(done, sum1, swap(sum1[0, 1]))


def solution(mesh):
    rows, cols = mesh.shape["row"], mesh.shape["col"]
    fine = Mesh(mesh.devices.reshape(rows, cols // N_X, N_X), ("row", "z", "xl"))
    col = ("z", "xl")
    return jax.shard_map(
        on_device,
        mesh=fine,
        in_specs=(P("row", None, col), P(col, None), P(col, None), P(col), P()),
        out_specs=P(col, "row"),
        check_vma=False,
    )
```

```python
import functools

import jax
import jax.numpy as jnp
from jax import lax
from jax.experimental import pallas as pl
from jax.experimental.pallas import tpu as pltpu
from jax.sharding import Mesh
from jax.sharding import PartitionSpec as P

TILE = 128
N_X = 2
PAIR = N_X * TILE
N_S = 4
N_IRREP = 4
BUNDLE = 4
AHEAD = 2
FIRST = 8
UNIT = 2


def params(mib=60):
    return pltpu.CompilerParams(vmem_limit_bytes=mib * 2**20)


def digits(count, last, middle):
    row = lax.broadcasted_iota(jnp.int32, (count, 1), 0)

    def over(value, size):
        return ((value.astype(jnp.float32) + 0.5) * (1.0 / size)).astype(jnp.int32)

    upper = over(row, last)
    top = over(upper, middle)
    return top, upper - top * middle, row - upper * last


def send_order(rows, first, n_i):
    s, jl, i = digits(N_S * n_i * rows, rows, n_i)
    return (i * N_S + s) * rows + first + jl


def receive_order(rows, count, first, n_i):
    i, s, jl = digits(n_i * N_S * rows, rows, N_S)
    return (s * count + first + i) * rows + jl


def pack_kernel(first, n_i, amp_ref, out_ref, held, sent, in_sem, out_sem):
    rows, occ, width = amp_ref.shape
    steps, per = sent.shape[:2]
    wide = occ // steps
    loads = [
        pltpu.make_async_copy(amp_ref.at[:, q * wide : (q + 1) * wide, :], held.at[q], in_sem.at[q])
        for q in range(steps)
    ]
    stores = [
        pltpu.make_async_copy(sent.at[q], out_ref.at[q * per : (q + 1) * per, :], out_sem.at[q])
        for q in range(steps)
    ]
    for copy in loads[:AHEAD]:
        copy.start()
    order = picker(send_order(rows, first, n_i), rows * wide)
    for q in range(steps):
        loads[q].wait()
        if q + AHEAD < steps:
            loads[q + AHEAD].start()
        block = held[q].reshape(rows * wide, width)
        sent[q] = jnp.dot(order, block, preferred_element_type=jnp.float32).astype(sent.dtype)
        stores[q].start()
    for copy in stores:
        copy.wait()


def pack(amplitudes, first, n_i):
    rows, occ, width = amplitudes.shape
    wide = N_S * rows
    steps = occ // wide
    per = N_S * n_i * rows
    hbm = pl.BlockSpec(memory_space=pl.ANY)
    return pl.pallas_call(
        functools.partial(pack_kernel, first, n_i),
        in_specs=[hbm],
        out_specs=hbm,
        out_shape=jax.ShapeDtypeStruct((steps * per, width), jnp.bfloat16),
        scratch_shapes=[
            pltpu.VMEM((steps, rows, wide, width), jnp.bfloat16),
            pltpu.VMEM((steps, per, width), jnp.bfloat16),
            pltpu.SemaphoreType.DMA((steps,)),
            pltpu.SemaphoreType.DMA((steps,)),
        ],
        compiler_params=params(),
        cost_estimate=pl.CostEstimate(
            flops=0, bytes_accessed=4 * rows * occ * width, transcendentals=0
        ),
    )(amplitudes)


def picker(places, width):
    lanes = lax.broadcasted_iota(jnp.int32, (places.shape[0], width), 1)
    return jnp.where(lanes == places, 1.0, 0.0).astype(jnp.bfloat16)

def match_kernel(cd_ref, ab_ref, plus_ref, minus_ref, lists, out_ref, held, packed, in_sem, out_sem):
    kt = cd_ref.shape[0]
    tiles = ab_ref.shape[0]
    loads = [
        pltpu.make_async_copy(plus_ref, held.at[0], in_sem.at[0]),
        pltpu.make_async_copy(minus_ref, held.at[1], in_sem.at[1]),
    ]
    for copy in loads:
        copy.start()
    there = 2 * N_IRREP
    first_step = there + 2 * kt + 2

    def of_irrep(g, carry):
        begin, step, block = carry

        def tile_of(p, n):
            same = cd_ref[p] == g

            @pl.when(same)
            def _():
                lists[there + p] = begin + n
                lists[there + kt + begin + n] = p

            return n + same.astype(jnp.int32)

        n = lax.fori_loop(0, kt, tile_of, 0)
        lists[g] = n
        lists[N_IRREP + g] = begin

        def target(q, carry):
            step, waiting, block = carry
            same = ab_ref[q] == g
            alone = same & (waiting < 0)
            second = same & (waiting >= 0)

            @pl.when(alone)
            def _():
                for k, value in enumerate((g, q, q, block)):
                    lists[first_step + 4 * step + k] = value

            @pl.when(second)
            def _():
                lists[first_step + 4 * step + 2] = q

            return (
                jnp.where(second, step + 1, step),
                jnp.where(same, jnp.where(second, -1, q), waiting),
                jnp.where(alone, block + n, block),
            )

        step, waiting, block = lax.fori_loop(0, tiles, target, (step, -1, block))
        return begin + n, jnp.where(waiting >= 0, step + 1, step), block

    _, steps, blocks = lax.fori_loop(0, N_IRREP, of_irrep, (0, 0, 0))
    bundles = (blocks + BUNDLE - 1) // BUNDLE
    lists[first_step - 2] = bundles
    lists[first_step - 1] = steps
    for copy in loads:
        copy.wait()

    @pl.loop(0, steps)
    def _(step):
        g, a, b, block = (lists[first_step + 4 * step + k] for k in range(4))
        begin = lists[N_IRREP + g]

        @pl.loop(0, lists[g])
        def _(k):
            p = pl.ds(pl.multiple_of(lists[there + kt + begin + k] * TILE, TILE), TILE)
            for half in range(2):
                for w, q in enumerate((a, b)):
                    packed[block + k, half * TILE : (half + 1) * TILE, w * TILE : (w + 1) * TILE] = (
                        held[half, p, pl.ds(pl.multiple_of(q * TILE, TILE), TILE)]
                    )

    def store(k):
        where = pl.ds(k * BUNDLE, BUNDLE)
        return pltpu.make_async_copy(packed.at[where], out_ref.at[where], out_sem.at[k])

    @pl.loop(0, bundles)
    def _(k):
        store(k).start()

    @pl.loop(0, bundles)
    def _(k):
        store(k).wait()


def match(cd_irrep, ab_irrep, plus, minus):
    width, slab = plus.shape
    kt, tiles = width // TILE, slab // TILE
    steps = (tiles + N_IRREP) // 2
    smem = pl.BlockSpec(memory_space=pltpu.SMEM)
    hbm = pl.BlockSpec(memory_space=pl.ANY)
    blocks = (tiles + 1) // N_X * kt
    shape = (blocks, PAIR, PAIR)
    return pl.pallas_call(
        match_kernel,
        in_specs=[smem, smem, hbm, hbm],
        out_specs=[smem, hbm],
        out_shape=[
            jax.ShapeDtypeStruct((2 * N_IRREP + 2 * kt + 2 + 4 * steps,), jnp.int32),
            jax.ShapeDtypeStruct(shape, jnp.bfloat16),
        ],
        scratch_shapes=[
            pltpu.VMEM((2, width, slab), jnp.bfloat16),
            pltpu.VMEM(shape, jnp.bfloat16),
            pltpu.SemaphoreType.DMA((2,)),
            pltpu.SemaphoreType.DMA((blocks // BUNDLE,)),
        ],
        compiler_params=params(),
        cost_estimate=pl.CostEstimate(
            flops=0, bytes_accessed=8 * width * slab, transcendentals=0
        ),
    )(cd_irrep, ab_irrep, plus, minus)


def ladder_kernel(begin_i, first, me_ref, lists, amp_ref, got_ref, weight_ref, *refs):
    n_out = len(refs) - 8
    out_refs = refs[:n_out]
    own, got, weights, both, staged, load_sem, weight_sem, out_sem = refs[n_out:]
    n_i, occ, width = own.shape
    kt = width // TILE
    tiles, per = staged.shape[:2]
    rows = n_i * occ
    me = me_ref[0]
    there = 2 * N_IRREP
    first_step = there + 2 * kt + 2
    bundles, steps = lists[first_step - 2], lists[first_step - 1]
    loads = [
        pltpu.make_async_copy(amp_ref.at[begin_i + first : begin_i + first + n_i], own, load_sem.at[0]),
        pltpu.make_async_copy(got_ref, got, load_sem.at[1]),
    ]
    for copy in loads:
        copy.start()

    def weights_copy(k):
        where = pl.ds(k * BUNDLE, BUNDLE)
        return pltpu.make_async_copy(weight_ref.at[where], weights.at[where], weight_sem.at[k])

    @pl.loop(0, bundles)
    def _(k):
        weights_copy(k).start()

    local = amp_ref.shape[0]
    piece = N_S * local
    span = n_i * piece
    received = got.shape[0] * piece // occ
    order = picker(receive_order(local, received // piece, first, n_i), received)
    for copy in loads:
        copy.wait()
    for q in range(occ // piece):
        other = jnp.dot(
            order, got[q * received : (q + 1) * received, :], preferred_element_type=jnp.float32
        )
        mine = own[:, q * piece : (q + 1) * piece, :].reshape(span, width).astype(jnp.float32)
        for half, value in enumerate((mine + other, mine - other)):
            value = value.astype(jnp.bfloat16).reshape(n_i, piece, width)
            for p in range(kt):
                lanes = pl.ds(pl.multiple_of(lists[there + p] * PAIR + half * TILE, TILE), TILE)
                both[:, q * piece : (q + 1) * piece, lanes] = value[:, :, p * TILE : (p + 1) * TILE]

    def out_copy(q, dst):
        return pltpu.make_async_copy(staged.at[q], dst, out_sem)

    def start(q):
        z, w = q // N_X, (q % N_X) ^ me
        if n_out == 1:
            out_copy(q, out_refs[0].at[z, pl.ds(w * per, per)]).start()
        else:
            for k in range(N_X):

                @pl.when(w == k)
                def _():
                    out_copy(q, out_refs[k].at[z]).start()

    @pl.loop(0, bundles)
    def _(k):
        weights_copy(k).wait()

    @pl.loop(0, steps)
    def _(step):
        g, a, b, block = (lists[first_step + 4 * step + k] for k in range(4))
        n, begin = lists[g], lists[N_IRREP + g]

        @pl.when(n == 0)
        def _():
            zero = jnp.zeros(staged.shape[1:], staged.dtype)
            staged[a] = zero
            staged[b] = zero

        for size in range(1, kt + 1):

            @pl.when(n == size)
            def _():
                lanes = pl.ds(pl.multiple_of(begin * PAIR, PAIR), size * PAIR)
                left = both[:, :, lanes].reshape(rows, size * PAIR)
                right = weights[pl.ds(block, size)].reshape(size * PAIR, PAIR)
                term = 0.5 * jnp.dot(left, right, preferred_element_type=jnp.float32)
                staged[a] = term[:, :TILE].astype(staged.dtype).reshape(staged.shape[1:])
                staged[b] = term[:, TILE:].astype(staged.dtype).reshape(staged.shape[1:])

        start(a)

        @pl.when(b != a)
        def _():
            start(b)

    pltpu.make_async_copy(staged, staged, out_sem).wait()


def ladder(me, lists, amplitudes, received, weights, begin, first, n_i, n_z, per, slots):
    _, occ, width = amplitudes.shape
    rows = n_i * occ
    tiles = n_z * N_X
    blocks = weights.shape[0]
    if slots:
        shapes = [(n_z, slots, rows // per, TILE)]
    else:
        shapes = [(n_z, per, rows // per, TILE)] * N_X
    smem = pl.BlockSpec(memory_space=pltpu.SMEM)
    hbm = pl.BlockSpec(memory_space=pl.ANY)
    dma = pltpu.SemaphoreType.DMA
    bf16 = jnp.bfloat16
    return pl.pallas_call(
        functools.partial(ladder_kernel, begin, first),
        in_specs=[smem, smem, hbm, hbm, hbm],
        out_specs=[hbm] * len(shapes),
        out_shape=[jax.ShapeDtypeStruct(s, bf16) for s in shapes],
        scratch_shapes=[
            pltpu.VMEM((n_i, occ, width), bf16),
            pltpu.VMEM(received.shape, bf16),
            pltpu.VMEM(weights.shape, bf16),
            pltpu.VMEM((n_i, occ, 2 * width), bf16),
            pltpu.VMEM((tiles, per, rows // per, TILE), bf16),
            dma((2,)),
            dma((blocks // BUNDLE,)),
            dma,
        ],
        compiler_params=params(50),
        cost_estimate=pl.CostEstimate(
            flops=0, bytes_accessed=8 * rows * (width + n_z * TILE), transcendentals=0
        ),
    )(me, lists, amplitudes, received, weights)


def finish_kernel(near, far, *refs):
    out_ref = refs[-1]
    total = near[...].astype(jnp.float32).reshape(-1, TILE) + far[...].astype(jnp.float32)
    if len(refs) > 1:
        early = refs[0][...].astype(jnp.float32).reshape(-1, TILE)
        total = jnp.concatenate([early, total], 0)
    out_ref[...] = total.T.astype(out_ref.dtype)


def slots(ref, count, k):
    return pl.BlockSpec((1, count) + ref.shape[2:], lambda g: (0, k, 0, 0))


def finish_first(near, far):
    rows = far.shape[0]
    return pl.pallas_call(
        finish_kernel,
        grid=(1,),
        in_specs=[slots(near, 1, 0), pl.BlockSpec(far.shape, lambda g: (0, 0))],
        out_specs=pl.BlockSpec((TILE, rows), lambda g: (0, 0)),
        out_shape=jax.ShapeDtypeStruct((TILE, 2 * rows), jnp.bfloat16),
        compiler_params=params(57),
    )(near, far)


def finish_last(done, sum1, far):
    early = sum1.shape[1] - N_X
    return pl.pallas_call(
        lambda done_ref, *refs: finish_kernel(*refs),
        grid=(1,),
        in_specs=[
            pl.BlockSpec(memory_space=pl.ANY),
            slots(sum1, 1, 0),
            pl.BlockSpec(far.shape, lambda g: (0, 0)),
            slots(sum1, early, N_X // early),
        ],
        out_specs=pl.BlockSpec((TILE, done.shape[1] // 2), lambda g: (0, 1)),
        out_shape=jax.ShapeDtypeStruct(done.shape, jnp.bfloat16),
        input_output_aliases={0: 0},
        compiler_params=params(16),
    )(done, sum1, far, sum1)


def on_device(amplitudes, plus, minus, cd_irrep, ab_irrep):
    rows = amplitudes.shape[0]
    me = lax.axis_index("xl").reshape(1).astype(jnp.int32)
    swap = functools.partial(lax.ppermute, axis_name="xl", perm=[(0, 1), (1, 0)])

    def exchange(packed):
        return lax.all_to_all(packed, "row", split_axis=0, concat_axis=0, tiled=True)

    def scatter(terms):
        return lax.psum_scatter(terms, "z", scatter_dimension=0, tiled=True)

    def product(received, begin, first, n_i, slots):
        return ladder(
            me,
            lists,
            amplitudes,
            received,
            weights,
            begin,
            first,
            n_i,
            plus.shape[1] // PAIR,
            1,
            slots,
        )

    rest = rows - FIRST
    packed0 = pack(amplitudes, 0, FIRST)
    received0 = exchange(packed0)
    packed0, later = lax.optimization_barrier((packed0, amplitudes))
    packed1 = pack(later, FIRST, rest)
    packed0, first_plus = lax.optimization_barrier((packed0, plus))
    lists, weights = match(cd_irrep, ab_irrep, first_plus, minus)
    received0, packed1, weights = lax.optimization_barrier((received0, packed1, weights))
    received1 = exchange(packed1)
    (terms0,) = product(received0, 0, 0, FIRST - UNIT, N_X)
    sum0 = scatter(terms0)
    received0, _ = lax.optimization_barrier((received0, terms0))
    near0, far0 = product(received0, 0, FIRST - UNIT, UNIT, 0)
    far0 = swap(far0)
    received1, _ = lax.optimization_barrier((received1, near0))
    near1, far1 = product(received1, FIRST, 0, UNIT, 0)
    far1 = swap(far1)
    received1, _ = lax.optimization_barrier((received1, near1))
    (terms1,) = product(received1, FIRST, UNIT, rest - UNIT, 2 * N_X)
    for k, (near, far) in enumerate(((near0, far0), (near1, far1))):
        early = (near.astype(jnp.float32) + far.astype(jnp.float32)).astype(jnp.bfloat16)
        terms1 = lax.dynamic_update_slice(terms1, early, (0, N_X + k, 0, 0))
    sum1 = scatter(terms1)
    done = finish_first(sum0, swap(sum0[0, 1]))
    return finish_last(done, sum1, swap(sum1[0, 1]))


def solution(mesh):
    rows, cols = mesh.shape["row"], mesh.shape["col"]
    fine = Mesh(mesh.devices.reshape(rows, cols // N_X, N_X), ("row", "z", "xl"))
    col = ("z", "xl")
    return jax.shard_map(
        on_device,
        mesh=fine,
        in_specs=(P("row", None, col), P(col, None), P(col, None), P(col), P()),
        out_specs=P(col, "row"),
        check_vma=False,
    )
```

```python
import functools

import jax
import jax.numpy as jnp
from jax import lax
from jax.experimental import pallas as pl
from jax.experimental.pallas import tpu as pltpu
from jax.sharding import Mesh
from jax.sharding import PartitionSpec as P

TILE = 128
N_X = 2
PAIR = N_X * TILE
N_S = 4
N_IRREP = 4
BUNDLE = 4
AHEAD = 2
FIRST = 8
EARLY = (3, 2)


def params(mib=60):
    return pltpu.CompilerParams(vmem_limit_bytes=mib * 2**20)


def digits(count, last, middle):
    row = lax.broadcasted_iota(jnp.int32, (count, 1), 0)

    def over(value, size):
        return ((value.astype(jnp.float32) + 0.5) * (1.0 / size)).astype(jnp.int32)

    upper = over(row, last)
    top = over(upper, middle)
    return top, upper - top * middle, row - upper * last


def send_order(rows, first, n_i):
    s, jl, i = digits(N_S * n_i * rows, rows, n_i)
    return (i * N_S + s) * rows + first + jl


def receive_order(rows, n_i):
    i, s, jl = digits(n_i * N_S * rows, rows, N_S)
    return (s * n_i + i) * rows + jl


def pack_kernel(first, n_i, amp_ref, out_ref, held, sent, in_sem, out_sem):
    rows, occ, width = amp_ref.shape
    steps, per = sent.shape[:2]
    wide = occ // steps
    loads = [
        pltpu.make_async_copy(amp_ref.at[:, q * wide : (q + 1) * wide, :], held.at[q], in_sem.at[q])
        for q in range(steps)
    ]
    stores = [
        pltpu.make_async_copy(sent.at[q], out_ref.at[q * per : (q + 1) * per, :], out_sem.at[q])
        for q in range(steps)
    ]
    for copy in loads[:AHEAD]:
        copy.start()
    order = picker(send_order(rows, first, n_i), rows * wide)
    for q in range(steps):
        loads[q].wait()
        if q + AHEAD < steps:
            loads[q + AHEAD].start()
        block = held[q].reshape(rows * wide, width)
        sent[q] = jnp.dot(order, block, preferred_element_type=jnp.float32).astype(sent.dtype)
        stores[q].start()
    for copy in stores:
        copy.wait()


def pack(amplitudes, first, n_i):
    rows, occ, width = amplitudes.shape
    wide = N_S * rows
    steps = occ // wide
    per = N_S * n_i * rows
    hbm = pl.BlockSpec(memory_space=pl.ANY)
    return pl.pallas_call(
        functools.partial(pack_kernel, first, n_i),
        in_specs=[hbm],
        out_specs=hbm,
        out_shape=jax.ShapeDtypeStruct((steps * per, width), jnp.bfloat16),
        scratch_shapes=[
            pltpu.VMEM((steps, rows, wide, width), jnp.bfloat16),
            pltpu.VMEM((steps, per, width), jnp.bfloat16),
            pltpu.SemaphoreType.DMA((steps,)),
            pltpu.SemaphoreType.DMA((steps,)),
        ],
        compiler_params=params(),
        cost_estimate=pl.CostEstimate(
            flops=0, bytes_accessed=4 * rows * occ * width, transcendentals=0
        ),
    )(amplitudes)


def picker(places, width):
    lanes = lax.broadcasted_iota(jnp.int32, (places.shape[0], width), 1)
    return jnp.where(lanes == places, 1.0, 0.0).astype(jnp.bfloat16)

def match_kernel(cd_ref, ab_ref, plus_ref, minus_ref, lists, out_ref, held, packed, in_sem, out_sem):
    kt = cd_ref.shape[0]
    tiles = ab_ref.shape[0]
    loads = [
        pltpu.make_async_copy(plus_ref, held.at[0], in_sem.at[0]),
        pltpu.make_async_copy(minus_ref, held.at[1], in_sem.at[1]),
    ]
    for copy in loads:
        copy.start()
    there = 2 * N_IRREP
    first_step = there + 2 * kt + 2

    def of_irrep(g, carry):
        begin, step, block = carry

        def tile_of(p, n):
            same = cd_ref[p] == g

            @pl.when(same)
            def _():
                lists[there + p] = begin + n
                lists[there + kt + begin + n] = p

            return n + same.astype(jnp.int32)

        n = lax.fori_loop(0, kt, tile_of, 0)
        lists[g] = n
        lists[N_IRREP + g] = begin

        def target(q, carry):
            step, waiting, block = carry
            same = ab_ref[q] == g
            alone = same & (waiting < 0)
            second = same & (waiting >= 0)

            @pl.when(alone)
            def _():
                for k, value in enumerate((g, q, q, block)):
                    lists[first_step + 4 * step + k] = value

            @pl.when(second)
            def _():
                lists[first_step + 4 * step + 2] = q

            return (
                jnp.where(second, step + 1, step),
                jnp.where(same, jnp.where(second, -1, q), waiting),
                jnp.where(alone, block + n, block),
            )

        step, waiting, block = lax.fori_loop(0, tiles, target, (step, -1, block))
        return begin + n, jnp.where(waiting >= 0, step + 1, step), block

    _, steps, blocks = lax.fori_loop(0, N_IRREP, of_irrep, (0, 0, 0))
    bundles = (blocks + BUNDLE - 1) // BUNDLE
    lists[first_step - 2] = bundles
    lists[first_step - 1] = steps
    for copy in loads:
        copy.wait()

    @pl.loop(0, steps)
    def _(step):
        g, a, b, block = (lists[first_step + 4 * step + k] for k in range(4))
        begin = lists[N_IRREP + g]

        @pl.loop(0, lists[g])
        def _(k):
            p = pl.ds(pl.multiple_of(lists[there + kt + begin + k] * TILE, TILE), TILE)
            for half in range(2):
                for w, q in enumerate((a, b)):
                    packed[block + k, half * TILE : (half + 1) * TILE, w * TILE : (w + 1) * TILE] = (
                        held[half, p, pl.ds(pl.multiple_of(q * TILE, TILE), TILE)]
                    )

    def store(k):
        where = pl.ds(k * BUNDLE, BUNDLE)
        return pltpu.make_async_copy(packed.at[where], out_ref.at[where], out_sem.at[k])

    @pl.loop(0, bundles)
    def _(k):
        store(k).start()

    @pl.loop(0, bundles)
    def _(k):
        store(k).wait()


def match(cd_irrep, ab_irrep, plus, minus):
    width, slab = plus.shape
    kt, tiles = width // TILE, slab // TILE
    steps = (tiles + N_IRREP) // 2
    smem = pl.BlockSpec(memory_space=pltpu.SMEM)
    hbm = pl.BlockSpec(memory_space=pl.ANY)
    blocks = (tiles + 1) // N_X * kt
    shape = (blocks, PAIR, PAIR)
    return pl.pallas_call(
        match_kernel,
        in_specs=[smem, smem, hbm, hbm],
        out_specs=[smem, hbm],
        out_shape=[
            jax.ShapeDtypeStruct((2 * N_IRREP + 2 * kt + 2 + 4 * steps,), jnp.int32),
            jax.ShapeDtypeStruct(shape, jnp.bfloat16),
        ],
        scratch_shapes=[
            pltpu.VMEM((2, width, slab), jnp.bfloat16),
            pltpu.VMEM(shape, jnp.bfloat16),
            pltpu.SemaphoreType.DMA((2,)),
            pltpu.SemaphoreType.DMA((blocks // BUNDLE,)),
        ],
        compiler_params=params(),
        cost_estimate=pl.CostEstimate(
            flops=0, bytes_accessed=8 * width * slab, transcendentals=0
        ),
    )(cd_irrep, ab_irrep, plus, minus)


def ladder_kernel(begin_i, parts, me_ref, lists, amp_ref, got_ref, weight_ref, *refs):
    terms, near, far, own, got, weights, both, staged, load_sem, weight_sem, out_sem = refs
    late, early = parts
    n_i, occ, width = own.shape
    kt = width // TILE
    tiles = staged.shape[0]
    rows = n_i * occ
    me = me_ref[0]
    there = 2 * N_IRREP
    first_step = there + 2 * kt + 2
    bundles, steps = lists[first_step - 2], lists[first_step - 1]
    loads = [
        pltpu.make_async_copy(amp_ref.at[begin_i : begin_i + n_i], own, load_sem.at[0]),
        pltpu.make_async_copy(got_ref, got, load_sem.at[1]),
    ]
    for copy in loads:
        copy.start()

    def weights_copy(k):
        where = pl.ds(k * BUNDLE, BUNDLE)
        return pltpu.make_async_copy(weight_ref.at[where], weights.at[where], weight_sem.at[k])

    @pl.loop(0, bundles)
    def _(k):
        weights_copy(k).start()

    local = amp_ref.shape[0]
    piece = N_S * local
    span = n_i * piece
    received = got.shape[0] * piece // occ
    order = picker(receive_order(local, n_i), received)
    for copy in loads:
        copy.wait()
    for q in range(occ // piece):
        other = jnp.dot(
            order, got[q * received : (q + 1) * received, :], preferred_element_type=jnp.float32
        )
        mine = own[:, q * piece : (q + 1) * piece, :].reshape(span, width).astype(jnp.float32)
        for half, value in enumerate((mine + other, mine - other)):
            value = value.astype(jnp.bfloat16).reshape(n_i, piece, width)
            for p in range(kt):
                lanes = pl.ds(pl.multiple_of(lists[there + p] * PAIR + half * TILE, TILE), TILE)
                both[:, q * piece : (q + 1) * piece, lanes] = value[:, :, p * TILE : (p + 1) * TILE]

    def start(q):
        z, w = q // N_X, (q % N_X) ^ me
        per = late.stop - late.start
        pltpu.make_async_copy(
            staged.at[q, late], terms.at[z, pl.ds(w * per, per)], out_sem
        ).start()
        for k, ref in enumerate((near, far)):

            @pl.when(w == k)
            def _():
                pltpu.make_async_copy(staged.at[q, early], ref.at[z], out_sem).start()

    @pl.loop(0, bundles)
    def _(k):
        weights_copy(k).wait()

    @pl.loop(0, steps)
    def _(step):
        g, a, b, block = (lists[first_step + 4 * step + k] for k in range(4))
        n, begin = lists[g], lists[N_IRREP + g]

        @pl.when(n == 0)
        def _():
            zero = jnp.zeros(staged.shape[1:], staged.dtype)
            staged[a] = zero
            staged[b] = zero

        for size in range(1, kt + 1):

            @pl.when(n == size)
            def _():
                lanes = pl.ds(pl.multiple_of(begin * PAIR, PAIR), size * PAIR)
                left = both[:, :, lanes].reshape(rows, size * PAIR)
                right = weights[pl.ds(block, size)].reshape(size * PAIR, PAIR)
                term = 0.5 * jnp.dot(left, right, preferred_element_type=jnp.float32)
                staged[a] = term[:, :TILE].astype(staged.dtype).reshape(staged.shape[1:])
                staged[b] = term[:, TILE:].astype(staged.dtype).reshape(staged.shape[1:])

        start(a)

        @pl.when(b != a)
        def _():
            start(b)

    pltpu.make_async_copy(staged, staged, out_sem).wait()


def ladder(me, lists, amplitudes, received, weights, begin, n_i, n_z, late, early, slots):
    _, occ, width = amplitudes.shape
    tiles = n_z * N_X
    blocks = weights.shape[0]
    apart = (n_z, early.stop - early.start, occ, TILE)
    smem = pl.BlockSpec(memory_space=pltpu.SMEM)
    hbm = pl.BlockSpec(memory_space=pl.ANY)
    dma = pltpu.SemaphoreType.DMA
    bf16 = jnp.bfloat16
    return pl.pallas_call(
        functools.partial(ladder_kernel, begin, (late, early)),
        in_specs=[smem, smem, hbm, hbm, hbm],
        out_specs=[hbm] * 3,
        out_shape=[
            jax.ShapeDtypeStruct(s, bf16) for s in ((n_z, slots, occ, TILE), apart, apart)
        ],
        scratch_shapes=[
            pltpu.VMEM((n_i, occ, width), bf16),
            pltpu.VMEM(received.shape, bf16),
            pltpu.VMEM(weights.shape, bf16),
            pltpu.VMEM((n_i, occ, 2 * width), bf16),
            pltpu.VMEM((tiles, n_i, occ, TILE), bf16),
            dma((2,)),
            dma((blocks // BUNDLE,)),
            dma,
        ],
        compiler_params=params(48),
        cost_estimate=pl.CostEstimate(
            flops=0, bytes_accessed=8 * n_i * occ * (width + n_z * TILE), transcendentals=0
        ),
    )(me, lists, amplitudes, received, weights)


def total(*refs):
    terms = [ref[...].astype(jnp.float32).reshape(-1, TILE) for ref in refs]
    return functools.reduce(jnp.add, terms)


def slots(ref, count, k):
    return pl.BlockSpec((1, count) + ref.shape[2:], lambda g: (0, k, 0, 0))


def finish_first(near, far, n_i, n_all):
    occ = near.shape[2]
    rows = n_i * occ

    def kernel(near_ref, far_ref, out_ref):
        out_ref[...] = total(near_ref, far_ref).T.astype(out_ref.dtype)

    return pl.pallas_call(
        kernel,
        grid=(1,),
        in_specs=[slots(near, n_i, 0), pl.BlockSpec((rows, TILE), lambda g: (0, 0))],
        out_specs=pl.BlockSpec((TILE, rows), lambda g: (0, 0)),
        out_shape=jax.ShapeDtypeStruct((TILE, n_all * occ), jnp.bfloat16),
        compiler_params=params(57),
    )(near, far)


def finish_last(done, n_done, sum0, far0, sum1, far1):
    occ = sum1.shape[2]
    late = far1.shape[0] // occ
    left = far0.shape[0] // occ - n_done
    begin = n_done * occ
    whole = pl.BlockSpec(memory_space=pltpu.VMEM)
    hbm = pl.BlockSpec(memory_space=pl.ANY)

    def kernel(done_ref, near0_ref, far0_ref, sum1_ref, far1_ref, out_ref, held, sem):
        summed = sum1_ref[0].astype(jnp.float32)
        parts = [
            total(near0_ref, far0_ref),
            summed[N_X * late :].reshape(-1, TILE),
            summed[:late].reshape(-1, TILE) + far1_ref[...].astype(jnp.float32),
        ]
        held[...] = jnp.concatenate(parts, 0).T.astype(held.dtype)
        copy = pltpu.make_async_copy(held, out_ref.at[:, begin:], sem)
        copy.start()
        copy.wait()

    return pl.pallas_call(
        kernel,
        grid=(1,),
        in_specs=[
            hbm,
            slots(sum0, left, n_done // left),
            pl.BlockSpec((left * occ, TILE), lambda g: (n_done // left, 0)),
            whole,
            whole,
        ],
        out_specs=hbm,
        out_shape=jax.ShapeDtypeStruct(done.shape, jnp.bfloat16),
        scratch_shapes=[
            pltpu.VMEM((TILE, done.shape[1] - begin), jnp.bfloat16),
            pltpu.SemaphoreType.DMA,
        ],
        input_output_aliases={0: 0},
        compiler_params=params(57),
    )(done, sum0, far0, sum1, far1)


def on_device(amplitudes, plus, minus, cd_irrep, ab_irrep):
    rows = amplitudes.shape[0]
    me = lax.axis_index("xl").reshape(1).astype(jnp.int32)
    swap = functools.partial(lax.ppermute, axis_name="xl", perm=[(0, 1), (1, 0)])

    def exchange(packed):
        return lax.all_to_all(packed, "row", split_axis=0, concat_axis=0, tiled=True)

    def scatter(terms):
        return lax.psum_scatter(terms, "z", scatter_dimension=0, tiled=True)

    def product(received, begin, n_i, late, early, slots):
        n_z = plus.shape[1] // PAIR
        return ladder(
            me, lists, amplitudes, received, weights, begin, n_i, n_z, late, early, slots
        )

    rest = rows - FIRST
    packed0 = pack(amplitudes, 0, FIRST)
    received0 = exchange(packed0)
    packed0, later = lax.optimization_barrier((packed0, amplitudes))
    packed1 = pack(later, FIRST, rest)
    packed0, first_plus = lax.optimization_barrier((packed0, plus))
    lists, weights = match(cd_irrep, ab_irrep, first_plus, minus)
    received0, packed1, weights = lax.optimization_barrier((received0, packed1, weights))
    received1 = exchange(packed1)
    n0, n1 = FIRST - EARLY[0], rest - EARLY[1]
    terms0, near0, far0 = product(
        received0, 0, FIRST, slice(0, n0), slice(n0, FIRST), N_X * n0
    )
    sum0 = scatter(terms0)
    far0 = swap(far0)
    received1, _ = lax.optimization_barrier((received1, near0))
    terms1, near1, far1 = product(
        received1, FIRST, rest, slice(EARLY[1], rest), slice(0, EARLY[1]), N_X * n1 + sum(EARLY)
    )
    far1 = swap(far1)
    at = N_X * n1
    for near, far in ((near0, far0), (near1, far1)):
        early = (near.astype(jnp.float32) + far.astype(jnp.float32)).astype(jnp.bfloat16)
        terms1 = lax.dynamic_update_slice(terms1, early, (0, at, 0, 0))
        at += near.shape[1]
    sum1 = scatter(terms1)
    last0 = swap(sum0[0, n0:].reshape(-1, TILE))
    n_done = n0 // 2 * 2
    done = finish_first(sum0, last0, n_done, rows)
    last1 = swap(sum1[0, n1 : N_X * n1].reshape(-1, TILE))
    return finish_last(done, n_done, sum0, last0, sum1, last1)


def solution(mesh):
    rows, cols = mesh.shape["row"], mesh.shape["col"]
    fine = Mesh(mesh.devices.reshape(rows, cols // N_X, N_X), ("row", "z", "xl"))
    col = ("z", "xl")
    return jax.shard_map(
        on_device,
        mesh=fine,
        in_specs=(P("row", None, col), P(col, None), P(col, None), P(col), P()),
        out_specs=P(col, "row"),
        check_vma=False,
    )
```

```python
import functools

import jax
import jax.numpy as jnp
from jax import lax
from jax.experimental import pallas as pl
from jax.experimental.pallas import tpu as pltpu
from jax.sharding import Mesh
from jax.sharding import PartitionSpec as P

TILE = 128
N_X = 2
PAIR = N_X * TILE
N_S = 4
N_IRREP = 4
BUNDLE = 4
AHEAD = 2
FIRST = 8
UNIT = 2


def params(mib=60):
    return pltpu.CompilerParams(vmem_limit_bytes=mib * 2**20)


def digits(count, last, middle):
    row = lax.broadcasted_iota(jnp.int32, (count, 1), 0)

    def over(value, size):
        return ((value.astype(jnp.float32) + 0.5) * (1.0 / size)).astype(jnp.int32)

    upper = over(row, last)
    top = over(upper, middle)
    return top, upper - top * middle, row - upper * last


def send_order(rows, first, n_i):
    s, jl, i = digits(N_S * n_i * rows, rows, n_i)
    return (i * N_S + s) * rows + first + jl


def receive_order(rows, count, first, n_i):
    i, s, jl = digits(n_i * N_S * rows, rows, N_S)
    return (s * count + first + i) * rows + jl


def pack_kernel(first, n_i, amp_ref, out_ref, held, sent, in_sem, out_sem):
    rows, occ, width = amp_ref.shape
    steps, per = sent.shape[:2]
    wide = occ // steps
    loads = [
        pltpu.make_async_copy(amp_ref.at[:, q * wide : (q + 1) * wide, :], held.at[q], in_sem.at[q])
        for q in range(steps)
    ]
    stores = [
        pltpu.make_async_copy(sent.at[q], out_ref.at[q * per : (q + 1) * per, :], out_sem.at[q])
        for q in range(steps)
    ]
    for copy in loads[:AHEAD]:
        copy.start()
    order = picker(send_order(rows, first, n_i), rows * wide)
    for q in range(steps):
        loads[q].wait()
        if q + AHEAD < steps:
            loads[q + AHEAD].start()
        block = held[q].reshape(rows * wide, width)
        sent[q] = jnp.dot(order, block, preferred_element_type=jnp.float32).astype(sent.dtype)
        stores[q].start()
    for copy in stores:
        copy.wait()


def pack(amplitudes, first, n_i):
    rows, occ, width = amplitudes.shape
    wide = N_S * rows
    steps = occ // wide
    per = N_S * n_i * rows
    hbm = pl.BlockSpec(memory_space=pl.ANY)
    return pl.pallas_call(
        functools.partial(pack_kernel, first, n_i),
        in_specs=[hbm],
        out_specs=hbm,
        out_shape=jax.ShapeDtypeStruct((steps * per, width), jnp.bfloat16),
        scratch_shapes=[
            pltpu.VMEM((steps, rows, wide, width), jnp.bfloat16),
            pltpu.VMEM((steps, per, width), jnp.bfloat16),
            pltpu.SemaphoreType.DMA((steps,)),
            pltpu.SemaphoreType.DMA((steps,)),
        ],
        compiler_params=params(),
        cost_estimate=pl.CostEstimate(
            flops=0, bytes_accessed=4 * rows * occ * width, transcendentals=0
        ),
    )(amplitudes)


def picker(places, width):
    lanes = lax.broadcasted_iota(jnp.int32, (places.shape[0], width), 1)
    return jnp.where(lanes == places, 1.0, 0.0).astype(jnp.bfloat16)

def match_kernel(cd_ref, ab_ref, plus_ref, minus_ref, lists, out_ref, held, packed, in_sem, out_sem):
    kt = cd_ref.shape[0]
    tiles = ab_ref.shape[0]
    loads = [
        pltpu.make_async_copy(plus_ref, held.at[0], in_sem.at[0]),
        pltpu.make_async_copy(minus_ref, held.at[1], in_sem.at[1]),
    ]
    for copy in loads:
        copy.start()
    there = 2 * N_IRREP
    first_step = there + 2 * kt + 2

    def of_irrep(g, carry):
        begin, step, block = carry

        def tile_of(p, n):
            same = cd_ref[p] == g

            @pl.when(same)
            def _():
                lists[there + p] = begin + n
                lists[there + kt + begin + n] = p

            return n + same.astype(jnp.int32)

        n = lax.fori_loop(0, kt, tile_of, 0)
        lists[g] = n
        lists[N_IRREP + g] = begin

        def target(q, carry):
            step, waiting, block = carry
            same = ab_ref[q] == g
            alone = same & (waiting < 0)
            second = same & (waiting >= 0)

            @pl.when(alone)
            def _():
                for k, value in enumerate((g, q, q, block)):
                    lists[first_step + 4 * step + k] = value

            @pl.when(second)
            def _():
                lists[first_step + 4 * step + 2] = q

            return (
                jnp.where(second, step + 1, step),
                jnp.where(same, jnp.where(second, -1, q), waiting),
                jnp.where(alone, block + n, block),
            )

        step, waiting, block = lax.fori_loop(0, tiles, target, (step, -1, block))
        return begin + n, jnp.where(waiting >= 0, step + 1, step), block

    _, steps, blocks = lax.fori_loop(0, N_IRREP, of_irrep, (0, 0, 0))
    bundles = (blocks + BUNDLE - 1) // BUNDLE
    lists[first_step - 2] = bundles
    lists[first_step - 1] = steps
    for copy in loads:
        copy.wait()

    @pl.loop(0, steps)
    def _(step):
        g, a, b, block = (lists[first_step + 4 * step + k] for k in range(4))
        begin = lists[N_IRREP + g]

        @pl.loop(0, lists[g])
        def _(k):
            p = pl.ds(pl.multiple_of(lists[there + kt + begin + k] * TILE, TILE), TILE)
            for half in range(2):
                for w, q in enumerate((a, b)):
                    packed[block + k, half * TILE : (half + 1) * TILE, w * TILE : (w + 1) * TILE] = (
                        held[half, p, pl.ds(pl.multiple_of(q * TILE, TILE), TILE)]
                    )

    def store(k):
        where = pl.ds(k * BUNDLE, BUNDLE)
        return pltpu.make_async_copy(packed.at[where], out_ref.at[where], out_sem.at[k])

    @pl.loop(0, bundles)
    def _(k):
        store(k).start()

    @pl.loop(0, bundles)
    def _(k):
        store(k).wait()


def match(cd_irrep, ab_irrep, plus, minus):
    width, slab = plus.shape
    kt, tiles = width // TILE, slab // TILE
    steps = (tiles + N_IRREP) // 2
    smem = pl.BlockSpec(memory_space=pltpu.SMEM)
    hbm = pl.BlockSpec(memory_space=pl.ANY)
    blocks = (tiles + 1) // N_X * kt
    shape = (blocks, PAIR, PAIR)
    return pl.pallas_call(
        match_kernel,
        in_specs=[smem, smem, hbm, hbm],
        out_specs=[smem, hbm],
        out_shape=[
            jax.ShapeDtypeStruct((2 * N_IRREP + 2 * kt + 2 + 4 * steps,), jnp.int32),
            jax.ShapeDtypeStruct(shape, jnp.bfloat16),
        ],
        scratch_shapes=[
            pltpu.VMEM((2, width, slab), jnp.bfloat16),
            pltpu.VMEM(shape, jnp.bfloat16),
            pltpu.SemaphoreType.DMA((2,)),
            pltpu.SemaphoreType.DMA((blocks // BUNDLE,)),
        ],
        compiler_params=params(),
        cost_estimate=pl.CostEstimate(
            flops=0, bytes_accessed=8 * width * slab, transcendentals=0
        ),
    )(cd_irrep, ab_irrep, plus, minus)


def ladder_kernel(begin_i, first, me_ref, lists, amp_ref, got_ref, weight_ref, *refs):
    n_out = len(refs) - 8
    out_refs = refs[:n_out]
    own, got, weights, both, staged, load_sem, weight_sem, out_sem = refs[n_out:]
    n_i, occ, width = own.shape
    kt = width // TILE
    tiles, per = staged.shape[:2]
    rows = n_i * occ
    me = me_ref[0]
    there = 2 * N_IRREP
    first_step = there + 2 * kt + 2
    bundles, steps = lists[first_step - 2], lists[first_step - 1]
    loads = [
        pltpu.make_async_copy(amp_ref.at[begin_i + first : begin_i + first + n_i], own, load_sem.at[0]),
        pltpu.make_async_copy(got_ref, got, load_sem.at[1]),
    ]
    for copy in loads:
        copy.start()

    def weights_copy(k):
        where = pl.ds(k * BUNDLE, BUNDLE)
        return pltpu.make_async_copy(weight_ref.at[where], weights.at[where], weight_sem.at[k])

    @pl.loop(0, bundles)
    def _(k):
        weights_copy(k).start()

    local = amp_ref.shape[0]
    piece = N_S * local
    span = n_i * piece
    received = got.shape[0] * piece // occ
    order = picker(receive_order(local, received // piece, first, n_i), received)
    for copy in loads:
        copy.wait()
    for q in range(occ // piece):
        other = jnp.dot(
            order, got[q * received : (q + 1) * received, :], preferred_element_type=jnp.float32
        )
        mine = own[:, q * piece : (q + 1) * piece, :].reshape(span, width).astype(jnp.float32)
        for half, value in enumerate((mine + other, mine - other)):
            value = value.astype(jnp.bfloat16).reshape(n_i, piece, width)
            for p in range(kt):
                lanes = pl.ds(pl.multiple_of(lists[there + p] * PAIR + half * TILE, TILE), TILE)
                both[:, q * piece : (q + 1) * piece, lanes] = value[:, :, p * TILE : (p + 1) * TILE]

    def out_copy(q, dst):
        return pltpu.make_async_copy(staged.at[q], dst, out_sem)

    def start(q):
        z, w = (q // N_X - me_ref[1]) & (tiles // N_X - 1), (q % N_X) ^ me
        if n_out == 1:
            out_copy(q, out_refs[0].at[z, pl.ds(w * per, per)]).start()
        else:
            for k in range(N_X):

                @pl.when(w == k)
                def _():
                    out_copy(q, out_refs[k].at[z]).start()

    @pl.loop(0, bundles)
    def _(k):
        weights_copy(k).wait()

    @pl.loop(0, steps)
    def _(step):
        g, a, b, block = (lists[first_step + 4 * step + k] for k in range(4))
        n, begin = lists[g], lists[N_IRREP + g]

        @pl.when(n == 0)
        def _():
            zero = jnp.zeros(staged.shape[1:], staged.dtype)
            staged[a] = zero
            staged[b] = zero

        for size in range(1, kt + 1):

            @pl.when(n == size)
            def _():
                lanes = pl.ds(pl.multiple_of(begin * PAIR, PAIR), size * PAIR)
                left = both[:, :, lanes].reshape(rows, size * PAIR)
                right = weights[pl.ds(block, size)].reshape(size * PAIR, PAIR)
                term = 0.5 * jnp.dot(left, right, preferred_element_type=jnp.float32)
                staged[a] = term[:, :TILE].astype(staged.dtype).reshape(staged.shape[1:])
                staged[b] = term[:, TILE:].astype(staged.dtype).reshape(staged.shape[1:])

        start(a)

        @pl.when(b != a)
        def _():
            start(b)

    pltpu.make_async_copy(staged, staged, out_sem).wait()


def ladder(place, lists, amplitudes, received, weights, begin, first, n_i, n_z, per, slots):
    _, occ, width = amplitudes.shape
    rows = n_i * occ
    tiles = n_z * N_X
    blocks = weights.shape[0]
    if slots:
        shapes = [(n_z, slots, rows // per, TILE)]
    else:
        shapes = [(n_z, per, rows // per, TILE)] * N_X
    smem = pl.BlockSpec(memory_space=pltpu.SMEM)
    hbm = pl.BlockSpec(memory_space=pl.ANY)
    dma = pltpu.SemaphoreType.DMA
    bf16 = jnp.bfloat16
    return pl.pallas_call(
        functools.partial(ladder_kernel, begin, first),
        in_specs=[smem, smem, hbm, hbm, hbm],
        out_specs=[hbm] * len(shapes),
        out_shape=[jax.ShapeDtypeStruct(s, bf16) for s in shapes],
        scratch_shapes=[
            pltpu.VMEM((n_i, occ, width), bf16),
            pltpu.VMEM(received.shape, bf16),
            pltpu.VMEM(weights.shape, bf16),
            pltpu.VMEM((n_i, occ, 2 * width), bf16),
            pltpu.VMEM((tiles, per, rows // per, TILE), bf16),
            dma((2,)),
            dma((blocks // BUNDLE,)),
            dma,
        ],
        compiler_params=params(50),
        cost_estimate=pl.CostEstimate(
            flops=0, bytes_accessed=8 * rows * (width + n_z * TILE), transcendentals=0
        ),
    )(place, lists, amplitudes, received, weights)


def finish_kernel(near, far, *refs):
    out_ref = refs[-1]
    total = near[...].astype(jnp.float32).reshape(-1, TILE) + far[...].astype(jnp.float32)
    if len(refs) > 1:
        early = refs[0][...].astype(jnp.float32).reshape(-1, TILE)
        total = jnp.concatenate([early, total], 0)
    out_ref[...] = total.T.astype(out_ref.dtype)


def slots(ref, count, k):
    return pl.BlockSpec((1, count) + ref.shape[2:], lambda g: (0, k, 0, 0))


def finish_first(near, far):
    rows = far.shape[0]
    return pl.pallas_call(
        finish_kernel,
        grid=(1,),
        in_specs=[slots(near, 1, 0), pl.BlockSpec(far.shape, lambda g: (0, 0))],
        out_specs=pl.BlockSpec((TILE, rows), lambda g: (0, 0)),
        out_shape=jax.ShapeDtypeStruct((TILE, 2 * rows), jnp.bfloat16),
        compiler_params=params(57),
    )(near, far)


def finish_last(done, early, up, down, late, far):
    whole = pl.BlockSpec(memory_space=pltpu.VMEM)
    hbm = pl.BlockSpec(memory_space=pl.ANY)
    rows = early.shape[0] + late.shape[0]
    begin = done.shape[1] - rows

    def kernel(done_ref, early_ref, up_ref, down_ref, late_ref, far_ref, out_ref, held, sem):
        first = early_ref[...]
        for ref in (up_ref, down_ref):
            first = first + ref[...].astype(jnp.float32).reshape(-1, TILE)
        last = late_ref[...] + far_ref[...].astype(jnp.float32)
        held[...] = jnp.concatenate([first, last], 0).T.astype(held.dtype)
        copy = pltpu.make_async_copy(held, out_ref.at[:, begin:], sem)
        copy.start()
        copy.wait()

    return pl.pallas_call(
        kernel,
        in_specs=[hbm] + [whole] * 5,
        out_specs=hbm,
        out_shape=jax.ShapeDtypeStruct(done.shape, jnp.bfloat16),
        scratch_shapes=[pltpu.VMEM((TILE, rows), jnp.bfloat16), pltpu.SemaphoreType.DMA],
        input_output_aliases={0: 0},
        compiler_params=params(16),
    )(done, early, up, down, late, far)


def add(*parts):
    total = parts[0].astype(jnp.float32)
    for part in parts[1:]:
        total = total + part.astype(jnp.float32)
    return total


def on_device(amplitudes, plus, minus, cd_irrep, ab_irrep):
    rows = amplitudes.shape[0]
    me, mine = (lax.axis_index(name).astype(jnp.int32) for name in ("xl", "z"))
    fixed, turned = jnp.stack([me, jnp.zeros_like(me)]), jnp.stack([me, mine])
    n_z = plus.shape[1] // PAIR
    half = n_z // 2
    swap = functools.partial(lax.ppermute, axis_name="xl", perm=[(0, 1), (1, 0)])

    def exchange(packed):
        return lax.all_to_all(packed, "row", split_axis=0, concat_axis=0, tiled=True)

    def scatter(terms):
        return lax.psum_scatter(terms, "z", scatter_dimension=0, tiled=True)

    up = functools.partial(
        lax.ppermute, axis_name="z", perm=[(k, (k + 1) % n_z) for k in range(n_z)]
    )
    down = functools.partial(
        lax.ppermute, axis_name="z", perm=[((k + 1) % n_z, k) for k in range(n_z)]
    )

    def send(*pair):
        pair = lax.optimization_barrier(tuple(p.astype(jnp.bfloat16) for p in pair))
        return lax.optimization_barrier((up(pair[0]), down(pair[1])))

    def set_out(terms):
        first = terms(half)
        return send(add(*[t[:1] for t in first]), add(*[t[1:] for t in first]))

    def go_on(terms, step, goes_up, goes_down):
        if step == 1:
            goes_up = jnp.pad(goes_up, ((0, 1), (0, 0), (0, 0)))
            goes_down = jnp.pad(goes_down, ((1, 0), (0, 0), (0, 0)))
        return send(
            add(goes_up, *terms(half - step)), add(goes_down, *terms(half + step))
        )

    def product(place, received, begin, first, n_i, slots):
        return ladder(
            place,
            lists,
            amplitudes,
            received,
            weights,
            begin,
            first,
            n_i,
            n_z,
            1,
            slots,
        )

    rest = rows - FIRST
    packed0 = pack(amplitudes, 0, FIRST)
    received0 = exchange(packed0)
    packed0, later = lax.optimization_barrier((packed0, amplitudes))
    packed1 = pack(later, FIRST, rest)
    packed0, first_plus = lax.optimization_barrier((packed0, plus))
    lists, weights = match(cd_irrep, ab_irrep, first_plus, minus)
    received0, packed1, weights = lax.optimization_barrier((received0, packed1, weights))
    received1 = exchange(packed1)
    (terms0,) = product(fixed, received0, 0, 0, FIRST - UNIT, N_X)
    sum0 = scatter(terms0)
    received0, _ = lax.optimization_barrier((received0, terms0))
    near0, far0 = product(turned, received0, 0, FIRST - UNIT, UNIT, 0)
    far0 = swap(far0)
    received1, _ = lax.optimization_barrier((received1, near0))
    near1, far1 = product(turned, received1, FIRST, 0, UNIT, 0)
    far1 = swap(far1)
    received1, _ = lax.optimization_barrier((received1, near1))
    (terms1,) = product(turned, received1, FIRST, UNIT, rest - UNIT, N_X)

    def late(k):
        return (terms1[k],)

    def early(k):
        return [jnp.concatenate(pair, 0) for pair in ((near0[k], near1[k]), (far0[k], far1[k]))]

    late_ring = set_out(late)
    late_ring, far0, far1 = lax.optimization_barrier((late_ring, far0, far1))
    early_ring = set_out(early)
    for step in range(1, half):
        late_ring = go_on(late, step, *late_ring)
        early_ring = go_on(early, step, *early_ring)
    late_sum = add(terms1[0], *late_ring)
    far_late = swap(late_sum[1].astype(jnp.bfloat16))
    done = finish_first(sum0, swap(sum0[0, 1]))
    return finish_last(
        done, add(*early(0)).reshape(-1, TILE), *early_ring, late_sum[0], far_late
    )


def solution(mesh):
    rows, cols = mesh.shape["row"], mesh.shape["col"]
    fine = Mesh(mesh.devices.reshape(rows, cols // N_X, N_X), ("row", "z", "xl"))
    col = ("z", "xl")
    return jax.shard_map(
        on_device,
        mesh=fine,
        in_specs=(P("row", None, col), P(col, None), P(col, None), P(col), P()),
        out_specs=P(col, "row"),
        check_vma=False,
    )
```

```python
import functools

import jax
import jax.numpy as jnp
from jax import lax
from jax.experimental import pallas as pl
from jax.experimental.pallas import tpu as pltpu
from jax.sharding import Mesh
from jax.sharding import PartitionSpec as P

TILE = 128
N_X = 2
PAIR = N_X * TILE
N_S = 4
N_IRREP = 4
BUNDLE = 4
AHEAD = 2
FIRST = 8
UNIT = 2


def params(mib=60):
    return pltpu.CompilerParams(vmem_limit_bytes=mib * 2**20)


def digits(count, last, middle):
    row = lax.broadcasted_iota(jnp.int32, (count, 1), 0)

    def over(value, size):
        return ((value.astype(jnp.float32) + 0.5) * (1.0 / size)).astype(jnp.int32)

    upper = over(row, last)
    top = over(upper, middle)
    return top, upper - top * middle, row - upper * last


def send_order(rows, first, n_i):
    s, jl, i = digits(N_S * n_i * rows, rows, n_i)
    return (i * N_S + s) * rows + first + jl


def receive_order(rows, count, first, n_i):
    i, s, jl = digits(n_i * N_S * rows, rows, N_S)
    return (s * count + first + i) * rows + jl


def pack_kernel(first, n_i, amp_ref, out_ref, held, sent, in_sem, out_sem):
    rows, occ, width = amp_ref.shape
    steps, per = sent.shape[:2]
    wide = occ // steps
    loads = [
        pltpu.make_async_copy(amp_ref.at[:, q * wide : (q + 1) * wide, :], held.at[q], in_sem.at[q])
        for q in range(steps)
    ]
    stores = [
        pltpu.make_async_copy(sent.at[q], out_ref.at[q * per : (q + 1) * per, :], out_sem.at[q])
        for q in range(steps)
    ]
    for copy in loads[:AHEAD]:
        copy.start()
    order = picker(send_order(rows, first, n_i), rows * wide)
    for q in range(steps):
        loads[q].wait()
        if q + AHEAD < steps:
            loads[q + AHEAD].start()
        block = held[q].reshape(rows * wide, width)
        sent[q] = jnp.dot(order, block, preferred_element_type=jnp.float32).astype(sent.dtype)
        stores[q].start()
    for copy in stores:
        copy.wait()


def pack(amplitudes, first, n_i):
    rows, occ, width = amplitudes.shape
    wide = N_S * rows
    steps = occ // wide
    per = N_S * n_i * rows
    hbm = pl.BlockSpec(memory_space=pl.ANY)
    return pl.pallas_call(
        functools.partial(pack_kernel, first, n_i),
        in_specs=[hbm],
        out_specs=hbm,
        out_shape=jax.ShapeDtypeStruct((steps * per, width), jnp.bfloat16),
        scratch_shapes=[
            pltpu.VMEM((steps, rows, wide, width), jnp.bfloat16),
            pltpu.VMEM((steps, per, width), jnp.bfloat16),
            pltpu.SemaphoreType.DMA((steps,)),
            pltpu.SemaphoreType.DMA((steps,)),
        ],
        compiler_params=params(),
        cost_estimate=pl.CostEstimate(
            flops=0, bytes_accessed=4 * rows * occ * width, transcendentals=0
        ),
    )(amplitudes)


def picker(places, width):
    lanes = lax.broadcasted_iota(jnp.int32, (places.shape[0], width), 1)
    return jnp.where(lanes == places, 1.0, 0.0).astype(jnp.bfloat16)

def match_kernel(cd_ref, ab_ref, plus_ref, minus_ref, lists, out_ref, held, packed, in_sem, out_sem):
    kt = cd_ref.shape[0]
    tiles = ab_ref.shape[0]
    loads = [
        pltpu.make_async_copy(plus_ref, held.at[0], in_sem.at[0]),
        pltpu.make_async_copy(minus_ref, held.at[1], in_sem.at[1]),
    ]
    for copy in loads:
        copy.start()
    there = 2 * N_IRREP
    first_step = there + 2 * kt + 2

    def of_irrep(g, carry):
        begin, step, block = carry

        def tile_of(p, n):
            same = cd_ref[p] == g

            @pl.when(same)
            def _():
                lists[there + p] = begin + n
                lists[there + kt + begin + n] = p

            return n + same.astype(jnp.int32)

        n = lax.fori_loop(0, kt, tile_of, 0)
        lists[g] = n
        lists[N_IRREP + g] = begin

        def target(q, carry):
            step, waiting, block = carry
            same = ab_ref[q] == g
            alone = same & (waiting < 0)
            second = same & (waiting >= 0)

            @pl.when(alone)
            def _():
                for k, value in enumerate((g, q, q, block)):
                    lists[first_step + 4 * step + k] = value

            @pl.when(second)
            def _():
                lists[first_step + 4 * step + 2] = q

            return (
                jnp.where(second, step + 1, step),
                jnp.where(same, jnp.where(second, -1, q), waiting),
                jnp.where(alone, block + n, block),
            )

        step, waiting, block = lax.fori_loop(0, tiles, target, (step, -1, block))
        return begin + n, jnp.where(waiting >= 0, step + 1, step), block

    _, steps, blocks = lax.fori_loop(0, N_IRREP, of_irrep, (0, 0, 0))
    bundles = (blocks + BUNDLE - 1) // BUNDLE
    lists[first_step - 2] = bundles
    lists[first_step - 1] = steps
    for copy in loads:
        copy.wait()

    @pl.loop(0, steps)
    def _(step):
        g, a, b, block = (lists[first_step + 4 * step + k] for k in range(4))
        begin = lists[N_IRREP + g]

        @pl.loop(0, lists[g])
        def _(k):
            p = pl.ds(pl.multiple_of(lists[there + kt + begin + k] * TILE, TILE), TILE)
            for half in range(2):
                for w, q in enumerate((a, b)):
                    packed[block + k, half * TILE : (half + 1) * TILE, w * TILE : (w + 1) * TILE] = (
                        held[half, p, pl.ds(pl.multiple_of(q * TILE, TILE), TILE)]
                    )

    def store(k):
        where = pl.ds(k * BUNDLE, BUNDLE)
        return pltpu.make_async_copy(packed.at[where], out_ref.at[where], out_sem.at[k])

    @pl.loop(0, bundles)
    def _(k):
        store(k).start()

    @pl.loop(0, bundles)
    def _(k):
        store(k).wait()


def match(cd_irrep, ab_irrep, plus, minus):
    width, slab = plus.shape
    kt, tiles = width // TILE, slab // TILE
    steps = (tiles + N_IRREP) // 2
    smem = pl.BlockSpec(memory_space=pltpu.SMEM)
    hbm = pl.BlockSpec(memory_space=pl.ANY)
    blocks = (tiles + 1) // N_X * kt
    shape = (blocks, PAIR, PAIR)
    return pl.pallas_call(
        match_kernel,
        in_specs=[smem, smem, hbm, hbm],
        out_specs=[smem, hbm],
        out_shape=[
            jax.ShapeDtypeStruct((2 * N_IRREP + 2 * kt + 2 + 4 * steps,), jnp.int32),
            jax.ShapeDtypeStruct(shape, jnp.bfloat16),
        ],
        scratch_shapes=[
            pltpu.VMEM((2, width, slab), jnp.bfloat16),
            pltpu.VMEM(shape, jnp.bfloat16),
            pltpu.SemaphoreType.DMA((2,)),
            pltpu.SemaphoreType.DMA((blocks // BUNDLE,)),
        ],
        compiler_params=params(),
        cost_estimate=pl.CostEstimate(
            flops=0, bytes_accessed=8 * width * slab, transcendentals=0
        ),
    )(cd_irrep, ab_irrep, plus, minus)


def ladder_kernel(begin_i, first, me_ref, lists, amp_ref, got_ref, weight_ref, *refs):
    n_out = len(refs) - 8
    out_refs = refs[:n_out]
    own, got, weights, both, staged, load_sem, weight_sem, out_sem = refs[n_out:]
    n_i, occ, width = own.shape
    kt = width // TILE
    tiles, per = staged.shape[:2]
    rows = n_i * occ
    me = me_ref[0]
    there = 2 * N_IRREP
    first_step = there + 2 * kt + 2
    bundles, steps = lists[first_step - 2], lists[first_step - 1]
    loads = [
        pltpu.make_async_copy(amp_ref.at[begin_i + first : begin_i + first + n_i], own, load_sem.at[0]),
        pltpu.make_async_copy(got_ref, got, load_sem.at[1]),
    ]
    for copy in loads:
        copy.start()

    def weights_copy(k):
        where = pl.ds(k * BUNDLE, BUNDLE)
        return pltpu.make_async_copy(weight_ref.at[where], weights.at[where], weight_sem.at[k])

    @pl.loop(0, bundles)
    def _(k):
        weights_copy(k).start()

    local = amp_ref.shape[0]
    piece = N_S * local
    span = n_i * piece
    received = got.shape[0] * piece // occ
    order = picker(receive_order(local, received // piece, first, n_i), received)
    for copy in loads:
        copy.wait()
    for q in range(occ // piece):
        other = jnp.dot(
            order, got[q * received : (q + 1) * received, :], preferred_element_type=jnp.float32
        )
        mine = own[:, q * piece : (q + 1) * piece, :].reshape(span, width).astype(jnp.float32)
        for half, value in enumerate((mine + other, mine - other)):
            value = value.astype(jnp.bfloat16).reshape(n_i, piece, width)
            for p in range(kt):
                lanes = pl.ds(pl.multiple_of(lists[there + p] * PAIR + half * TILE, TILE), TILE)
                both[:, q * piece : (q + 1) * piece, lanes] = value[:, :, p * TILE : (p + 1) * TILE]

    def out_copy(q, dst):
        return pltpu.make_async_copy(staged.at[q], dst, out_sem)

    def start(q):
        z, w = (q // N_X - me_ref[1]) & (tiles // N_X - 1), (q % N_X) ^ me
        if n_out == 1:
            out_copy(q, out_refs[0].at[z, pl.ds(w * per, per)]).start()
        else:
            for k in range(N_X):

                @pl.when(w == k)
                def _():
                    out_copy(q, out_refs[k].at[z]).start()

    @pl.loop(0, bundles)
    def _(k):
        weights_copy(k).wait()

    @pl.loop(0, steps)
    def _(step):
        g, a, b, block = (lists[first_step + 4 * step + k] for k in range(4))
        n, begin = lists[g], lists[N_IRREP + g]

        @pl.when(n == 0)
        def _():
            zero = jnp.zeros(staged.shape[1:], staged.dtype)
            staged[a] = zero
            staged[b] = zero

        for size in range(1, kt + 1):

            @pl.when(n == size)
            def _():
                lanes = pl.ds(pl.multiple_of(begin * PAIR, PAIR), size * PAIR)
                left = both[:, :, lanes].reshape(rows, size * PAIR)
                right = weights[pl.ds(block, size)].reshape(size * PAIR, PAIR)
                term = 0.5 * jnp.dot(left, right, preferred_element_type=jnp.float32)
                staged[a] = term[:, :TILE].astype(staged.dtype).reshape(staged.shape[1:])
                staged[b] = term[:, TILE:].astype(staged.dtype).reshape(staged.shape[1:])

        start(a)

        @pl.when(b != a)
        def _():
            start(b)

    pltpu.make_async_copy(staged, staged, out_sem).wait()


def ladder(place, lists, amplitudes, received, weights, begin, first, n_i, n_z, per, slots):
    _, occ, width = amplitudes.shape
    rows = n_i * occ
    tiles = n_z * N_X
    blocks = weights.shape[0]
    if slots:
        shapes = [(n_z, slots, rows // per, TILE)]
    else:
        shapes = [(n_z, per, rows // per, TILE)] * N_X
    smem = pl.BlockSpec(memory_space=pltpu.SMEM)
    hbm = pl.BlockSpec(memory_space=pl.ANY)
    dma = pltpu.SemaphoreType.DMA
    bf16 = jnp.bfloat16
    return pl.pallas_call(
        functools.partial(ladder_kernel, begin, first),
        in_specs=[smem, smem, hbm, hbm, hbm],
        out_specs=[hbm] * len(shapes),
        out_shape=[jax.ShapeDtypeStruct(s, bf16) for s in shapes],
        scratch_shapes=[
            pltpu.VMEM((n_i, occ, width), bf16),
            pltpu.VMEM(received.shape, bf16),
            pltpu.VMEM(weights.shape, bf16),
            pltpu.VMEM((n_i, occ, 2 * width), bf16),
            pltpu.VMEM((tiles, per, rows // per, TILE), bf16),
            dma((2,)),
            dma((blocks // BUNDLE,)),
            dma,
        ],
        compiler_params=params(50),
        cost_estimate=pl.CostEstimate(
            flops=0, bytes_accessed=8 * rows * (width + n_z * TILE), transcendentals=0
        ),
    )(place, lists, amplitudes, received, weights)


def finish_kernel(near, far, *refs):
    out_ref = refs[-1]
    total = near[...].astype(jnp.float32).reshape(-1, TILE) + far[...].astype(jnp.float32)
    if len(refs) > 1:
        early = refs[0][...].astype(jnp.float32).reshape(-1, TILE)
        total = jnp.concatenate([early, total], 0)
    out_ref[...] = total.T.astype(out_ref.dtype)


def slots(ref, count, k):
    return pl.BlockSpec((1, count) + ref.shape[2:], lambda g: (0, k, 0, 0))


def finish_first(near, far):
    rows = far.shape[0]
    return pl.pallas_call(
        finish_kernel,
        grid=(1,),
        in_specs=[slots(near, 1, 0), pl.BlockSpec(far.shape, lambda g: (0, 0))],
        out_specs=pl.BlockSpec((TILE, rows), lambda g: (0, 0)),
        out_shape=jax.ShapeDtypeStruct((TILE, 2 * rows), jnp.bfloat16),
        compiler_params=params(57),
    )(near, far)


def finish_last(done, early, up, down, late, far):
    whole = pl.BlockSpec(memory_space=pltpu.VMEM)
    hbm = pl.BlockSpec(memory_space=pl.ANY)
    rows = early.shape[0] + late.shape[0]
    begin = done.shape[1] - rows

    def kernel(done_ref, early_ref, up_ref, down_ref, late_ref, far_ref, out_ref, held, sem):
        first = early_ref[...]
        for ref in (up_ref, down_ref):
            first = first + ref[...].astype(jnp.float32).reshape(-1, TILE)
        last = late_ref[...] + far_ref[...].astype(jnp.float32)
        held[...] = jnp.concatenate([first, last], 0).T.astype(held.dtype)
        copy = pltpu.make_async_copy(held, out_ref.at[:, begin:], sem)
        copy.start()
        copy.wait()

    return pl.pallas_call(
        kernel,
        in_specs=[hbm] + [whole] * 5,
        out_specs=hbm,
        out_shape=jax.ShapeDtypeStruct(done.shape, jnp.bfloat16),
        scratch_shapes=[pltpu.VMEM((TILE, rows), jnp.bfloat16), pltpu.SemaphoreType.DMA],
        input_output_aliases={0: 0},
        compiler_params=params(16),
    )(done, early, up, down, late, far)


def add(*parts):
    total = parts[0].astype(jnp.float32)
    for part in parts[1:]:
        total = total + part.astype(jnp.float32)
    return total


def on_device(amplitudes, plus, minus, cd_irrep, ab_irrep):
    rows = amplitudes.shape[0]
    me, mine = (lax.axis_index(name).astype(jnp.int32) for name in ("xl", "z"))
    fixed, turned = jnp.stack([me, jnp.zeros_like(me)]), jnp.stack([me, mine])
    n_z = plus.shape[1] // PAIR
    half = n_z // 2
    swap = functools.partial(lax.ppermute, axis_name="xl", perm=[(0, 1), (1, 0)])

    def exchange(packed):
        return lax.all_to_all(packed, "row", split_axis=0, concat_axis=0, tiled=True)

    def scatter(terms):
        return lax.psum_scatter(terms, "z", scatter_dimension=0, tiled=True)

    up = functools.partial(
        lax.ppermute, axis_name="z", perm=[(k, (k + 1) % n_z) for k in range(n_z)]
    )
    down = functools.partial(
        lax.ppermute, axis_name="z", perm=[((k + 1) % n_z, k) for k in range(n_z)]
    )

    def send(*pair):
        pair = lax.optimization_barrier(tuple(p.astype(jnp.bfloat16) for p in pair))
        return lax.optimization_barrier((up(pair[0]), down(pair[1])))

    def set_out(terms):
        first = terms(half)
        return send(add(*[t[:1] for t in first]), add(*[t[1:] for t in first]))

    def go_on(terms, step, goes_up, goes_down):
        if step == 1:
            goes_up = jnp.pad(goes_up, ((0, 1), (0, 0), (0, 0)))
            goes_down = jnp.pad(goes_down, ((1, 0), (0, 0), (0, 0)))
        return send(
            add(goes_up, *terms(half - step)), add(goes_down, *terms(half + step))
        )

    def product(place, received, begin, first, n_i, slots):
        return ladder(
            place,
            lists,
            amplitudes,
            received,
            weights,
            begin,
            first,
            n_i,
            n_z,
            1,
            slots,
        )

    rest = rows - FIRST
    packed0 = pack(amplitudes, 0, FIRST)
    received0 = exchange(packed0)
    packed0, later = lax.optimization_barrier((packed0, amplitudes))
    packed1 = pack(later, FIRST, rest)
    packed0, first_plus = lax.optimization_barrier((packed0, plus))
    lists, weights = match(cd_irrep, ab_irrep, first_plus, minus)
    received0, packed1, weights = lax.optimization_barrier((received0, packed1, weights))
    received1 = exchange(packed1)
    (terms0,) = product(fixed, received0, 0, 0, FIRST - UNIT, N_X)
    sum0 = scatter(terms0)
    received0, _ = lax.optimization_barrier((received0, terms0))
    near0, far0 = product(turned, received0, 0, FIRST - UNIT, UNIT, 0)
    far0 = swap(far0)
    received1, _ = lax.optimization_barrier((received1, near0))
    near1, far1 = product(turned, received1, FIRST, 0, UNIT, 0)
    far1 = swap(far1)
    received1, _ = lax.optimization_barrier((received1, near1))
    (terms1,) = product(turned, received1, FIRST, UNIT, rest - UNIT, N_X)

    def late(k):
        return (terms1[k],)

    def early(k):
        return [jnp.concatenate(pair, 0) for pair in ((near0[k], near1[k]), (far0[k], far1[k]))]

    late_ring = set_out(late)
    late_ring, far0, far1 = lax.optimization_barrier((late_ring, far0, far1))
    early_ring = set_out(early)
    for step in range(1, half):
        late_ring = go_on(late, step, *late_ring)
        if step == half - 1:
            last0 = swap(sum0[0, 1])
            early_ring, late_ring, last0 = lax.optimization_barrier(
                (early_ring, late_ring, last0)
            )
        early_ring = go_on(early, step, *early_ring)
    late_sum = add(terms1[0], *late_ring)
    far_late = swap(late_sum[1].astype(jnp.bfloat16))
    done = finish_first(sum0, last0)
    return finish_last(
        done, add(*early(0)).reshape(-1, TILE), *early_ring, late_sum[0], far_late
    )


def solution(mesh):
    rows, cols = mesh.shape["row"], mesh.shape["col"]
    fine = Mesh(mesh.devices.reshape(rows, cols // N_X, N_X), ("row", "z", "xl"))
    col = ("z", "xl")
    return jax.shard_map(
        on_device,
        mesh=fine,
        in_specs=(P("row", None, col), P(col, None), P(col, None), P(col), P()),
        out_specs=P(col, "row"),
        check_vma=False,
    )
```

```python
import functools

import jax
import jax.numpy as jnp
from jax import lax
from jax.experimental import pallas as pl
from jax.experimental.pallas import tpu as pltpu
from jax.sharding import Mesh
from jax.sharding import PartitionSpec as P

TILE = 128
N_X = 2
PAIR = N_X * TILE
N_S = 4
N_IRREP = 4
BUNDLE = 4
AHEAD = 2
FIRST = 8
UNIT = 2


def params(mib=60):
    return pltpu.CompilerParams(vmem_limit_bytes=mib * 2**20)


def digits(count, last, middle):
    row = lax.broadcasted_iota(jnp.int32, (count, 1), 0)

    def over(value, size):
        return ((value.astype(jnp.float32) + 0.5) * (1.0 / size)).astype(jnp.int32)

    upper = over(row, last)
    top = over(upper, middle)
    return top, upper - top * middle, row - upper * last


def send_order(rows, first, n_i):
    s, jl, i = digits(N_S * n_i * rows, rows, n_i)
    return (i * N_S + s) * rows + first + jl


def receive_order(rows, count, first, n_i):
    i, s, jl = digits(n_i * N_S * rows, rows, N_S)
    return (s * count + first + i) * rows + jl


def pack_kernel(first, n_i, amp_ref, out_ref, held, sent, in_sem, out_sem):
    rows, occ, width = amp_ref.shape
    steps, per = sent.shape[:2]
    wide = occ // steps
    loads = [
        pltpu.make_async_copy(amp_ref.at[:, q * wide : (q + 1) * wide, :], held.at[q], in_sem.at[q])
        for q in range(steps)
    ]
    stores = [
        pltpu.make_async_copy(sent.at[q], out_ref.at[q * per : (q + 1) * per, :], out_sem.at[q])
        for q in range(steps)
    ]
    for copy in loads[:AHEAD]:
        copy.start()
    order = picker(send_order(rows, first, n_i), rows * wide)
    for q in range(steps):
        loads[q].wait()
        if q + AHEAD < steps:
            loads[q + AHEAD].start()
        block = held[q].reshape(rows * wide, width)
        sent[q] = jnp.dot(order, block, preferred_element_type=jnp.float32).astype(sent.dtype)
        stores[q].start()
    for copy in stores:
        copy.wait()


def pack(amplitudes, first, n_i):
    rows, occ, width = amplitudes.shape
    wide = N_S * rows
    steps = occ // wide
    per = N_S * n_i * rows
    hbm = pl.BlockSpec(memory_space=pl.ANY)
    return pl.pallas_call(
        functools.partial(pack_kernel, first, n_i),
        in_specs=[hbm],
        out_specs=hbm,
        out_shape=jax.ShapeDtypeStruct((steps * per, width), jnp.bfloat16),
        scratch_shapes=[
            pltpu.VMEM((steps, rows, wide, width), jnp.bfloat16),
            pltpu.VMEM((steps, per, width), jnp.bfloat16),
            pltpu.SemaphoreType.DMA((steps,)),
            pltpu.SemaphoreType.DMA((steps,)),
        ],
        compiler_params=params(),
        cost_estimate=pl.CostEstimate(
            flops=0, bytes_accessed=4 * rows * occ * width, transcendentals=0
        ),
    )(amplitudes)


def picker(places, width):
    lanes = lax.broadcasted_iota(jnp.int32, (places.shape[0], width), 1)
    return jnp.where(lanes == places, 1.0, 0.0).astype(jnp.bfloat16)

def match_kernel(cd_ref, ab_ref, plus_ref, minus_ref, lists, out_ref, held, packed, in_sem, out_sem):
    kt = cd_ref.shape[0]
    tiles = ab_ref.shape[0]
    loads = [
        pltpu.make_async_copy(plus_ref, held.at[0], in_sem.at[0]),
        pltpu.make_async_copy(minus_ref, held.at[1], in_sem.at[1]),
    ]
    for copy in loads:
        copy.start()
    there = 2 * N_IRREP
    first_step = there + 2 * kt + 2

    def of_irrep(g, carry):
        begin, step, block = carry

        def tile_of(p, n):
            same = cd_ref[p] == g

            @pl.when(same)
            def _():
                lists[there + p] = begin + n
                lists[there + kt + begin + n] = p

            return n + same.astype(jnp.int32)

        n = lax.fori_loop(0, kt, tile_of, 0)
        lists[g] = n
        lists[N_IRREP + g] = begin

        def target(q, carry):
            step, waiting, block = carry
            same = ab_ref[q] == g
            alone = same & (waiting < 0)
            second = same & (waiting >= 0)

            @pl.when(alone)
            def _():
                for k, value in enumerate((g, q, q, block)):
                    lists[first_step + 4 * step + k] = value

            @pl.when(second)
            def _():
                lists[first_step + 4 * step + 2] = q

            return (
                jnp.where(second, step + 1, step),
                jnp.where(same, jnp.where(second, -1, q), waiting),
                jnp.where(alone, block + n, block),
            )

        step, waiting, block = lax.fori_loop(0, tiles, target, (step, -1, block))
        return begin + n, jnp.where(waiting >= 0, step + 1, step), block

    _, steps, blocks = lax.fori_loop(0, N_IRREP, of_irrep, (0, 0, 0))
    bundles = (blocks + BUNDLE - 1) // BUNDLE
    lists[first_step - 2] = bundles
    lists[first_step - 1] = steps
    for copy in loads:
        copy.wait()

    @pl.loop(0, steps)
    def _(step):
        g, a, b, block = (lists[first_step + 4 * step + k] for k in range(4))
        begin = lists[N_IRREP + g]

        @pl.loop(0, lists[g])
        def _(k):
            p = pl.ds(pl.multiple_of(lists[there + kt + begin + k] * TILE, TILE), TILE)
            for half in range(2):
                for w, q in enumerate((a, b)):
                    packed[block + k, half * TILE : (half + 1) * TILE, w * TILE : (w + 1) * TILE] = (
                        held[half, p, pl.ds(pl.multiple_of(q * TILE, TILE), TILE)]
                    )

    def store(k):
        where = pl.ds(k * BUNDLE, BUNDLE)
        return pltpu.make_async_copy(packed.at[where], out_ref.at[where], out_sem.at[k])

    @pl.loop(0, bundles)
    def _(k):
        store(k).start()

    @pl.loop(0, bundles)
    def _(k):
        store(k).wait()


def match(cd_irrep, ab_irrep, plus, minus):
    width, slab = plus.shape
    kt, tiles = width // TILE, slab // TILE
    steps = (tiles + N_IRREP) // 2
    smem = pl.BlockSpec(memory_space=pltpu.SMEM)
    hbm = pl.BlockSpec(memory_space=pl.ANY)
    blocks = (tiles + 1) // N_X * kt
    shape = (blocks, PAIR, PAIR)
    return pl.pallas_call(
        match_kernel,
        in_specs=[smem, smem, hbm, hbm],
        out_specs=[smem, hbm],
        out_shape=[
            jax.ShapeDtypeStruct((2 * N_IRREP + 2 * kt + 2 + 4 * steps,), jnp.int32),
            jax.ShapeDtypeStruct(shape, jnp.bfloat16),
        ],
        scratch_shapes=[
            pltpu.VMEM((2, width, slab), jnp.bfloat16),
            pltpu.VMEM(shape, jnp.bfloat16),
            pltpu.SemaphoreType.DMA((2,)),
            pltpu.SemaphoreType.DMA((blocks // BUNDLE,)),
        ],
        compiler_params=params(),
        cost_estimate=pl.CostEstimate(
            flops=0, bytes_accessed=8 * width * slab, transcendentals=0
        ),
    )(cd_irrep, ab_irrep, plus, minus)


def ladder_kernel(begin_i, first, me_ref, lists, amp_ref, got_ref, weight_ref, *refs):
    n_out = len(refs) - 8
    out_refs = refs[:n_out]
    own, got, weights, both, staged, load_sem, weight_sem, out_sem = refs[n_out:]
    n_i, occ, width = own.shape
    kt = width // TILE
    tiles, per = staged.shape[:2]
    rows = n_i * occ
    me = me_ref[0]
    there = 2 * N_IRREP
    first_step = there + 2 * kt + 2
    bundles, steps = lists[first_step - 2], lists[first_step - 1]
    loads = [
        pltpu.make_async_copy(amp_ref.at[begin_i + first : begin_i + first + n_i], own, load_sem.at[0]),
        pltpu.make_async_copy(got_ref, got, load_sem.at[1]),
    ]
    for copy in loads:
        copy.start()

    def weights_copy(k):
        where = pl.ds(k * BUNDLE, BUNDLE)
        return pltpu.make_async_copy(weight_ref.at[where], weights.at[where], weight_sem.at[k])

    @pl.loop(0, bundles)
    def _(k):
        weights_copy(k).start()

    local = amp_ref.shape[0]
    piece = N_S * local
    span = n_i * piece
    received = got.shape[0] * piece // occ
    order = picker(receive_order(local, received // piece, first, n_i), received)
    for copy in loads:
        copy.wait()
    for q in range(occ // piece):
        other = jnp.dot(
            order, got[q * received : (q + 1) * received, :], preferred_element_type=jnp.float32
        )
        mine = own[:, q * piece : (q + 1) * piece, :].reshape(span, width).astype(jnp.float32)
        for half, value in enumerate((mine + other, mine - other)):
            value = value.astype(jnp.bfloat16).reshape(n_i, piece, width)
            for p in range(kt):
                lanes = pl.ds(pl.multiple_of(lists[there + p] * PAIR + half * TILE, TILE), TILE)
                both[:, q * piece : (q + 1) * piece, lanes] = value[:, :, p * TILE : (p + 1) * TILE]

    def out_copy(q, dst):
        return pltpu.make_async_copy(staged.at[q], dst, out_sem)

    def start(q):
        z, w = (q // N_X - me_ref[1]) & (tiles // N_X - 1), (q % N_X) ^ me
        if n_out == 1:
            out_copy(q, out_refs[0].at[z, pl.ds(w * per, per)]).start()
        else:
            for k in range(N_X):

                @pl.when(w == k)
                def _():
                    out_copy(q, out_refs[k].at[z]).start()

    @pl.loop(0, bundles)
    def _(k):
        weights_copy(k).wait()

    @pl.loop(0, steps)
    def _(step):
        g, a, b, block = (lists[first_step + 4 * step + k] for k in range(4))
        n, begin = lists[g], lists[N_IRREP + g]

        @pl.when(n == 0)
        def _():
            zero = jnp.zeros(staged.shape[1:], staged.dtype)
            staged[a] = zero
            staged[b] = zero

        for size in range(1, kt + 1):

            @pl.when(n == size)
            def _():
                lanes = pl.ds(pl.multiple_of(begin * PAIR, PAIR), size * PAIR)
                left = both[:, :, lanes].reshape(rows, size * PAIR)
                right = weights[pl.ds(block, size)].reshape(size * PAIR, PAIR)
                term = 0.5 * jnp.dot(left, right, preferred_element_type=jnp.float32)
                staged[a] = term[:, :TILE].astype(staged.dtype).reshape(staged.shape[1:])
                staged[b] = term[:, TILE:].astype(staged.dtype).reshape(staged.shape[1:])

        start(a)

        @pl.when(b != a)
        def _():
            start(b)

    pltpu.make_async_copy(staged, staged, out_sem).wait()


def ladder(place, lists, amplitudes, received, weights, begin, first, n_i, n_z, per, slots):
    _, occ, width = amplitudes.shape
    rows = n_i * occ
    tiles = n_z * N_X
    blocks = weights.shape[0]
    if slots:
        shapes = [(n_z, slots, rows // per, TILE)]
    else:
        shapes = [(n_z, per, rows // per, TILE)] * N_X
    smem = pl.BlockSpec(memory_space=pltpu.SMEM)
    hbm = pl.BlockSpec(memory_space=pl.ANY)
    dma = pltpu.SemaphoreType.DMA
    bf16 = jnp.bfloat16
    return pl.pallas_call(
        functools.partial(ladder_kernel, begin, first),
        in_specs=[smem, smem, hbm, hbm, hbm],
        out_specs=[hbm] * len(shapes),
        out_shape=[jax.ShapeDtypeStruct(s, bf16) for s in shapes],
        scratch_shapes=[
            pltpu.VMEM((n_i, occ, width), bf16),
            pltpu.VMEM(received.shape, bf16),
            pltpu.VMEM(weights.shape, bf16),
            pltpu.VMEM((n_i, occ, 2 * width), bf16),
            pltpu.VMEM((tiles, per, rows // per, TILE), bf16),
            dma((2,)),
            dma((blocks // BUNDLE,)),
            dma,
        ],
        compiler_params=params(50),
        cost_estimate=pl.CostEstimate(
            flops=0, bytes_accessed=8 * rows * (width + n_z * TILE), transcendentals=0
        ),
    )(place, lists, amplitudes, received, weights)


def finish_kernel(near, far, *refs):
    out_ref = refs[-1]
    total = near[...].astype(jnp.float32).reshape(-1, TILE) + far[...].astype(jnp.float32)
    if len(refs) > 1:
        early = refs[0][...].astype(jnp.float32).reshape(-1, TILE)
        total = jnp.concatenate([early, total], 0)
    out_ref[...] = total.T.astype(out_ref.dtype)


def slots(ref, count, k):
    return pl.BlockSpec((1, count) + ref.shape[2:], lambda g: (0, k, 0, 0))


def finish_first(near, far):
    rows = far.shape[0]
    return pl.pallas_call(
        finish_kernel,
        grid=(1,),
        in_specs=[slots(near, 1, 0), pl.BlockSpec(far.shape, lambda g: (0, 0))],
        out_specs=pl.BlockSpec((TILE, rows), lambda g: (0, 0)),
        out_shape=jax.ShapeDtypeStruct((TILE, 2 * rows), jnp.bfloat16),
        compiler_params=params(57),
    )(near, far)


def finish_last(done, early, up, down, late, far):
    whole = pl.BlockSpec(memory_space=pltpu.VMEM)
    hbm = pl.BlockSpec(memory_space=pl.ANY)
    rows = early.shape[0] + late.shape[0]
    begin = done.shape[1] - rows

    def kernel(done_ref, early_ref, up_ref, down_ref, late_ref, far_ref, out_ref, held, sem):
        first = early_ref[...]
        for ref in (up_ref, down_ref):
            first = first + ref[...].astype(jnp.float32).reshape(-1, TILE)
        last = late_ref[...] + far_ref[...].astype(jnp.float32)
        held[...] = jnp.concatenate([first, last], 0).T.astype(held.dtype)
        copy = pltpu.make_async_copy(held, out_ref.at[:, begin:], sem)
        copy.start()
        copy.wait()

    return pl.pallas_call(
        kernel,
        in_specs=[hbm] + [whole] * 5,
        out_specs=hbm,
        out_shape=jax.ShapeDtypeStruct(done.shape, jnp.bfloat16),
        scratch_shapes=[pltpu.VMEM((TILE, rows), jnp.bfloat16), pltpu.SemaphoreType.DMA],
        input_output_aliases={0: 0},
        compiler_params=params(16),
    )(done, early, up, down, late, far)


def add(*parts):
    total = parts[0].astype(jnp.float32)
    for part in parts[1:]:
        total = total + part.astype(jnp.float32)
    return total


def on_device(amplitudes, plus, minus, cd_irrep, ab_irrep):
    rows = amplitudes.shape[0]
    me, mine = (lax.axis_index(name).astype(jnp.int32) for name in ("xl", "z"))
    fixed, turned = jnp.stack([me, jnp.zeros_like(me)]), jnp.stack([me, mine])
    n_z = plus.shape[1] // PAIR
    half = n_z // 2
    swap = functools.partial(lax.ppermute, axis_name="xl", perm=[(0, 1), (1, 0)])

    def exchange(packed):
        return lax.all_to_all(packed, "row", split_axis=0, concat_axis=0, tiled=True)

    def scatter(terms):
        return lax.psum_scatter(terms, "z", scatter_dimension=0, tiled=True)

    up = functools.partial(
        lax.ppermute, axis_name="z", perm=[(k, (k + 1) % n_z) for k in range(n_z)]
    )
    down = functools.partial(
        lax.ppermute, axis_name="z", perm=[((k + 1) % n_z, k) for k in range(n_z)]
    )

    def send(*pair):
        pair = lax.optimization_barrier(tuple(p.astype(jnp.bfloat16) for p in pair))
        return lax.optimization_barrier((up(pair[0]), down(pair[1])))

    def set_out(terms):
        first = terms(half)
        return send(add(*[t[:1] for t in first]), add(*[t[1:] for t in first]))

    def go_on(terms, step, goes_up, goes_down):
        if step == 1:
            goes_up = jnp.pad(goes_up, ((0, 1), (0, 0), (0, 0)))
            goes_down = jnp.pad(goes_down, ((1, 0), (0, 0), (0, 0)))
        return send(
            add(goes_up, *terms(half - step)), add(goes_down, *terms(half + step))
        )

    def product(place, received, begin, first, n_i, slots):
        return ladder(
            place,
            lists,
            amplitudes,
            received,
            weights,
            begin,
            first,
            n_i,
            n_z,
            1,
            slots,
        )

    rest = rows - FIRST
    packed0 = pack(amplitudes, 0, FIRST)
    received0 = exchange(packed0)
    packed0, later = lax.optimization_barrier((packed0, amplitudes))
    packed1 = pack(later, FIRST, rest)
    packed0, first_plus = lax.optimization_barrier((packed0, plus))
    lists, weights = match(cd_irrep, ab_irrep, first_plus, minus)
    received0, packed1, weights = lax.optimization_barrier((received0, packed1, weights))
    received1 = exchange(packed1)
    (terms0,) = product(fixed, received0, 0, 0, FIRST - UNIT, N_X)
    sum0 = scatter(terms0)
    received0, _ = lax.optimization_barrier((received0, terms0))
    near0, far0 = product(turned, received0, 0, FIRST - UNIT, UNIT, 0)
    far0 = swap(far0)
    received1, _ = lax.optimization_barrier((received1, near0))
    (terms1,) = product(turned, received1, FIRST, UNIT, rest - UNIT, N_X)
    received1, _ = lax.optimization_barrier((received1, terms1))
    near1, far1 = product(turned, received1, FIRST, 0, UNIT, 0)
    far1 = swap(far1)

    def late(k):
        return (terms1[k],)

    def early(k):
        return [jnp.concatenate(pair, 0) for pair in ((near0[k], near1[k]), (far0[k], far1[k]))]

    late_ring = go_on(late, 1, *set_out(late))
    late_ring, far0, far1 = lax.optimization_barrier((late_ring, far0, far1))
    early_ring = set_out(early)
    for step in range(2, half):
        late_ring = go_on(late, step, *late_ring)
        if step == half - 1:
            last0 = swap(sum0[0, 1])
            early_ring, last0 = lax.optimization_barrier((early_ring, last0))
        early_ring = go_on(early, step - 1, *early_ring)
    early_ring = go_on(early, half - 1, *early_ring)
    late_sum = add(terms1[0], *late_ring)
    far_late = swap(late_sum[1].astype(jnp.bfloat16))
    done = finish_first(sum0, last0)
    return finish_last(
        done, add(*early(0)).reshape(-1, TILE), *early_ring, late_sum[0], far_late
    )


def solution(mesh):
    rows, cols = mesh.shape["row"], mesh.shape["col"]
    fine = Mesh(mesh.devices.reshape(rows, cols // N_X, N_X), ("row", "z", "xl"))
    col = ("z", "xl")
    return jax.shard_map(
        on_device,
        mesh=fine,
        in_specs=(P("row", None, col), P(col, None), P(col, None), P(col), P()),
        out_specs=P(col, "row"),
        check_vma=False,
    )
```

```python
import functools

import jax
import jax.numpy as jnp
from jax import lax
from jax.experimental import pallas as pl
from jax.experimental.pallas import tpu as pltpu
from jax.sharding import Mesh
from jax.sharding import PartitionSpec as P

TILE = 128
N_X = 2
PAIR = N_X * TILE
N_S = 4
N_IRREP = 4
BUNDLE = 4
AHEAD = 2
FIRST = 8
UNIT = 2


def params(mib=60):
    return pltpu.CompilerParams(vmem_limit_bytes=mib * 2**20)


def digits(count, last, middle):
    row = lax.broadcasted_iota(jnp.int32, (count, 1), 0)

    def over(value, size):
        return ((value.astype(jnp.float32) + 0.5) * (1.0 / size)).astype(jnp.int32)

    upper = over(row, last)
    top = over(upper, middle)
    return top, upper - top * middle, row - upper * last


def send_order(rows, first, n_i):
    s, jl, i = digits(N_S * n_i * rows, rows, n_i)
    return (i * N_S + s) * rows + first + jl


def receive_order(rows, count, first, n_i):
    i, s, jl = digits(n_i * N_S * rows, rows, N_S)
    return (s * count + first + i) * rows + jl


def pack_kernel(first, n_i, amp_ref, out_ref, held, sent, in_sem, out_sem):
    rows, occ, width = amp_ref.shape
    steps, per = sent.shape[:2]
    wide = occ // steps
    loads = [
        pltpu.make_async_copy(amp_ref.at[:, q * wide : (q + 1) * wide, :], held.at[q], in_sem.at[q])
        for q in range(steps)
    ]
    stores = [
        pltpu.make_async_copy(sent.at[q], out_ref.at[q * per : (q + 1) * per, :], out_sem.at[q])
        for q in range(steps)
    ]
    for copy in loads[:AHEAD]:
        copy.start()
    order = picker(send_order(rows, first, n_i), rows * wide)
    for q in range(steps):
        loads[q].wait()
        if q + AHEAD < steps:
            loads[q + AHEAD].start()
        block = held[q].reshape(rows * wide, width)
        sent[q] = jnp.dot(order, block, preferred_element_type=jnp.float32).astype(sent.dtype)
        stores[q].start()
    for copy in stores:
        copy.wait()


def pack(amplitudes, first, n_i):
    rows, occ, width = amplitudes.shape
    wide = N_S * rows
    steps = occ // wide
    per = N_S * n_i * rows
    hbm = pl.BlockSpec(memory_space=pl.ANY)
    return pl.pallas_call(
        functools.partial(pack_kernel, first, n_i),
        in_specs=[hbm],
        out_specs=hbm,
        out_shape=jax.ShapeDtypeStruct((steps * per, width), jnp.bfloat16),
        scratch_shapes=[
            pltpu.VMEM((steps, rows, wide, width), jnp.bfloat16),
            pltpu.VMEM((steps, per, width), jnp.bfloat16),
            pltpu.SemaphoreType.DMA((steps,)),
            pltpu.SemaphoreType.DMA((steps,)),
        ],
        compiler_params=params(),
        cost_estimate=pl.CostEstimate(
            flops=0, bytes_accessed=4 * rows * occ * width, transcendentals=0
        ),
    )(amplitudes)


def picker(places, width):
    lanes = lax.broadcasted_iota(jnp.int32, (places.shape[0], width), 1)
    return jnp.where(lanes == places, 1.0, 0.0).astype(jnp.bfloat16)

def match_kernel(cd_ref, ab_ref, plus_ref, minus_ref, lists, out_ref, held, packed, in_sem, out_sem):
    kt = cd_ref.shape[0]
    tiles = ab_ref.shape[0]
    loads = [
        pltpu.make_async_copy(plus_ref, held.at[0], in_sem.at[0]),
        pltpu.make_async_copy(minus_ref, held.at[1], in_sem.at[1]),
    ]
    for copy in loads:
        copy.start()
    there = 2 * N_IRREP
    first_step = there + 2 * kt + 2

    def of_irrep(g, carry):
        begin, step, block = carry

        def tile_of(p, n):
            same = cd_ref[p] == g

            @pl.when(same)
            def _():
                lists[there + p] = begin + n
                lists[there + kt + begin + n] = p

            return n + same.astype(jnp.int32)

        n = lax.fori_loop(0, kt, tile_of, 0)
        lists[g] = n
        lists[N_IRREP + g] = begin

        def target(q, carry):
            step, waiting, block = carry
            same = ab_ref[q] == g
            alone = same & (waiting < 0)
            second = same & (waiting >= 0)

            @pl.when(alone)
            def _():
                for k, value in enumerate((g, q, q, block)):
                    lists[first_step + 4 * step + k] = value

            @pl.when(second)
            def _():
                lists[first_step + 4 * step + 2] = q

            return (
                jnp.where(second, step + 1, step),
                jnp.where(same, jnp.where(second, -1, q), waiting),
                jnp.where(alone, block + n, block),
            )

        step, waiting, block = lax.fori_loop(0, tiles, target, (step, -1, block))
        return begin + n, jnp.where(waiting >= 0, step + 1, step), block

    _, steps, blocks = lax.fori_loop(0, N_IRREP, of_irrep, (0, 0, 0))
    bundles = (blocks + BUNDLE - 1) // BUNDLE
    lists[first_step - 2] = bundles
    lists[first_step - 1] = steps
    for copy in loads:
        copy.wait()

    @pl.loop(0, steps)
    def _(step):
        g, a, b, block = (lists[first_step + 4 * step + k] for k in range(4))
        begin = lists[N_IRREP + g]

        @pl.loop(0, lists[g])
        def _(k):
            p = pl.ds(pl.multiple_of(lists[there + kt + begin + k] * TILE, TILE), TILE)
            for half in range(2):
                for w, q in enumerate((a, b)):
                    packed[block + k, half * TILE : (half + 1) * TILE, w * TILE : (w + 1) * TILE] = (
                        held[half, p, pl.ds(pl.multiple_of(q * TILE, TILE), TILE)]
                    )

    def store(k):
        where = pl.ds(k * BUNDLE, BUNDLE)
        return pltpu.make_async_copy(packed.at[where], out_ref.at[where], out_sem.at[k])

    @pl.loop(0, bundles)
    def _(k):
        store(k).start()

    @pl.loop(0, bundles)
    def _(k):
        store(k).wait()


def match(cd_irrep, ab_irrep, plus, minus):
    width, slab = plus.shape
    kt, tiles = width // TILE, slab // TILE
    steps = (tiles + N_IRREP) // 2
    smem = pl.BlockSpec(memory_space=pltpu.SMEM)
    hbm = pl.BlockSpec(memory_space=pl.ANY)
    blocks = (tiles + 1) // N_X * kt
    shape = (blocks, PAIR, PAIR)
    return pl.pallas_call(
        match_kernel,
        in_specs=[smem, smem, hbm, hbm],
        out_specs=[smem, hbm],
        out_shape=[
            jax.ShapeDtypeStruct((2 * N_IRREP + 2 * kt + 2 + 4 * steps,), jnp.int32),
            jax.ShapeDtypeStruct(shape, jnp.bfloat16),
        ],
        scratch_shapes=[
            pltpu.VMEM((2, width, slab), jnp.bfloat16),
            pltpu.VMEM(shape, jnp.bfloat16),
            pltpu.SemaphoreType.DMA((2,)),
            pltpu.SemaphoreType.DMA((blocks // BUNDLE,)),
        ],
        compiler_params=params(),
        cost_estimate=pl.CostEstimate(
            flops=0, bytes_accessed=8 * width * slab, transcendentals=0
        ),
    )(cd_irrep, ab_irrep, plus, minus)


def ladder_kernel(begin_i, first, me_ref, lists, amp_ref, got_ref, weight_ref, *refs):
    n_out = len(refs) - 8
    out_refs = refs[:n_out]
    own, got, weights, both, staged, load_sem, weight_sem, out_sem = refs[n_out:]
    n_i, occ, width = own.shape
    kt = width // TILE
    tiles, per = staged.shape[:2]
    rows = n_i * occ
    me = me_ref[0]
    there = 2 * N_IRREP
    first_step = there + 2 * kt + 2
    bundles, steps = lists[first_step - 2], lists[first_step - 1]
    loads = [
        pltpu.make_async_copy(amp_ref.at[begin_i + first : begin_i + first + n_i], own, load_sem.at[0]),
        pltpu.make_async_copy(got_ref, got, load_sem.at[1]),
    ]
    for copy in loads:
        copy.start()

    def weights_copy(k):
        where = pl.ds(k * BUNDLE, BUNDLE)
        return pltpu.make_async_copy(weight_ref.at[where], weights.at[where], weight_sem.at[k])

    @pl.loop(0, bundles)
    def _(k):
        weights_copy(k).start()

    local = amp_ref.shape[0]
    piece = N_S * local
    span = n_i * piece
    received = got.shape[0] * piece // occ
    order = picker(receive_order(local, received // piece, first, n_i), received)
    for copy in loads:
        copy.wait()
    for q in range(occ // piece):
        other = jnp.dot(
            order, got[q * received : (q + 1) * received, :], preferred_element_type=jnp.float32
        )
        mine = own[:, q * piece : (q + 1) * piece, :].reshape(span, width).astype(jnp.float32)
        for half, value in enumerate((mine + other, mine - other)):
            value = value.astype(jnp.bfloat16).reshape(n_i, piece, width)
            for p in range(kt):
                lanes = pl.ds(pl.multiple_of(lists[there + p] * PAIR + half * TILE, TILE), TILE)
                both[:, q * piece : (q + 1) * piece, lanes] = value[:, :, p * TILE : (p + 1) * TILE]

    def out_copy(q, dst):
        return pltpu.make_async_copy(staged.at[q], dst, out_sem)

    def start(q):
        z, w = (q // N_X - me_ref[1]) & (tiles // N_X - 1), (q % N_X) ^ me
        if n_out == 1:
            out_copy(q, out_refs[0].at[z, pl.ds(w * per, per)]).start()
        else:
            for k in range(N_X):

                @pl.when(w == k)
                def _():
                    out_copy(q, out_refs[k].at[z]).start()

    @pl.loop(0, bundles)
    def _(k):
        weights_copy(k).wait()

    @pl.loop(0, steps)
    def _(step):
        g, a, b, block = (lists[first_step + 4 * step + k] for k in range(4))
        n, begin = lists[g], lists[N_IRREP + g]

        @pl.when(n == 0)
        def _():
            zero = jnp.zeros(staged.shape[1:], staged.dtype)
            staged[a] = zero
            staged[b] = zero

        for size in range(1, kt + 1):

            @pl.when(n == size)
            def _():
                lanes = pl.ds(pl.multiple_of(begin * PAIR, PAIR), size * PAIR)
                left = both[:, :, lanes].reshape(rows, size * PAIR)
                right = weights[pl.ds(block, size)].reshape(size * PAIR, PAIR)
                term = 0.5 * jnp.dot(left, right, preferred_element_type=jnp.float32)
                staged[a] = term[:, :TILE].astype(staged.dtype).reshape(staged.shape[1:])
                staged[b] = term[:, TILE:].astype(staged.dtype).reshape(staged.shape[1:])

        start(a)

        @pl.when(b != a)
        def _():
            start(b)

    pltpu.make_async_copy(staged, staged, out_sem).wait()


def ladder(place, lists, amplitudes, received, weights, begin, first, n_i, n_z, per, slots):
    _, occ, width = amplitudes.shape
    rows = n_i * occ
    tiles = n_z * N_X
    blocks = weights.shape[0]
    if slots:
        shapes = [(n_z, slots, rows // per, TILE)]
    else:
        shapes = [(n_z, per, rows // per, TILE)] * N_X
    smem = pl.BlockSpec(memory_space=pltpu.SMEM)
    hbm = pl.BlockSpec(memory_space=pl.ANY)
    dma = pltpu.SemaphoreType.DMA
    bf16 = jnp.bfloat16
    return pl.pallas_call(
        functools.partial(ladder_kernel, begin, first),
        in_specs=[smem, smem, hbm, hbm, hbm],
        out_specs=[hbm] * len(shapes),
        out_shape=[jax.ShapeDtypeStruct(s, bf16) for s in shapes],
        scratch_shapes=[
            pltpu.VMEM((n_i, occ, width), bf16),
            pltpu.VMEM(received.shape, bf16),
            pltpu.VMEM(weights.shape, bf16),
            pltpu.VMEM((n_i, occ, 2 * width), bf16),
            pltpu.VMEM((tiles, per, rows // per, TILE), bf16),
            dma((2,)),
            dma((blocks // BUNDLE,)),
            dma,
        ],
        compiler_params=params(50),
        cost_estimate=pl.CostEstimate(
            flops=0, bytes_accessed=8 * rows * (width + n_z * TILE), transcendentals=0
        ),
    )(place, lists, amplitudes, received, weights)


def finish_kernel(near, far, *refs):
    out_ref = refs[-1]
    total = near[...].astype(jnp.float32).reshape(-1, TILE) + far[...].astype(jnp.float32)
    if len(refs) > 1:
        early = refs[0][...].astype(jnp.float32).reshape(-1, TILE)
        total = jnp.concatenate([early, total], 0)
    out_ref[...] = total.T.astype(out_ref.dtype)


def slots(ref, count, k):
    return pl.BlockSpec((1, count) + ref.shape[2:], lambda g: (0, k, 0, 0))


def finish_first(near, far):
    rows = far.shape[0]
    return pl.pallas_call(
        finish_kernel,
        grid=(1,),
        in_specs=[slots(near, 1, 0), pl.BlockSpec(far.shape, lambda g: (0, 0))],
        out_specs=pl.BlockSpec((TILE, rows), lambda g: (0, 0)),
        out_shape=jax.ShapeDtypeStruct((TILE, 2 * rows), jnp.bfloat16),
        compiler_params=params(16),
    )(near, far)


def finish_last(done, early, up, down, late, far):
    whole = pl.BlockSpec(memory_space=pltpu.VMEM)
    hbm = pl.BlockSpec(memory_space=pl.ANY)
    rows = early.shape[0] + late.shape[0]
    begin = done.shape[1] - rows

    def kernel(done_ref, early_ref, up_ref, down_ref, late_ref, far_ref, out_ref, held, sem):
        first = early_ref[...]
        for ref in (up_ref, down_ref):
            first = first + ref[...].astype(jnp.float32).reshape(-1, TILE)
        last = late_ref[...] + far_ref[...].astype(jnp.float32)
        held[...] = jnp.concatenate([first, last], 0).T.astype(held.dtype)
        copy = pltpu.make_async_copy(held, out_ref.at[:, begin:], sem)
        copy.start()
        copy.wait()

    return pl.pallas_call(
        kernel,
        in_specs=[hbm] + [whole] * 5,
        out_specs=hbm,
        out_shape=jax.ShapeDtypeStruct(done.shape, jnp.bfloat16),
        scratch_shapes=[pltpu.VMEM((TILE, rows), jnp.bfloat16), pltpu.SemaphoreType.DMA],
        input_output_aliases={0: 0},
        compiler_params=params(16),
    )(done, early, up, down, late, far)


def add(*parts):
    total = parts[0].astype(jnp.float32)
    for part in parts[1:]:
        total = total + part.astype(jnp.float32)
    return total


def on_device(amplitudes, plus, minus, cd_irrep, ab_irrep):
    rows = amplitudes.shape[0]
    me, mine = (lax.axis_index(name).astype(jnp.int32) for name in ("xl", "z"))
    fixed, turned = jnp.stack([me, jnp.zeros_like(me)]), jnp.stack([me, mine])
    n_z = plus.shape[1] // PAIR
    half = n_z // 2
    swap = functools.partial(lax.ppermute, axis_name="xl", perm=[(0, 1), (1, 0)])

    def exchange(packed):
        return lax.all_to_all(packed, "row", split_axis=0, concat_axis=0, tiled=True)

    def scatter(terms):
        return lax.psum_scatter(terms, "z", scatter_dimension=0, tiled=True)

    up = functools.partial(
        lax.ppermute, axis_name="z", perm=[(k, (k + 1) % n_z) for k in range(n_z)]
    )
    down = functools.partial(
        lax.ppermute, axis_name="z", perm=[((k + 1) % n_z, k) for k in range(n_z)]
    )

    def send(*pair):
        pair = lax.optimization_barrier(tuple(p.astype(jnp.bfloat16) for p in pair))
        return lax.optimization_barrier((up(pair[0]), down(pair[1])))

    def set_out(terms):
        first = terms(half)
        return send(add(*[t[:1] for t in first]), add(*[t[1:] for t in first]))

    def go_on(terms, step, goes_up, goes_down):
        if step == 1:
            goes_up = jnp.pad(goes_up, ((0, 1), (0, 0), (0, 0)))
            goes_down = jnp.pad(goes_down, ((1, 0), (0, 0), (0, 0)))
        return send(
            add(goes_up, *terms(half - step)), add(goes_down, *terms(half + step))
        )

    def product(place, received, begin, first, n_i, slots):
        return ladder(
            place,
            lists,
            amplitudes,
            received,
            weights,
            begin,
            first,
            n_i,
            n_z,
            1,
            slots,
        )

    rest = rows - FIRST
    packed0 = pack(amplitudes, 0, FIRST)
    received0 = exchange(packed0)
    packed0, later = lax.optimization_barrier((packed0, amplitudes))
    packed1 = pack(later, FIRST, rest)
    packed0, first_plus = lax.optimization_barrier((packed0, plus))
    lists, weights = match(cd_irrep, ab_irrep, first_plus, minus)
    received0, packed1, weights = lax.optimization_barrier((received0, packed1, weights))
    received1 = exchange(packed1)
    (terms0,) = product(fixed, received0, 0, 0, FIRST - UNIT, N_X)
    sum0 = scatter(terms0)
    received0, _ = lax.optimization_barrier((received0, terms0))
    near0, far0 = product(turned, received0, 0, FIRST - UNIT, UNIT, 0)
    far0 = swap(far0)
    received1, _ = lax.optimization_barrier((received1, near0))
    near1, far1 = product(turned, received1, FIRST, 0, UNIT, 0)
    far1 = swap(far1)
    received1, _ = lax.optimization_barrier((received1, near1))
    (terms1,) = product(turned, received1, FIRST, UNIT, rest - UNIT, N_X)

    def late(k):
        return (terms1[k],)

    def early(k):
        return [jnp.concatenate(pair, 0) for pair in ((near0[k], near1[k]), (far0[k], far1[k]))]

    late_ring = set_out(late)
    late_ring, far0, far1 = lax.optimization_barrier((late_ring, far0, far1))
    early_ring = set_out(early)
    for step in range(1, half):
        late_ring = go_on(late, step, *late_ring)
        early_ring = go_on(early, step, *early_ring)
    late_ring, last0 = lax.optimization_barrier((late_ring, swap(sum0[0, 1])))
    late_sum = add(terms1[0], *late_ring)
    far_late = swap(late_sum[1].astype(jnp.bfloat16))
    done = finish_first(sum0, last0)
    return finish_last(
        done, add(*early(0)).reshape(-1, TILE), *early_ring, late_sum[0], far_late
    )


def solution(mesh):
    rows, cols = mesh.shape["row"], mesh.shape["col"]
    fine = Mesh(mesh.devices.reshape(rows, cols // N_X, N_X), ("row", "z", "xl"))
    col = ("z", "xl")
    return jax.shard_map(
        on_device,
        mesh=fine,
        in_specs=(P("row", None, col), P(col, None), P(col, None), P(col), P()),
        out_specs=P(col, "row"),
        check_vma=False,
    )
```
